256 devices in a mesh: dp: 16 (over y, z_lo), ctx: 16 (over x, z_hi, core).
Axes of the slice: x: 4, y: 4, z: 8 (z_hi: 2, z_lo: 4; z = z_hi * 4 + z_lo), core: 2. Of those that a mesh axis runs over, the one named last changes fastest.
Arguments:
- layer_inputs: bfloat16 [32768, 6144], P(('dp', 'ctx')), may hold values from -6 to 6
- queries: bfloat16 [32768, 6144], P(('dp', 'ctx')), may hold values from -128 to 128
- key_states: bfloat16 [32768, 512], P(('dp', 'ctx')), may hold values from -6 to 6
- value_states: bfloat16 [32768, 512], P(('dp', 'ctx')), may hold values from -6 to 6
- output_grad: bfloat16 [32768, 6144], P(('dp', 'ctx')), may hold values from -6 to 6
- short_segments: int32 [256, 64], P(('dp', 'ctx')), may hold values from 0 to 7, never falling along the last dimension, each value on 1 to 16 neighbouring positions
- master: float32 [16, 384, 512], P('ctx', 'dp'), may hold values from -0.078125 to 0.078125
- first_moment: float32 [16, 384, 512], P('ctx', 'dp'), may hold values from -0.015625 to 0.015625
- second_moment: float32 [16, 384, 512], P('ctx', 'dp'), may hold values from 1e-07 to 1e-05
Outputs:
- grad_queries: bfloat16 [32768, 6144], P(('dp', 'ctx'))
- grad_values: bfloat16 [32768, 512], P(('dp', 'ctx'))
- new_master: float32 [16, 384, 512], P('ctx', 'dp')
- new_first: float32 [16, 384, 512], P('ctx', 'dp')
- new_second: float32 [16, 384, 512], P('ctx', 'dp')
- new_weight: bfloat16 [16, 384, 512], P('ctx')
The draws below stay inside these ranges and needn't reach their ends.
Inputs may be any that keep to these rules, and one draw needn't show every extreme that they name: `short_segments`: on each device the short tokens form 8 documents numbered in order, each of 1 to 16 tokens, one of exactly that length.
All inputs are finite; a program needn't handle non-finite values.
Results may differ from the reference program's by a relative error of at most 0.0074.
Values may be sent and summed in bfloat16 or wider, within the bound.
A program may use at most 128 MiB of HBM per device.

```python
import math
import jax
import jax.numpy as jnp
import numpy as np
from jax import lax

D = 6144
HQ = 48
HK = 4
HEAD = 128
LONG_DEV = 64
SHORT_DEV = 64
SEGS = 8
GROUPS = 12
QD = 6144
KD = 512
TOK_DEV = 128
TOKENS = 32768
LONG_LEN = 1024
N_DP = 16
N_CTX = 16
DEVICES = 256


def shared_keys(key):
    single = jax.random.normal(jax.random.fold_in(key, 5), (TOKENS, HK * HEAD), jnp.float32)
    return jnp.clip(single, -6.0, 6.0)


def draw_key_states(key, part):
    shared = shared_keys(key)
    return shared.astype(jnp.bfloat16)


def draw_queries(key, part):
    key = jax.random.fold_in(key, 4)
    result = jnp.clip(jax.random.normal(key, (TOKENS, HQ * HEAD), jnp.float32), -6.0, 6.0)
    return result.astype(jnp.bfloat16)


def block_scale(key, dims, cuts, least, top_value):
    loudness = 1.0
    for dim, shards_of in cuts:
        draws = jax.random.uniform(jax.random.fold_in(jax.random.fold_in(key, 6), dim), (shards_of,), jnp.float32, least / len(cuts), top_value / len(cuts))
        loudness = loudness * jnp.repeat(jnp.exp(draws), dims[dim] // shards_of).reshape((-1,) + (1,) * (len(dims) - 1 - dim))
    return loudness


def profile(amount, total, bound, slope):
    weights = [(1 << 20) // math.isqrt(grade ** slope) + 1 for grade in range(2, amount + 1)]
    spare, given = total - bound - (amount - 1), [1] * (amount - 1)
    while spare > 0:
        candidates = [i for i in range(amount - 1) if given[i] < bound]
        mass, remaining = sum([weights[i] for i in candidates]), spare
        for i in candidates:
            more = min(bound - given[i], max(1, remaining * weights[i] // mass), spare)
            given[i] = given[i] + more
            spare = spare - more
    return np.array([bound] + given)


def uneven_parts(own_key, number_of, total, bound, slope):
    if number_of == 2:
        one = jax.random.randint(own_key, (), max(1, total - bound), min(bound, total - 1) + 1)
        return jnp.stack([one, total - one])
    lengths = jnp.asarray(profile(number_of, total, bound, slope), jnp.int32)
    twos = (number_of - 1) // 2
    giver, sink = lengths[1:1 + 2 * twos:2], lengths[2:2 + 2 * twos:2]
    slack = jnp.minimum(giver - 1, bound - sink)
    shifted = jax.random.randint(jax.random.fold_in(own_key, 1), (twos,), 0, 1 << 20) % (slack + 1)
    lengths = lengths.at[1:1 + 2 * twos:2].set(giver - shifted).at[2:2 + 2 * twos:2].set(sink + shifted)
    return lengths[jax.random.permutation(jax.random.fold_in(own_key, 2), number_of)]


def centred(own_key, dims, deviation, reach, shards=(), kind=jnp.bfloat16):
    loudness = block_scale(own_key, dims, shards, -0.22, 0.18) if shards else 1.0
    entries = jax.random.normal(own_key, dims, jnp.float32) * deviation * loudness
    return jnp.minimum(jnp.maximum(entries, -reach), reach).astype(kind)


def setup_inputs(seed: int = 0) -> dict:
    splits = jax.random.split(jax.random.key(seed), 10)
    layer_inputs = centred(splits[0], (TOKENS, D), 1.0, 6.0, ((0, 256),))
    queries = draw_queries(jax.random.fold_in(splits[9], 71), 0)
    key_states = draw_key_states(jax.random.fold_in(splits[9], 71), 0)
    value_states = centred(splits[3], (TOKENS, KD), 1.0, 6.0, ((0, 256),))
    output_grad = centred(splits[4], (TOKENS, QD), 1.0, 6.0, ((0, 256),))
    short_segments = jax.vmap(lambda own: jnp.searchsorted(jnp.cumsum(uneven_parts(own, SEGS, SHORT_DEV, SHORT_DEV // 4, 2)), jnp.arange(SHORT_DEV), side="right"))(jax.random.split(splits[5], DEVICES)).reshape((DEVICES, SHORT_DEV)).astype(jnp.int32)
    master = centred(splits[6], (N_CTX, D // N_CTX, KD), D ** -0.5, 0.078125, ((0, 16), (1, 16)), jnp.float32)
    first_moment = centred(splits[7], (N_CTX, D // N_CTX, KD), 0.001, 0.015625, ((0, 16), (1, 16)), jnp.float32)
    second_moment = jnp.clip(jnp.exp(math.log(9.999999747378752e-06) - 4.6051701 * jax.random.uniform(splits[8], (N_CTX, D // N_CTX, KD), jnp.float32) ** block_scale(splits[8], (N_CTX, D // N_CTX, KD), ((0, 16), (1, 16)), -0.2, 0.2)), 1.0000000116860974e-07, 9.999999747378752e-06)
    return dict(layer_inputs=layer_inputs, queries=queries, key_states=key_states, value_states=value_states, output_grad=output_grad, short_segments=short_segments, master=master, first_moment=first_moment, second_moment=second_moment)


LEARN_RATE = 0.001
BETA_ONE = 0.9
BETA_TWO = 0.95
ADAM_EPS = 1e-08
DECAY = 0.1
STEP_COUNT = 10

def head_backward(query_head, key_head, value_head, grad_head, allowed):
    factor = query_head.shape[-1] ** (-0.5)
    scores = jnp.dot(query_head, key_head.T, preferred_element_type=jnp.float32) * factor
    scores = jnp.where(allowed, scores, -jnp.inf)
    row_max = lax.optimization_barrier(jnp.max(scores, axis=-1, keepdims=True))
    raised = jnp.exp(scores - row_max)
    soft_probs = raised / lax.optimization_barrier(jnp.sum(raised, axis=-1, keepdims=True))
    probs_low = soft_probs.astype(jnp.bfloat16)
    recomputed = jnp.dot(probs_low, value_head, preferred_element_type=jnp.float32)
    row_delta = lax.optimization_barrier(jnp.sum(grad_head.astype(jnp.float32) * recomputed, axis=-1, keepdims=True))
    grad_probs = jnp.dot(grad_head, value_head.T, preferred_element_type=jnp.float32)
    grad_scores = (soft_probs * (grad_probs - row_delta) * factor).astype(jnp.bfloat16)
    grad_query = jnp.dot(grad_scores, key_head, preferred_element_type=jnp.float32)
    grad_key = jnp.dot(grad_scores.T, query_head, preferred_element_type=jnp.float32)
    grad_value = jnp.dot(probs_low.T, grad_head, preferred_element_type=jnp.float32)
    return (grad_query, grad_key, grad_value)

def reference(layer_inputs, queries, key_states, value_states, output_grad, short_segments, master, first_moment, second_moment):
    query_rows = queries.reshape(DEVICES, TOK_DEV, HQ, HEAD)
    key_rows = key_states.reshape(DEVICES, TOK_DEV, HK, HEAD)
    value_rows = value_states.reshape(DEVICES, TOK_DEV, HK, HEAD)
    grad_rows = output_grad.reshape(DEVICES, TOK_DEV, HQ, HEAD)

    def long_view(source):
        return source[:, :LONG_DEV].reshape(N_DP, LONG_LEN, source.shape[2], HEAD)
    causal = jnp.arange(LONG_LEN)[:, None] >= jnp.arange(LONG_LEN)[None, :]

    def long_group(pieces):
        group_queries, group_keys, group_values, group_grads = pieces

        def one_head(which_head):
            key_index = which_head // GROUPS
            return head_backward(group_queries[:, which_head], group_keys[:, key_index], group_values[:, key_index], group_grads[:, which_head], causal)
        return lax.map(one_head, jnp.arange(HQ))
    long_query, long_key, long_value = lax.map(long_group, (long_view(query_rows), long_view(key_rows), long_view(value_rows), long_view(grad_rows)))
    long_query = jnp.transpose(long_query, (0, 2, 1, 3)).reshape(DEVICES, LONG_DEV, QD)
    long_key = jnp.transpose(long_key.reshape(N_DP, HK, GROUPS, LONG_LEN, HEAD).sum(2), (0, 2, 1, 3)).reshape(DEVICES, LONG_DEV, KD)
    long_value = jnp.transpose(long_value.reshape(N_DP, HK, GROUPS, LONG_LEN, HEAD).sum(2), (0, 2, 1, 3)).reshape(DEVICES, LONG_DEV, KD)
    position = jnp.arange(SHORT_DEV)

    def short_device(pieces):
        short_queries, short_keys, short_values, short_grads, segment = pieces
        allowed = (segment[:, None] == segment[None, :]) & (position[:, None] >= position[None, :])

        def short_head(which_head):
            key_index = which_head // GROUPS
            return head_backward(short_queries[:, which_head], short_keys[:, key_index], short_values[:, key_index], short_grads[:, which_head], allowed)
        grad_query, grad_key, grad_value = lax.map(short_head, jnp.arange(HQ))
        grad_query = jnp.transpose(grad_query, (1, 0, 2)).reshape(SHORT_DEV, QD)
        grad_key = jnp.transpose(grad_key.reshape(HK, GROUPS, SHORT_DEV, HEAD).sum(1), (1, 0, 2)).reshape(SHORT_DEV, KD)
        grad_value = jnp.transpose(grad_value.reshape(HK, GROUPS, SHORT_DEV, HEAD).sum(1), (1, 0, 2)).reshape(SHORT_DEV, KD)
        return (grad_query, grad_key, grad_value)
    short_query, short_key, short_value = lax.map(short_device, (query_rows[:, LONG_DEV:], key_rows[:, LONG_DEV:], value_rows[:, LONG_DEV:], grad_rows[:, LONG_DEV:], short_segments))
    grad_queries = jnp.concatenate([long_query.astype(jnp.bfloat16), short_query.astype(jnp.bfloat16)], axis=1).reshape(TOKENS, QD)
    grad_keys = jnp.concatenate([long_key, short_key], axis=1).reshape(TOKENS, KD).astype(jnp.bfloat16)
    grad_values = jnp.concatenate([long_value, short_value], axis=1).reshape(TOKENS, KD).astype(jnp.bfloat16)
    weight_grad = jnp.dot(layer_inputs.T, grad_keys, preferred_element_type=jnp.float32) * (1.0 / TOKENS)
    weight_grad = weight_grad.reshape(N_CTX, D // N_CTX, KD)
    new_first = BETA_ONE * first_moment + (1.0 - BETA_ONE) * weight_grad
    new_second = BETA_TWO * second_moment + (1.0 - BETA_TWO) * weight_grad * weight_grad
    first_hat = new_first / (1.0 - BETA_ONE ** STEP_COUNT)
    second_hat = new_second / (1.0 - BETA_TWO ** STEP_COUNT)
    new_master = master - LEARN_RATE * (first_hat / (jnp.sqrt(second_hat) + ADAM_EPS) + DECAY * master)
    new_weight = new_master.astype(jnp.bfloat16)
    return (grad_queries, grad_values, new_master, new_first, new_second, new_weight)
```

```python
import functools

import jax
import jax.numpy as jnp
from jax import lax
from jax.experimental import pallas as pl
from jax.experimental.pallas import tpu as pltpu
from jax.sharding import PartitionSpec as P

D = 6144
HEAD = 128
GROUPS = 12
LONG_DEV = 64
SHORT_DEV = 64
TOK_DEV = 128
CHUNK = 128
KD = 512
QD = 6144
HALF_Q = 3072
HALF_K = 256
NY, NZL, NX, NZH, NC = 4, 4, 4, 2, 2
NZ = NZL * NZH

LEARN_RATE = 0.001
BETA_ONE = 0.9
BETA_TWO = 0.95
ADAM_EPS = 1e-08
DECAY = 0.1
STEP_COUNT = 10

MESH = pl.DeviceIdType.MESH
FACTOR = HEAD**-0.5
EXP_FACTOR = FACTOR * 1.4426950408889634
NEG = -1e30
BF = jnp.bfloat16
F32 = jnp.float32
NT = (((1,), (1,)), ((), ()))
TN = (((0,), (0,)), ((), ()))


def dot(a, b, dims=(((1,), (0,)), ((), ()))):
    return lax.dot_general(a, b, dims, preferred_element_type=F32)


def place():
    d = lax.axis_index("dp")
    c = lax.axis_index("ctx")
    return d // NZL, d % NZL, c // (NZH * NC), (c // NC) % NZH, c % NC


def device(y, z_lo, x, z_hi, core):
    return (y * NZL + z_lo, (x * NZH + z_hi) * NC + core)


def enter(peers):
    barrier = pltpu.get_barrier_semaphore()
    for peer in peers:
        pl.semaphore_signal(barrier, inc=1, device_id=peer, device_id_type=MESH)
    pl.semaphore_wait(barrier, len(peers))


def remote(src, dst, send, recv, peer):
    return pltpu.make_async_remote_copy(
        src_ref=src, dst_ref=dst, send_sem=send, recv_sem=recv, device_id=peer, device_id_type=MESH
    )


def lanes(start, size):
    return pl.ds(pl.multiple_of(start, 128), size)


def rows(start, size, unit):
    return pl.ds(pl.multiple_of(start, unit), size)


def short_mask(seg_ref):
    segment = seg_ref[...]
    square = jnp.broadcast_to(segment, (SHORT_DEV, SHORT_DEV))
    diag = lax.broadcasted_iota(jnp.int32, (SHORT_DEV, SHORT_DEV), 0) == lax.broadcasted_iota(
        jnp.int32, (SHORT_DEV, SHORT_DEV), 1
    )
    column = jnp.sum(jnp.where(diag, square.astype(F32), 0.0), axis=1, keepdims=True)
    row = jnp.concatenate([segment.astype(F32)] * 2, axis=1)
    key = lax.broadcasted_iota(jnp.int32, (SHORT_DEV, 128), 0)
    token = lax.broadcasted_iota(jnp.int32, (SHORT_DEV, 128), 1) % SHORT_DEV
    pair = jnp.where((column == row) & (key <= token), 0.0, NEG)
    return jnp.concatenate([pair] * (GROUPS // 2), axis=1)


def short_head(kh, bias, q_ref, g_ref, k_ref, v_ref, dq_ref, dk_ref, dv_ref):
    width = GROUPS * HEAD
    q = q_ref[:, lanes(kh * width, width)]
    g = g_ref[:, lanes(kh * width, width)]
    k = k_ref[:, lanes(kh * HEAD, HEAD)]
    v = v_ref[:, lanes(kh * HEAD, HEAD)]
    q = jnp.concatenate([q[:, i * HEAD : (i + 1) * HEAD] for i in range(GROUPS)], axis=0)
    g = jnp.concatenate([g[:, i * HEAD : (i + 1) * HEAD] for i in range(GROUPS)], axis=0)
    scores = dot(k, q, NT) + bias
    top = jnp.max(scores, axis=0, keepdims=True)
    raised = jnp.exp2((scores - top) * EXP_FACTOR)
    probs = raised * (1.0 / jnp.sum(raised, axis=0, keepdims=True))
    probs_low = probs.astype(BF)
    grad_probs = dot(v, g, NT)
    delta = jnp.sum(probs_low.astype(F32) * grad_probs, axis=0, keepdims=True)
    grad_scores = (probs * FACTOR * (grad_probs - delta)).astype(BF)
    dv_ref[:, lanes(kh * HEAD, HEAD)] = dot(probs_low, g).astype(BF)
    dk_ref[:, lanes(kh * HEAD, HEAD)] = dot(grad_scores, q).astype(BF)
    dq = dot(grad_scores, k, TN).astype(BF)
    dq_ref[:, lanes(kh * width, width)] = jnp.concatenate(
        [dq[i * SHORT_DEV : (i + 1) * SHORT_DEV] for i in range(GROUPS)], axis=1
    )


def gather_kernel(
    q_hbm, g_hbm, k_hbm, v_hbm, x_hbm, seg_ref,
    qb, gb, kb, vb, sdq, sgk, sgv, xt,
    qs, gs, ks, vs, xs,
    load_sem, own_sem, q_send, q_recv, kv_send, kv_recv, fw_send, fw_recv,
):
    y, z_lo, x, z_hi, core = place()
    c = lax.axis_index("ctx")
    loads = [
        pltpu.make_async_copy(hbm.at[rows(LONG_DEV, SHORT_DEV, 64), :], vmem, load_sem.at[i])
        for i, (hbm, vmem) in enumerate(((q_hbm, qs), (g_hbm, gs), (k_hbm, ks), (v_hbm, vs)))
    ]
    loads.append(pltpu.make_async_copy(x_hbm, xs, load_sem.at[4]))
    for copy in loads:
        copy.start()
    own_rows = rows(c * LONG_DEV, LONG_DEV, 64)
    pair_rows = rows(core * LONG_DEV, LONG_DEV, 64)
    first = pl.ds(0, LONG_DEV)
    mine = [
        pltpu.make_async_copy(src.at[first, lanes(core * width, width)], dst.at[where, :], own_sem.at[i])
        for i, (src, dst, width, where) in enumerate(
            (
                (k_hbm, kb, HALF_K, own_rows),
                (v_hbm, vb, HALF_K, own_rows),
                (q_hbm, qb, HALF_Q, pair_rows),
                (g_hbm, gb, HALF_Q, pair_rows),
            )
        )
    ]
    for copy in mine:
        copy.start()

    offsets = [(dx, 0, dc) for dx in range(NX) for dc in range(NC) if (dx, dc) != (0, 0)]
    offsets += [(0, 1, 0), (0, 1, 1)]

    def peer_at(dx, dz, dc, sign):
        return ((x + sign * dx + NX) % NX, (z_hi + dz) % NZH, (core + dc) % NC)

    enter([device(y, z_lo, *peer_at(*o, 1)) for o in offsets])

    def kv_copies(i, sign):
        px, pz, pc = peer_at(*offsets[i], sign)
        peer = device(y, z_lo, px, pz, pc)
        if sign > 0:
            col, where = pc, own_rows
        else:
            col, where = core, rows(((px * NZH + pz) * NC + pc) * LONG_DEV, LONG_DEV, 64)
        return [
            remote(
                src.at[first, lanes(col * HALF_K, HALF_K)],
                dst.at[where, :],
                kv_send.at[n, i],
                kv_recv.at[n, i],
                peer,
            )
            for n, (src, dst) in enumerate(((k_hbm, kb), (v_hbm, vb)))
        ]

    order = [7, 8] + list(range(7))
    sent = []
    for i in order:
        for copy in kv_copies(i, 1):
            copy.start()
            sent.append(copy)
    other = 1 - core
    sibling = device(y, z_lo, x, z_hi, other)
    swaps = [
        remote(
            src.at[first, lanes(other * HALF_Q, HALF_Q)], dst.at[pair_rows, :], q_send.at[n], q_recv.at[n], sibling
        )
        for n, (src, dst) in enumerate(((q_hbm, qb), (g_hbm, gb)))
    ]
    for copy in swaps:
        copy.start()

    for copy in loads[:4]:
        copy.wait()
    bias = short_mask(seg_ref)

    def heads(start, stop):
        @pl.loop(start, stop)
        def _(kh):
            short_head(kh, bias, qs, gs, ks, vs, sdq, sgk, sgv)

    heads(0, 2)
    for i in (7, 8):
        for copy in kv_copies(i, -1):
            copy.wait_recv()
    theirs = rows((x * NZH + 1 - z_hi) * CHUNK, CHUNK, 128)

    def forward(dx, sign):
        px = (x + sign * dx + NX) % NX
        where = rows((px * NZH + 1 - z_hi) * CHUNK, CHUNK, 128) if sign < 0 else theirs
        return [
            remote(
                b.at[where, :], b.at[where, :], fw_send.at[n, dx - 1], fw_recv.at[n, dx - 1],
                device(y, z_lo, px, z_hi, core),
            )
            for n, b in enumerate((kb, vb))
        ]

    for dx in (1, 3, 2):
        for copy in forward(dx, 1):
            copy.start()
            sent.append(copy)
    heads(2, 4)
    loads[4].wait()

    @pl.loop(0, D // 128)
    def _(i):
        xt[rows(i * 128, 128, 128), :] = xs[:, lanes(i * 128, 128)].T

    for copy in mine:
        copy.wait()
    for copy in swaps:
        copy.wait()
    for i in range(7):
        for copy in kv_copies(i, -1):
            copy.wait_recv()
    for dx in (1, 2, 3):
        for copy in forward(dx, -1):
            copy.wait_recv()
    for copy in sent:
        copy.wait_send()


PAIR = 2
WIDE = PAIR * CHUNK


def long_heads(keys, z_hi, q, g, k, v, dq, dkv, scores, grads, low, acc_k, acc_v):
    chunks = keys // CHUNK

    def step(kv, p):
        col = kv * GROUPS * HEAD + p * PAIR * HEAD
        head = lanes(kv * HEAD, HEAD)
        q2 = q[:, lanes(col, PAIR * HEAD)]
        g2 = g[:, lanes(col, PAIR * HEAD)]
        qs = jnp.concatenate([q2[:, i * HEAD : (i + 1) * HEAD] for i in range(PAIR)], axis=0)
        gs = jnp.concatenate([g2[:, i * HEAD : (i + 1) * HEAD] for i in range(PAIR)], axis=0)
        top = None
        for n in range(chunks):
            s = dot(k[n * CHUNK : (n + 1) * CHUNK, head], qs, NT)
            if n >= chunks - 2:
                key = lax.broadcasted_iota(jnp.int32, (CHUNK, WIDE), 0) + (n - chunks + 2) * CHUNK
                token = lax.broadcasted_iota(jnp.int32, (CHUNK, WIDE), 1) % CHUNK + z_hi * CHUNK
                s = jnp.where(key <= token, s, NEG)
            scores[n * CHUNK : (n + 1) * CHUNK, :] = s
            m = jnp.max(s, axis=0, keepdims=True)
            top = m if top is None else jnp.maximum(top, m)
        total = None
        for n in range(chunks):
            at = slice(n * CHUNK, (n + 1) * CHUNK)
            e = jnp.exp2((scores[at, :] - top) * EXP_FACTOR)
            scores[at, :] = e
            part = jnp.sum(e, axis=0, keepdims=True)
            total = part if total is None else total + part
            grads[at, :] = dot(v[at, head], gs, NT)
        scale = 1.0 / total
        delta = None
        for n in range(chunks):
            at = slice(n * CHUNK, (n + 1) * CHUNK)
            pr = scores[at, :] * scale
            pb = pr.astype(BF)
            part = jnp.sum(pb.astype(F32) * grads[at, :], axis=0, keepdims=True)
            delta = part if delta is None else delta + part
            acc_v[at, :] += dot(pb, gs)
        scale = scale * FACTOR
        for n in range(chunks):
            at = slice(n * CHUNK, (n + 1) * CHUNK)
            ds = (scores[at, :] * scale * (grads[at, :] - delta)).astype(BF)
            low[at, :] = ds
            acc_k[at, :] += dot(ds, qs)
        out = dot(low[0:keys, :], k[0:keys, head], TN).astype(BF)
        dq[:, lanes(col, PAIR * HEAD)] = jnp.concatenate(
            [out[i * CHUNK : (i + 1) * CHUNK] for i in range(PAIR)], axis=1
        )

    for kv in range(2):
        acc_k[0:keys, :] = jnp.zeros((keys, HEAD), F32)
        acc_v[0:keys, :] = jnp.zeros((keys, HEAD), F32)

        @pl.loop(0, GROUPS // PAIR)
        def _(p):
            step(kv, p)

        for n in range(chunks):
            at = slice(n * CHUNK, (n + 1) * CHUNK)
            dkv[n, :, kv * HEAD : (kv + 1) * HEAD] = acc_k[at, :].astype(BF)
            dkv[n, :, HALF_K + kv * HEAD : HALF_K + (kv + 1) * HEAD] = acc_v[at, :].astype(BF)


def long_kernel(q, g, k, v, dq, dkv, scores, grads, low, acc_k, acc_v):
    _, _, x, z_hi, _ = place()
    for n in range(NX):

        @pl.when(x == n)
        def _():
            long_heads(
                (n + 1) * NZH * CHUNK, z_hi, q, g, k, v, dq, dkv, scores, grads, low, acc_k, acc_v
            )


def fold(a):
    return jnp.concatenate([a[:, i * 128 : (i + 1) * 128] for i in range(4)], axis=0)


def unfold(a):
    return jnp.concatenate([a[i * 24 : (i + 1) * 24] for i in range(4)], axis=1)


def update_kernel(
    dq_hbm, dkv_hbm, xt_hbm, sdq_hbm, sgk_hbm, sgv_hbm, master, first, second,
    gq, gv, new_master, new_first, new_second, new_weight,
    own, total, rx, zs, zr, gkl, gvl, xg, gk, wp, wr, wsum, zf, zp, zq, nwp, nwr,
    own_sem, dq_send, dq_recv, rx_send, rx_recv, z_send, z_recv, x_send, x_recv, s_send, s_recv,
    l_send, l_recv, v_send, v_recv, w_send, w_recv, p_send, p_recv, n_send, n_recv,
):
    y, z_lo, x, z_hi, core = place()
    z = z_hi * NZL + z_lo
    other = 1 - core
    sibling = device(y, z_lo, x, z_hi, other)
    partner = device(y, z_lo, x, 1 - z_hi, core)
    top, low = pl.ds(0, LONG_DEV), pl.ds(LONG_DEV, SHORT_DEV)
    my_half = lanes(core * HALF_Q, HALF_Q)
    my_keys = lanes(core * HALF_K, HALF_K)
    my_tokens = lanes(core * TOK_DEV, TOK_DEV)
    mine = [
        pltpu.make_async_copy(dkv_hbm.at[rows(NZH * x, NZH, 1)], own, own_sem.at[0]),
        pltpu.make_async_copy(xt_hbm.at[:, core, y], xg.at[y, :, :, my_tokens], own_sem.at[1]),
        pltpu.make_async_copy(sgk_hbm, gk.at[y, core, low, :], own_sem.at[2]),
        pltpu.make_async_copy(sdq_hbm, gq.at[low, :], own_sem.at[3]),
        pltpu.make_async_copy(sgv_hbm, gv.at[low, :], own_sem.at[4]),
        pltpu.make_async_copy(
            dq_hbm.at[rows(core * LONG_DEV, LONG_DEV, 64), :], gq.at[top, my_half], own_sem.at[5]
        ),
    ]
    for copy in mine:
        copy.start()

    def x_peer(dx, sign):
        return (x + sign * dx + NX) % NX

    def z_peer(dz, sign):
        return (z + sign * dz + NZ) % NZ

    def z_device(pz):
        return device(y, pz % NZL, x, pz // NZL, core)

    group = [(dy, dc) for dy in range(NY) for dc in range(NC) if (dy, dc) != (0, 0)]
    data = [(dy, dz) for dy in range(NY) for dz in range(NZL) if (dy, dz) != (0, 0)]

    def group_peer(i, sign):
        dy, dc = group[i]
        return (y + sign * dy + NY) % NY, (core + dc) % NC

    def data_peer(i, sign):
        dy, dz = data[i]
        return (y + sign * dy + NY) % NY, (z_lo + sign * dz + NZL) % NZL

    peers = [device(y, z_lo, x_peer(dx, 1), z_hi, core) for dx in range(1, NX)]
    peers += [z_device(z_peer(dz, 1)) for dz in range(1, NZ)]
    for i in range(len(group)):
        py, pc = group_peer(i, 1)
        peers.append(device(py, z_lo, x, z_hi, pc))
    for i, (dy, dz) in enumerate(data):
        if dy and dz:
            py, pz = data_peer(i, 1)
            peers.append(device(py, pz, x, z_hi, core))
    enter(peers)

    def kv_copy(dx, sign):
        px = x - sign * dx
        return remote(
            dkv_hbm.at[rows(NZH * px, NZH, 1)], rx.at[dx - 1], rx_send.at[dx - 1], rx_recv.at[dx - 1],
            device(y, z_lo, px, z_hi, core),
        )

    for dx in range(1, NX):

        @pl.when(x >= dx)
        def _():
            kv_copy(dx, 1).start()

    def x_copy(i, sign):
        py, pc = group_peer(i, sign)
        sy, sc = (y, core) if sign > 0 else (py, pc)
        return remote(
            xt_hbm.at[:, pc, py], xg.at[sy, :, :, lanes(sc * TOK_DEV, TOK_DEV)], x_send.at[i], x_recv.at[i],
            device(py, z_lo, x, z_hi, pc),
        )

    def short_copy(i, sign):
        py, pc = group_peer(i, sign)
        sy, sc = (y, core) if sign > 0 else (py, pc)
        return remote(
            sgk_hbm, gk.at[sy, sc, low, :], s_send.at[i], s_recv.at[i], device(py, z_lo, x, z_hi, pc)
        )

    for i in range(len(group)):
        x_copy(i, 1).start()
        short_copy(i, 1).start()
    dq_copy = remote(
        dq_hbm.at[rows(other * LONG_DEV, LONG_DEV, 64), :], gq.at[top, my_half], dq_send.at[0], dq_recv.at[0], sibling
    )
    dq_copy.start()

    mine[0].wait()
    total[...] = own[...].astype(F32)
    for dx in range(1, NX):

        @pl.when(x + dx < NX)
        def _():
            kv_copy(dx, -1).wait_recv()
            total[...] += rx[dx - 1].astype(F32)

    zs[...] = total[1 - z_hi].astype(BF)
    z_copy = remote(zs, zr, z_send.at[0], z_recv.at[0], partner)
    z_copy.start()
    z_copy.wait_recv()
    both = (total[z_hi] + zr[...].astype(F32)).astype(BF)
    for half in range(NC):
        part = both[half * LONG_DEV : (half + 1) * LONG_DEV]
        gkl[half] = part[:, :HALF_K]
        gvl[half] = part[:, HALF_K:]

    def long_copy(i, sign):
        py, pc = group_peer(i, sign)
        sy, sc = (y, core) if sign > 0 else (py, pc)
        return remote(
            gkl, gk.at[sy, :, top, lanes(sc * HALF_K, HALF_K)], l_send.at[i], l_recv.at[i],
            device(py, z_lo, x, z_hi, pc),
        )

    for i in range(len(group)):
        long_copy(i, 1).start()
    v_copy = remote(gvl.at[other], gv.at[top, my_keys], v_send.at[0], v_recv.at[0], sibling)
    v_copy.start()
    mine.append(pltpu.make_async_copy(gkl, gk.at[y, :, top, my_keys], own_sem.at[6]))
    mine.append(pltpu.make_async_copy(gvl.at[core], gv.at[top, my_keys], own_sem.at[7]))
    for copy in mine[6:]:
        copy.start()
    for i in range(len(group)):
        x_copy(i, -1).wait_recv()
        short_copy(i, -1).wait_recv()
    mine[1].wait()
    mine[2].wait()
    mine[6].wait()
    for i in range(len(group)):
        long_copy(i, -1).wait_recv()

    def w_copy(dx, sign):
        px = x_peer(dx, sign)
        return remote(
            wp.at[px], wr.at[dx - 1], w_send.at[dx - 1], w_recv.at[dx - 1], device(y, z_lo, px, z_hi, core)
        )

    def product(px):
        result = None
        for sy in range(NY):
            left = xg[sy, rows(NZH * px, NZH, 1)].reshape(NZH * 96, NC * TOK_DEV)
            term = dot(left, gk[sy].reshape(NC * TOK_DEV, KD))
            result = term if result is None else result + term
        return result.reshape(NZH, 96, KD)

    for dx in (2, 1, 3):
        px = x_peer(dx, 1)
        wp[px] = product(px).astype(BF)
        w_copy(dx, 1).start()
    wsum[...] = product(x)
    for dx in (1, 3, 2):
        w_copy(dx, -1).wait_recv()
        wsum[...] += wr[dx - 1].astype(F32)
    for pz in range(NZ):
        zf[pz] = fold(wsum[pz // NZL, (pz % NZL) * 24 : (pz % NZL + 1) * 24, :])
    zp[...] = zf[...].astype(BF)

    def p_copy(dz, sign):
        pz = z_peer(dz, sign)
        return remote(zp.at[pz], zq.at[dz - 1], p_send.at[dz - 1], p_recv.at[dz - 1], z_device(pz))

    for dz in (4, 3, 5, 2, 6, 1, 7):
        p_copy(dz, 1).start()
    share = zf[z]
    for dz in range(1, NZ):
        p_copy(dz, -1).wait_recv()
        share = share + zq[dz - 1].astype(F32)
    weight_grad = unfold(share) * (1.0 / (TOK_DEV * NY * NZ * NX * NC))
    moment = BETA_ONE * first[0] + (1.0 - BETA_ONE) * weight_grad
    square = BETA_TWO * second[0] + (1.0 - BETA_TWO) * weight_grad * weight_grad
    first_hat = moment / (1.0 - BETA_ONE**STEP_COUNT)
    second_hat = square / (1.0 - BETA_TWO**STEP_COUNT)
    old = master[0]
    fresh = old - LEARN_RATE * (first_hat / (jnp.sqrt(second_hat) + ADAM_EPS) + DECAY * old)
    nwp[...] = fold(fresh).astype(BF)

    def n_copy(i, sign):
        py, pz = data_peer(i, sign)
        slot = lax.axis_index("dp") if sign > 0 else py * NZL + pz
        return remote(nwp, nwr.at[slot], n_send.at[i], n_recv.at[i], device(py, pz, x, z_hi, core))

    for i in range(len(data)):
        n_copy(i, 1).start()
    nwr[lax.axis_index("dp")] = nwp[...]
    new_first[0] = moment
    new_second[0] = square
    new_master[0] = fresh
    for i in range(len(data)):
        n_copy(i, -1).wait_recv()
    for pair in range(NY * NZL // 2):
        both = [unfold(nwr[2 * pair + i].astype(F32)) for i in range(2)]
        new_weight[0, pair * 48 : (pair + 1) * 48, :] = jnp.concatenate(both, axis=0).astype(BF)

    dq_copy.wait()
    v_copy.wait()
    for copy in mine[3:6] + mine[7:]:
        copy.wait()
    for dx in range(1, NX):

        @pl.when(x >= dx)
        def _():
            kv_copy(dx, 1).wait_send()

        w_copy(dx, 1).wait_send()
    z_copy.wait_send()
    for i in range(len(group)):
        x_copy(i, 1).wait_send()
        short_copy(i, 1).wait_send()
        long_copy(i, 1).wait_send()
    for dz in range(1, NZ):
        p_copy(dz, 1).wait_send()
    for i in range(len(data)):
        n_copy(i, 1).wait_send()


ANY = pl.BlockSpec(memory_space=pl.ANY)
VMEM = pl.BlockSpec(memory_space=pltpu.VMEM)
DMA = pltpu.SemaphoreType.DMA


def array(shape, dtype=BF):
    return jax.ShapeDtypeStruct(shape, dtype)


def params(collective_id=None):
    if collective_id is None:
        return pltpu.CompilerParams(vmem_limit_bytes=40 << 20)
    return pltpu.CompilerParams(
        vmem_limit_bytes=40 << 20, collective_id=collective_id, has_side_effects=True
    )


def on_device(
    layer_inputs, queries, key_states, value_states, output_grad, short_segments, master, first_moment, second_moment
):
    keys = NX * NZH * CHUNK
    qb, gb, kb, vb, sdq, sgk, sgv, xt = pl.pallas_call(
        gather_kernel,
        name="gather_short",
        out_shape=[
            array((CHUNK, HALF_Q)),
            array((CHUNK, HALF_Q)),
            array((keys, HALF_K)),
            array((keys, HALF_K)),
            array((SHORT_DEV, QD)),
            array((SHORT_DEV, KD)),
            array((SHORT_DEV, KD)),
            array((D, TOK_DEV)),
        ],
        in_specs=[ANY] * 5 + [VMEM],
        out_specs=[ANY] * 4 + [VMEM] * 4,
        scratch_shapes=[
            pltpu.VMEM((SHORT_DEV, QD), BF),
            pltpu.VMEM((SHORT_DEV, QD), BF),
            pltpu.VMEM((SHORT_DEV, KD), BF),
            pltpu.VMEM((SHORT_DEV, KD), BF),
            pltpu.VMEM((TOK_DEV, D), BF),
            DMA((5,)),
            DMA((4,)),
            DMA((2,)),
            DMA((2,)),
            DMA((2, 9)),
            DMA((2, 9)),
            DMA((2, 3)),
            DMA((2, 3)),
        ],
        compiler_params=params(1),
    )(queries, output_grad, key_states, value_states, layer_inputs, short_segments)
    dq, dkv = pl.pallas_call(
        long_kernel,
        name="long_documents",
        out_shape=[array((CHUNK, HALF_Q)), array((NX * NZH, CHUNK, 2 * HALF_K))],
        in_specs=[VMEM] * 4,
        out_specs=[VMEM] * 2,
        scratch_shapes=[
            pltpu.VMEM((keys, WIDE), F32),
            pltpu.VMEM((keys, WIDE), F32),
            pltpu.VMEM((keys, WIDE), BF),
            pltpu.VMEM((keys, HEAD), F32),
            pltpu.VMEM((keys, HEAD), F32),
        ],
        compiler_params=params(),
    )(qb, gb, kb, vb)
    xt = xt.reshape(NX * NZH, NC, NY, 96, TOK_DEV)
    tile = (1, 24, KD)
    return pl.pallas_call(
        update_kernel,
        name="update",
        out_shape=[
            array((TOK_DEV, QD)),
            array((TOK_DEV, KD)),
            array(tile, F32),
            array(tile, F32),
            array(tile, F32),
            array((1, 384, KD)),
        ],
        in_specs=[ANY] * 6 + [VMEM] * 3,
        out_specs=[ANY] * 2 + [VMEM] * 4,
        scratch_shapes=[
            pltpu.VMEM((NZH, CHUNK, 2 * HALF_K), BF),
            pltpu.VMEM((NZH, CHUNK, 2 * HALF_K), F32),
            pltpu.VMEM((NX - 1, NZH, CHUNK, 2 * HALF_K), BF),
            pltpu.VMEM((CHUNK, 2 * HALF_K), BF),
            pltpu.VMEM((CHUNK, 2 * HALF_K), BF),
            pltpu.VMEM((NC, LONG_DEV, HALF_K), BF),
            pltpu.VMEM((NC, LONG_DEV, HALF_K), BF),
            pltpu.VMEM((NY, NX * NZH, 96, NC * TOK_DEV), BF),
            pltpu.VMEM((NY, NC, TOK_DEV, KD), BF),
            pltpu.VMEM((NX, NZH, 96, KD), BF),
            pltpu.VMEM((NX - 1, NZH, 96, KD), BF),
            pltpu.VMEM((NZH, 96, KD), F32),
            pltpu.VMEM((NZ, 96, 128), F32),
            pltpu.VMEM((NZ, 96, 128), BF),
            pltpu.VMEM((NZ - 1, 96, 128), BF),
            pltpu.VMEM((96, 128), BF),
            pltpu.VMEM((NY * NZL, 96, 128), BF),
            DMA((8,)),
            DMA((1,)), DMA((1,)),
            DMA((3,)), DMA((3,)),
            DMA((1,)), DMA((1,)),
            DMA((7,)), DMA((7,)),
            DMA((7,)), DMA((7,)),
            DMA((7,)), DMA((7,)),
            DMA((1,)), DMA((1,)),
            DMA((3,)), DMA((3,)),
            DMA((7,)), DMA((7,)),
            DMA((15,)), DMA((15,)),
        ],
        compiler_params=params(2),
    )(dq, dkv, xt, sdq, sgk, sgv, master, first_moment, second_moment)


def solution(mesh):
    tokens = P(("dp", "ctx"), None)
    shard = P("ctx", "dp", None)
    return jax.shard_map(
        on_device,
        mesh=mesh,
        in_specs=(tokens,) * 6 + (shard,) * 3,
        out_specs=(tokens, tokens, shard, shard, shard, P("ctx", None, None)),
        check_vma=False,
    )
```

```python
import functools

import jax
import jax.numpy as jnp
from jax import lax
from jax.experimental import pallas as pl
from jax.experimental.pallas import tpu as pltpu
from jax.sharding import PartitionSpec as P

D = 6144
HEAD = 128
GROUPS = 12
HK = 4
SHORT_FIRST = 2
LONG_DEV = 64
SHORT_DEV = 64
TOK_DEV = 128
CHUNK = 128
KD = 512
QD = 6144
HALF_Q = 3072
HALF_K = 256
NY, NZL, NX, NZH, NC = 4, 4, 4, 2, 2
NZ = NZL * NZH

LEARN_RATE = 0.001
BETA_ONE = 0.9
BETA_TWO = 0.95
ADAM_EPS = 1e-08
DECAY = 0.1
STEP_COUNT = 10

MESH = pl.DeviceIdType.MESH
FACTOR = HEAD**-0.5
EXP_FACTOR = FACTOR * 1.4426950408889634
NEG = -1e30
BF = jnp.bfloat16
VMEM_LIMIT = 63 << 20
F32 = jnp.float32
NT = (((1,), (1,)), ((), ()))
TN = (((0,), (0,)), ((), ()))


def dot(a, b, dims=(((1,), (0,)), ((), ()))):
    return lax.dot_general(a, b, dims, preferred_element_type=F32)


def place():
    d = lax.axis_index("dp")
    c = lax.axis_index("ctx")
    return d // NZL, d % NZL, c // (NZH * NC), (c // NC) % NZH, c % NC


def device(y, z_lo, x, z_hi, core):
    return (y * NZL + z_lo, (x * NZH + z_hi) * NC + core)


def remote(src, dst, send, recv, peer):
    return pltpu.make_async_remote_copy(
        src_ref=src, dst_ref=dst, send_sem=send, recv_sem=recv, device_id=peer, device_id_type=MESH
    )


def lanes(start, size):
    return pl.ds(pl.multiple_of(start, 128), size)


def rows(start, size, unit):
    return pl.ds(pl.multiple_of(start, unit), size)


def short_mask(seg_ref):
    segment = seg_ref[...]
    square = jnp.broadcast_to(segment, (SHORT_DEV, SHORT_DEV))
    diag = lax.broadcasted_iota(jnp.int32, (SHORT_DEV, SHORT_DEV), 0) == lax.broadcasted_iota(
        jnp.int32, (SHORT_DEV, SHORT_DEV), 1
    )
    column = jnp.sum(jnp.where(diag, square.astype(F32), 0.0), axis=1, keepdims=True)
    row = jnp.concatenate([segment.astype(F32)] * 2, axis=1)
    key = lax.broadcasted_iota(jnp.int32, (SHORT_DEV, 128), 0)
    token = lax.broadcasted_iota(jnp.int32, (SHORT_DEV, 128), 1) % SHORT_DEV
    pair = jnp.where((column == row) & (key <= token), 0.0, NEG)
    return jnp.concatenate([pair] * (GROUPS // 2), axis=1)


def short_head(kh, bias, q_ref, g_ref, k_ref, v_ref, dq_ref, dk_ref, dv_ref):
    width = GROUPS * HEAD
    q = q_ref[:, lanes(kh * width, width)]
    g = g_ref[:, lanes(kh * width, width)]
    k = k_ref[:, lanes(kh * HEAD, HEAD)]
    v = v_ref[:, lanes(kh * HEAD, HEAD)]
    q = jnp.concatenate([q[:, i * HEAD : (i + 1) * HEAD] for i in range(GROUPS)], axis=0)
    g = jnp.concatenate([g[:, i * HEAD : (i + 1) * HEAD] for i in range(GROUPS)], axis=0)
    scores = dot(k, q, NT) + bias
    top = jnp.max(scores, axis=0, keepdims=True)
    raised = jnp.exp2((scores - top) * EXP_FACTOR)
    probs = raised * (1.0 / jnp.sum(raised, axis=0, keepdims=True))
    probs_low = probs.astype(BF)
    grad_probs = dot(v, g, NT)
    delta = jnp.sum(probs_low.astype(F32) * grad_probs, axis=0, keepdims=True)
    grad_scores = (probs * FACTOR * (grad_probs - delta)).astype(BF)
    dv_ref[:, lanes(kh * HEAD, HEAD)] = dot(probs_low, g).astype(BF)
    dk_ref[kh % 2, :, lanes(kh // 2 * HEAD, HEAD)] = dot(grad_scores, q).astype(BF)
    dq = dot(grad_scores, k, TN).astype(BF)
    dq_ref[:, lanes(kh * width, width)] = jnp.concatenate(
        [dq[i * SHORT_DEV : (i + 1) * SHORT_DEV] for i in range(GROUPS)], axis=1
    )


WIDE = 4 * CHUNK
STEPS = GROUPS // 4
OWN = NZH * CHUNK


def long_head(keys, hh, z_hi, q, g, k, v, dq, scores, grads, low, acc_k, acc_v, kt):
    chunks = keys // CHUNK
    head = lanes(hh * HEAD, HEAD)
    acc_k[0:keys, :] = jnp.zeros((keys, HEAD), F32)
    acc_v[0:keys, :] = jnp.zeros((keys, HEAD), F32)
    kt[:, 0:keys] = k[0:keys, head].T

    @pl.loop(0, STEPS)
    def _(p):
        col = lanes((hh * STEPS + p) * WIDE, WIDE)
        q4, g4 = q[:, col], g[:, col]
        qs = jnp.concatenate([q4[:, i * HEAD : (i + 1) * HEAD] for i in range(4)], axis=0)
        gs = jnp.concatenate([g4[:, i * HEAD : (i + 1) * HEAD] for i in range(4)], axis=0)
        top = None
        for n in range(chunks):
            at = slice(n * CHUNK, (n + 1) * CHUNK)
            s = dot(k[at, head], qs, NT)
            if n >= chunks - 2:
                key = lax.broadcasted_iota(jnp.int32, (CHUNK, WIDE), 0) + (n - chunks + 2) * CHUNK
                token = lax.broadcasted_iota(jnp.int32, (CHUNK, WIDE), 1) % CHUNK + z_hi * CHUNK
                s = jnp.where(key <= token, s, NEG)
            scores[at, :] = s
            m = jnp.max(s, axis=0, keepdims=True)
            top = m if top is None else jnp.maximum(top, m)
        total = None
        for n in range(chunks):
            at = slice(n * CHUNK, (n + 1) * CHUNK)
            e = jnp.exp2((scores[at, :] - top) * EXP_FACTOR)
            scores[at, :] = e
            part = jnp.sum(e, axis=0, keepdims=True)
            total = part if total is None else total + part
            grads[at, :] = dot(v[at, head], gs, NT)
        scale = 1.0 / total
        delta = None
        for n in range(chunks):
            at = slice(n * CHUNK, (n + 1) * CHUNK)
            pb = (scores[at, :] * scale).astype(BF)
            part = jnp.sum(pb.astype(F32) * grads[at, :], axis=0, keepdims=True)
            delta = part if delta is None else delta + part
            acc_v[at, :] += dot(pb, gs)
        scale = scale * FACTOR
        for n in range(chunks):
            at = slice(n * CHUNK, (n + 1) * CHUNK)
            ds = (scores[at, :] * scale * (grads[at, :] - delta)).astype(BF)
            low[at, :] = ds
            acc_k[at, :] += dot(ds, qs)
        out = dot(kt[:, 0:keys], low[0:keys, :]).astype(BF).T
        dq[:, col] = jnp.concatenate([out[i * CHUNK : (i + 1) * CHUNK] for i in range(4)], axis=1)


def fold(a):
    return jnp.concatenate([a[:, :128], a[:, 128:]], axis=0)


def kernel(
    q_hbm, g_hbm, k_hbm, v_hbm, x_hbm, seg_ref, master, first, second,
    gq, gv, new_master, new_first, new_second, new_weight,
    qs, gs, ks, vs, xs, xt, sdq, sgk, sgv,
    qb, gb, kb, vb, dq, scores, grads, low, acc_k, acc_v, kt, dks, dvs, totk, totv,
    rxk, rxv, zsk, zrk, zsv, zrv, gkl, gvl, xg, gk, wp, wr, wsum, zf, zp, zq, nwr,
    load_sem, own_sem, q_send, q_recv, kv_send, kv_recv, fw_send, fw_recv, dq_send, dq_recv,
    rk_send, rk_recv, rv_send, rv_recv, zk_send, zk_recv, zv_send, zv_recv, x_send, x_recv,
    s_send, s_recv, l_send, l_recv, v_send, v_recv, w_send, w_recv, p_send, p_recv,
    nz_send, nz_recv, ny_send, ny_recv,
):
    y, z_lo, x, z_hi, core = place()
    c = lax.axis_index("ctx")
    z = z_hi * NZL + z_lo
    other = 1 - core
    sibling = device(y, z_lo, x, z_hi, other)
    partner = device(y, z_lo, x, 1 - z_hi, core)
    early, late = pl.ds(0, LONG_DEV), pl.ds(LONG_DEV, SHORT_DEV)
    my_tokens = lanes(core * TOK_DEV, TOK_DEV)

    loads = [pltpu.make_async_copy(x_hbm, xs, load_sem.at[4])]
    loads += [
        pltpu.make_async_copy(hbm.at[late, :], vmem, load_sem.at[i])
        for i, (hbm, vmem) in enumerate(((q_hbm, qs), (g_hbm, gs), (k_hbm, ks), (v_hbm, vs)))
    ]
    own_rows = rows(c * LONG_DEV, LONG_DEV, 64)
    pair_rows = rows(core * LONG_DEV, LONG_DEV, 64)
    loads += [
        pltpu.make_async_copy(src.at[early, lanes(core * width, width)], dst.at[where, :], own_sem.at[i])
        for i, (src, dst, width, where) in enumerate(
            (
                (k_hbm, kb, HALF_K, own_rows),
                (v_hbm, vb, HALF_K, own_rows),
                (q_hbm, qb, HALF_Q, pair_rows),
                (g_hbm, gb, HALF_Q, pair_rows),
            )
        )
    ]
    for copy in loads:
        copy.start()

    def x_peer(dx, sign):
        return (x + sign * dx + NX) % NX

    def z_peer(dz, sign):
        return (z + sign * dz + NZ) % NZ

    def z_device(pz):
        return device(y, pz % NZL, x, pz // NZL, core)

    group = [(dy, dc) for dy in range(NY) for dc in range(NC) if (dy, dc) != (0, 0)]

    def group_peer(i, sign):
        dy, dc = group[i]
        return (y + sign * dy + NY) % NY, (core + dc) % NC

    peers = [device(y, z_lo, x_peer(dx, 1), z_hi, (core + dc) % NC) for dx in range(1, NX) for dc in range(NC)]
    peers += [z_device(z_peer(dz, 1)) for dz in range(1, NZ)]
    peers.append(device(y, z_lo, x, 1 - z_hi, other))
    for i in range(len(group)):
        py, pc = group_peer(i, 1)
        peers.append(device(py, z_lo, x, z_hi, pc))
    barrier = pltpu.get_barrier_semaphore()
    for peer in peers:
        pl.semaphore_signal(barrier, inc=1, device_id=peer, device_id_type=MESH)

    loads[0].wait()

    @pl.loop(0, D // 128)
    def _(i):
        at = i * 128
        xt[rows(at, 128, 128), :] = xs[:, lanes(at, 128)].T

    pl.semaphore_wait(barrier, len(peers))

    def kv_copies(px, pz, pc, slot, sending):
        if sending:
            col, where = pc, own_rows
        else:
            col, where = core, rows(((px * NZH + pz) * NC + pc) * LONG_DEV, LONG_DEV, 64)
        return [
            remote(
                src.at[early, lanes(col * HALF_K, HALF_K)], dst.at[where, :],
                kv_send.at[n, slot], kv_recv.at[n, slot], device(y, z_lo, px, pz, pc),
            )
            for n, (src, dst) in enumerate(((k_hbm, kb), (v_hbm, vb)))
        ]

    def partner_copies(dc, sending):
        return kv_copies(x, 1 - z_hi, (core + dc) % NC, dc, sending)

    def sibling_copies(sending):
        return kv_copies(x, z_hi, other, 2, sending)

    def x_copies(dx, dc, sending):
        return kv_copies(x + dx if sending else x - dx, z_hi, (core + dc) % NC, 1 + 2 * dx + dc, sending)

    for dc in range(NC):
        for copy in partner_copies(dc, True):
            copy.start()
    for dx in range(1, NX):

        @pl.when(x + dx < NX)
        def _():
            for dc in range(NC):
                for copy in x_copies(dx, dc, True):
                    copy.start()

    swaps = [
        remote(
            src.at[early, lanes(other * HALF_Q, HALF_Q)], dst.at[pair_rows, :], q_send.at[n], q_recv.at[n], sibling
        )
        for n, (src, dst) in enumerate(((q_hbm, qb), (g_hbm, gb)))
    ]
    for copy in sibling_copies(True) + swaps:
        copy.start()

    def x_copy(i, sign):
        py, pc = group_peer(i, sign)
        sy, sc = (y, core) if sign > 0 else (py, pc)
        return remote(
            xt.reshape(NX * NZH, NC, NY, 96, TOK_DEV).at[:, pc, py],
            xg.at[sy, :, :, lanes(sc * TOK_DEV, TOK_DEV)],
            x_send.at[i], x_recv.at[i], device(py, z_lo, x, z_hi, pc),
        )

    for i in range(len(group)):
        x_copy(i, 1).start()
    mine = [
        pltpu.make_async_copy(
            xt.reshape(NX * NZH, NC, NY, 96, TOK_DEV).at[:, core, y], xg.at[y, :, :, my_tokens], own_sem.at[4]
        )
    ]
    mine[0].start()

    for copy in loads[1:5]:
        copy.wait()
    bias = short_mask(seg_ref)

    def heads(start, stop):
        @pl.loop(start, stop)
        def _(kh):
            short_head(kh, bias, qs, gs, ks, vs, sdq, sgk, sgv)

    heads(0, SHORT_FIRST)
    for dc in range(NC):
        for copy in partner_copies(dc, False):
            copy.wait_recv()

    def forward(dx, sending):
        px = x + dx if sending else x - dx
        where = rows(((x if sending else px) * NZH + 1 - z_hi) * CHUNK, CHUNK, 128)
        return [
            remote(
                b.at[where, :], b.at[where, :], fw_send.at[n, dx - 1], fw_recv.at[n, dx - 1],
                device(y, z_lo, px, z_hi, core),
            )
            for n, b in enumerate((kb, vb))
        ]

    for dx in range(1, NX):

        @pl.when(x + dx < NX)
        def _():
            for copy in forward(dx, True):
                copy.start()

    heads(SHORT_FIRST, HK)

    def short_copy(i, sign):
        py, pc = group_peer(i, sign)
        sy, sc = (y, core) if sign > 0 else (py, pc)
        return remote(
            sgk, gk.at[:, sy, sc, late, :], s_send.at[i], s_recv.at[i], device(py, z_lo, x, z_hi, pc)
        )

    for i in range(len(group)):
        short_copy(i, 1).start()
    mine += [
        pltpu.make_async_copy(sgk, gk.at[:, y, core, late, :], own_sem.at[5]),
        pltpu.make_async_copy(sdq, gq.at[late, :], own_sem.at[6]),
        pltpu.make_async_copy(sgv, gv.at[late, :], own_sem.at[7]),
    ]
    for copy in mine[1:]:
        copy.start()

    for copy in loads[5:]:
        copy.wait()
    for copy in sibling_copies(False):
        copy.wait_recv()
    for dx in range(1, NX):

        @pl.when(x >= dx)
        def _():
            for dc in range(NC):
                for copy in x_copies(dx, dc, False):
                    copy.wait_recv()
            for copy in forward(dx, False):
                copy.wait_recv()

    for copy in swaps:
        copy.wait()

    def rk_copy(hh, dx, sending):
        px = x - dx if sending else x + dx
        at = rows((px if sending else x) * OWN, OWN, 256)
        return remote(
            dks.at[hh, at, :], rxk.at[dx - 1, hh], rk_send.at[hh, dx - 1], rk_recv.at[hh, dx - 1],
            device(y, z_lo, px, z_hi, core),
        )

    def rv_copy(dx, sending):
        px = x - dx if sending else x + dx
        at = rows((px if sending else x) * OWN, OWN, 256)
        return remote(
            dvs.at[:, at, :], rxv.at[dx - 1], rv_send.at[dx - 1], rv_recv.at[dx - 1],
            device(y, z_lo, px, z_hi, core),
        )

    def zk_copy(hh):
        return remote(zsk.at[hh], zrk.at[hh], zk_send.at[hh], zk_recv.at[hh], partner)

    zv_copy = remote(zsv, zrv, zv_send.at[0], zv_recv.at[0], partner)
    ours = rows(z_hi * CHUNK, CHUNK, 128)
    theirs = rows((1 - z_hi) * CHUNK, CHUNK, 128)

    @pl.loop(0, 2)
    def _(hh):
        for n in range(NX):

            @pl.when(x == n)
            def _():
                keys, below = (n + 1) * OWN, n * OWN
                long_head(keys, hh, z_hi, qb, gb, kb, vb, dq, scores, grads, low, acc_k, acc_v, kt)
                if below:
                    dks[hh, 0:below, :] = acc_k[0:below, :].astype(BF)
                totk[hh] = acc_k[below:keys, :]
                if below:
                    dvs[hh, 0:below, :] = acc_v[0:below, :].astype(BF)
                totv[hh] = acc_v[below:keys, :]

        for dx in range(1, NX):

            @pl.when(x >= dx)
            def _():
                rk_copy(hh, dx, True).start()

        @pl.when(x == NX - 1)
        def _():
            zsk[hh] = totk[hh, theirs, :].astype(BF)
            zk_copy(hh).start()

    for dx in range(1, NX):

        @pl.when(x >= dx)
        def _():
            rv_copy(dx, True).start()

    dq_copy = remote(
        dq.at[rows(other * LONG_DEV, LONG_DEV, 64), :], gq.at[early, lanes(core * HALF_Q, HALF_Q)],
        dq_send.at[0], dq_recv.at[0], sibling,
    )
    dq_copy.start()
    mine.append(
        pltpu.make_async_copy(dq.at[pair_rows, :], gq.at[early, lanes(core * HALF_Q, HALF_Q)], own_sem.at[8])
    )
    mine[-1].start()

    def sum_over_x(hh):
        @pl.when(x < NX - 1)
        def _():
            for dx in range(1, NX):

                @pl.when(x + dx < NX)
                def _():
                    rk_copy(hh, dx, False).wait_recv()
                    totk[hh] += rxk[dx - 1, hh].astype(F32)

            zsk[hh] = totk[hh, theirs, :].astype(BF)
            zk_copy(hh).start()

    def long_copy(hh, i, sign):
        py, pc = group_peer(i, sign)
        sy, sc = (y, core) if sign > 0 else (py, pc)
        return remote(
            gkl.at[hh], gk.at[hh, sy, :, early, lanes(sc * HEAD, HEAD)], l_send.at[hh, i], l_recv.at[hh, i],
            device(py, z_lo, x, z_hi, pc),
        )

    def spread(hh):
        zk_copy(hh).wait_recv()
        both = (totk[hh, ours, :] + zrk[hh].astype(F32)).astype(BF)
        gkl[hh, 0] = both[:LONG_DEV]
        gkl[hh, 1] = both[LONG_DEV:]
        for i in range(len(group)):
            long_copy(hh, i, 1).start()
        copy = pltpu.make_async_copy(
            gkl.at[hh], gk.at[hh, y, :, early, lanes(core * HEAD, HEAD)], own_sem.at[9 + hh]
        )
        copy.start()
        return copy

    def w_copy(hh, dx, sign):
        px = x_peer(dx, sign)
        return remote(
            wp.at[hh, px], wr.at[hh, dx - 1], w_send.at[hh, dx - 1], w_recv.at[hh, dx - 1],
            device(y, z_lo, px, z_hi, core),
        )

    def product(hh, px):
        result = None
        for sy in range(NY):
            left = xg[sy, rows(NZH * px, NZH, 1)].reshape(NZH * 96, NC * TOK_DEV)
            term = dot(left, gk[hh, sy].reshape(NC * TOK_DEV, HALF_K))
            result = term if result is None else result + term
        return result.reshape(NZH, 96, HALF_K)

    def multiply(hh, own):
        own.wait()
        for i in range(len(group)):
            long_copy(hh, i, -1).wait_recv()
        for dx in (2, 1, 3):
            px = x_peer(dx, 1)
            wp[hh, px] = product(hh, px).astype(BF)
            w_copy(hh, dx, 1).start()
        wsum[hh] = product(hh, x)

    def p_copy(hh, dz, sign):
        pz = z_peer(dz, sign)
        return remote(
            zp.at[hh, pz], zq.at[hh, dz - 1], p_send.at[hh, dz - 1], p_recv.at[hh, dz - 1], z_device(pz)
        )

    def reduce_x(hh):
        for dx in (1, 3, 2):
            w_copy(hh, dx, -1).wait_recv()
            wsum[hh] += wr[hh, dx - 1].astype(F32)
        for pz in range(NZ):
            zf[hh, pz] = fold(wsum[hh, pz // NZL, (pz % NZL) * 24 : (pz % NZL + 1) * 24, :])
        zp[hh] = zf[hh].astype(BF)
        for dz in (4, 3, 5, 2, 6, 1, 7):
            p_copy(hh, dz, 1).start()

    d = lax.axis_index("dp")

    def nz_copy(hh, dz, sign):
        pz = (z_lo + sign * dz + NZL) % NZL
        slot = d if sign > 0 else y * NZL + pz
        return remote(
            nwr.at[hh, slot], nwr.at[hh, slot], nz_send.at[hh, dz - 1], nz_recv.at[hh, dz - 1],
            device(y, pz, x, z_hi, core),
        )

    def ny_copy(hh, dy, dz, sign):
        py = (y + sign * dy + NY) % NY
        slot = (y if sign > 0 else py) * NZL + (z_lo - dz + NZL) % NZL
        return remote(
            nwr.at[hh, slot], nwr.at[hh, slot], ny_send.at[hh, dy - 1, dz], ny_recv.at[hh, dy - 1, dz],
            device(py, z_lo, x, z_hi, core),
        )

    def update(hh):
        share = zf[hh, z]
        for dz in range(1, NZ):
            p_copy(hh, dz, -1).wait_recv()
            share = share + zq[hh, dz - 1].astype(F32)
        share = share * (1.0 / (TOK_DEV * NY * NZ * NX * NC))
        fresh = []
        for b in range(2):
            col = slice((2 * b + hh) * 128, (2 * b + hh + 1) * 128)
            grad = share[b * 24 : (b + 1) * 24]
            moment = BETA_ONE * first[0, :, col] + (1.0 - BETA_ONE) * grad
            square = BETA_TWO * second[0, :, col] + (1.0 - BETA_TWO) * grad * grad
            first_hat = moment / (1.0 - BETA_ONE**STEP_COUNT)
            second_hat = square / (1.0 - BETA_TWO**STEP_COUNT)
            old = master[0, :, col]
            new = old - LEARN_RATE * (first_hat / (jnp.sqrt(second_hat) + ADAM_EPS) + DECAY * old)
            new_first[0, :, col] = moment
            new_second[0, :, col] = square
            new_master[0, :, col] = new
            fresh.append(new)
        nwr[hh, d] = jnp.concatenate(fresh, axis=0).astype(BF)
        for dz in range(1, NZL):
            nz_copy(hh, dz, 1).start()
        for dy in range(1, NY):
            ny_copy(hh, dy, 0, 1).start()

    def pass_on(hh):
        for dz in (1, 3, 2):
            nz_copy(hh, dz, -1).wait_recv()
            for dy in (2, 1, 3):
                ny_copy(hh, dy, dz, 1).start()

    def finish(hh):
        for dy in range(1, NY):
            for dz in range(NZL):
                ny_copy(hh, dy, dz, -1).wait_recv()
        for pair in range(NY * NZL // 2):
            two = [nwr[hh, 2 * pair + i].astype(F32) for i in range(2)]
            for b in range(2):
                both = jnp.concatenate([t[b * 24 : (b + 1) * 24] for t in two], axis=0)
                new_weight[0, pair * 48 : (pair + 1) * 48, (2 * b + hh) * 128 : (2 * b + hh + 1) * 128] = both.astype(BF)

    sum_over_x(0)
    own = spread(0)
    sum_over_x(1)
    mine[0].wait()
    mine[1].wait()
    for i in range(len(group)):
        x_copy(i, -1).wait_recv()
        short_copy(i, -1).wait_recv()
    multiply(0, own)
    own = spread(1)

    @pl.when(x < NX - 1)
    def _():
        for dx in range(1, NX):

            @pl.when(x + dx < NX)
            def _():
                rv_copy(dx, False).wait_recv()
                totv[...] += rxv[dx - 1].astype(F32)

    zsv[...] = totv[:, theirs, :].astype(BF)
    zv_copy.start()
    multiply(1, own)
    reduce_x(0)
    zv_copy.wait_recv()
    for hh in range(2):
        both = (totv[hh, ours, :] + zrv[hh].astype(F32)).astype(BF)
        gvl[0, :, hh * HEAD : (hh + 1) * HEAD] = both[:LONG_DEV]
        gvl[1, :, hh * HEAD : (hh + 1) * HEAD] = both[LONG_DEV:]
    my_keys = lanes(core * HALF_K, HALF_K)
    v_copy = remote(gvl.at[other], gv.at[early, my_keys], v_send.at[0], v_recv.at[0], sibling)
    v_copy.start()
    mine.append(pltpu.make_async_copy(gvl.at[core], gv.at[early, my_keys], own_sem.at[11]))
    mine[-1].start()
    update(0)
    reduce_x(1)
    pass_on(0)
    update(1)
    pass_on(1)
    finish(0)
    finish(1)

    for copy in mine[2:]:
        copy.wait()
    v_copy.wait()
    dq_copy.wait()
    zv_copy.wait_send()
    for copy in sibling_copies(True):
        copy.wait_send()
    for dc in range(NC):
        for copy in partner_copies(dc, True):
            copy.wait_send()
    for dx in range(1, NX):

        @pl.when(x + dx < NX)
        def _():
            for dc in range(NC):
                for copy in x_copies(dx, dc, True):
                    copy.wait_send()
            for copy in forward(dx, True):
                copy.wait_send()

        @pl.when(x >= dx)
        def _():
            for hh in range(2):
                rk_copy(hh, dx, True).wait_send()
            rv_copy(dx, True).wait_send()

    for i in range(len(group)):
        x_copy(i, 1).wait_send()
        short_copy(i, 1).wait_send()
    for hh in range(2):
        zk_copy(hh).wait_send()
        for i in range(len(group)):
            long_copy(hh, i, 1).wait_send()
        for dx in range(1, NX):
            w_copy(hh, dx, 1).wait_send()
        for dz in range(1, NZ):
            p_copy(hh, dz, 1).wait_send()
        for dz in range(1, NZL):
            nz_copy(hh, dz, 1).wait_send()
        for dy in range(1, NY):
            for dz in range(NZL):
                ny_copy(hh, dy, dz, 1).wait_send()


HBM = pl.BlockSpec(memory_space=pltpu.HBM)
VMEM = pl.BlockSpec(memory_space=pltpu.VMEM)
DMA = pltpu.SemaphoreType.DMA


def array(shape, dtype=BF):
    return jax.ShapeDtypeStruct(shape, dtype)


STORE_CUTS = 4


def store_kernel(*refs):
    sources, targets, held, (sem_in, sem_out) = refs[:6], refs[6:12], refs[12:18], refs[18:]
    cut = TOK_DEV // STORE_CUTS
    parts = [(0, pl.ds(i * cut, cut)) for i in range(STORE_CUTS)] + [(i, pl.ds(0, n)) for i, n in ((1, TOK_DEV), (2, 1), (3, 1), (4, 1), (5, 1))]
    loads = [
        pltpu.make_async_copy(sources[i].at[at], held[i].at[at], sem_in.at[n]) for n, (i, at) in enumerate(parts)
    ]
    stores = [
        pltpu.make_async_copy(held[i].at[at], targets[i].at[at], sem_out.at[n]) for n, (i, at) in enumerate(parts)
    ]
    for copy in loads:
        copy.start()
    for load, store in zip(loads, stores):
        load.wait()
        store.start()
    for copy in stores:
        copy.wait()


def on_device(
    layer_inputs, queries, key_states, value_states, output_grad, short_segments, master, first_moment, second_moment
):
    keys = NX * OWN
    tile = (1, 24, KD)
    pairs = lambda *shape: [DMA(shape), DMA(shape)]
    results = [
        array((TOK_DEV, QD)),
        array((TOK_DEV, KD)),
        array(tile, F32),
        array(tile, F32),
        array(tile, F32),
        array((1, 384, KD)),
    ]
    made = pl.pallas_call(
        kernel,
        name="step",
        out_shape=results,
        in_specs=[HBM] * 5 + [VMEM] * 4,
        out_specs=[HBM] * 2 + [VMEM] * 4,
        scratch_shapes=[
            pltpu.VMEM((SHORT_DEV, QD), BF),
            pltpu.VMEM((SHORT_DEV, QD), BF),
            pltpu.VMEM((SHORT_DEV, KD), BF),
            pltpu.VMEM((SHORT_DEV, KD), BF),
            pltpu.VMEM((TOK_DEV, D), BF),
            pltpu.VMEM((D, TOK_DEV), BF),
            pltpu.VMEM((SHORT_DEV, QD), BF),
            pltpu.VMEM((2, SHORT_DEV, HALF_K), BF),
            pltpu.VMEM((SHORT_DEV, KD), BF),
            pltpu.VMEM((CHUNK, HALF_Q), BF),
            pltpu.VMEM((CHUNK, HALF_Q), BF),
            pltpu.VMEM((keys, HALF_K), BF),
            pltpu.VMEM((keys, HALF_K), BF),
            pltpu.VMEM((CHUNK, HALF_Q), BF),
            pltpu.VMEM((keys, WIDE), F32),
            pltpu.VMEM((keys, WIDE), F32),
            pltpu.VMEM((keys, WIDE), BF),
            pltpu.VMEM((keys, HEAD), F32),
            pltpu.VMEM((keys, HEAD), F32),
            pltpu.VMEM((HEAD, keys), BF),
            pltpu.VMEM((2, keys, HEAD), BF),
            pltpu.VMEM((2, keys, HEAD), BF),
            pltpu.VMEM((2, OWN, HEAD), F32),
            pltpu.VMEM((2, OWN, HEAD), F32),
            pltpu.VMEM((NX - 1, 2, OWN, HEAD), BF),
            pltpu.VMEM((NX - 1, 2, OWN, HEAD), BF),
            pltpu.VMEM((2, CHUNK, HEAD), BF),
            pltpu.VMEM((2, CHUNK, HEAD), BF),
            pltpu.VMEM((2, CHUNK, HEAD), BF),
            pltpu.VMEM((2, CHUNK, HEAD), BF),
            pltpu.VMEM((2, NC, LONG_DEV, HEAD), BF),
            pltpu.VMEM((NC, LONG_DEV, HALF_K), BF),
            pltpu.VMEM((NY, NX * NZH, 96, NC * TOK_DEV), BF),
            pltpu.VMEM((2, NY, NC, TOK_DEV, HALF_K), BF),
            pltpu.VMEM((2, NX, NZH, 96, HALF_K), BF),
            pltpu.VMEM((2, NX - 1, NZH, 96, HALF_K), BF),
            pltpu.VMEM((2, NZH, 96, HALF_K), F32),
            pltpu.VMEM((2, NZ, 48, 128), F32),
            pltpu.VMEM((2, NZ, 48, 128), BF),
            pltpu.VMEM((2, NZ - 1, 48, 128), BF),
            pltpu.VMEM((2, NY * NZL, 48, 128), BF),
            DMA((5,)),
            DMA((12,)),
            *pairs(2),
            *pairs(2, 9),
            *pairs(2, 3),
            *pairs(1),
            *pairs(2, 3),
            *pairs(3),
            *pairs(2),
            *pairs(1),
            *pairs(7),
            *pairs(7),
            *pairs(2, 7),
            *pairs(1),
            *pairs(2, 3),
            *pairs(2, 7),
            *pairs(2, 3),
            *pairs(2, 3, 4),
        ],
        compiler_params=pltpu.CompilerParams(
            vmem_limit_bytes=VMEM_LIMIT, collective_id=1, has_side_effects=True
        ),
    )(
        queries, output_grad, key_states, value_states, layer_inputs, short_segments,
        master, first_moment, second_moment,
    )
    return pl.pallas_call(
        store_kernel,
        name="store",
        out_shape=results,
        in_specs=[HBM] * 6,
        out_specs=[HBM] * 6,
        scratch_shapes=[pltpu.VMEM(r.shape, r.dtype) for r in results]
        + [DMA((STORE_CUTS + 5,)), DMA((STORE_CUTS + 5,))],
        compiler_params=pltpu.CompilerParams(vmem_limit_bytes=VMEM_LIMIT),
    )(*made)


def solution(mesh):
    tokens = P(("dp", "ctx"), None)
    shard = P("ctx", "dp", None)
    return jax.shard_map(
        on_device,
        mesh=mesh,
        in_specs=(tokens,) * 6 + (shard,) * 3,
        out_specs=(tokens, tokens, shard, shard, shard, P("ctx", None, None)),
        check_vma=False,
    )
```

```python
import functools

import jax
import jax.numpy as jnp
from jax import lax
from jax.experimental import pallas as pl
from jax.experimental.pallas import tpu as pltpu
from jax.sharding import PartitionSpec as P

D = 6144
HEAD = 128
GROUPS = 12
HK = 4
SHORT_FIRST = 3
LONG_DEV = 64
SHORT_DEV = 64
TOK_DEV = 128
CHUNK = 128
KD = 512
QD = 6144
HALF_Q = 3072
HALF_K = 256
NY, NZL, NX, NZH, NC = 4, 4, 4, 2, 2
NZ = NZL * NZH

LEARN_RATE = 0.001
BETA_ONE = 0.9
BETA_TWO = 0.95
ADAM_EPS = 1e-08
DECAY = 0.1
STEP_COUNT = 10

MESH = pl.DeviceIdType.MESH
FACTOR = HEAD**-0.5
EXP_FACTOR = FACTOR * 1.4426950408889634
NEG = -1e30
BF = jnp.bfloat16
VMEM_LIMIT = 63 << 20
F32 = jnp.float32
NT = (((1,), (1,)), ((), ()))
TN = (((0,), (0,)), ((), ()))


def dot(a, b, dims=(((1,), (0,)), ((), ()))):
    return lax.dot_general(a, b, dims, preferred_element_type=F32)


def place():
    d = lax.axis_index("dp")
    c = lax.axis_index("ctx")
    return d // NZL, d % NZL, c // (NZH * NC), (c // NC) % NZH, c % NC


def device(y, z_lo, x, z_hi, core):
    return (y * NZL + z_lo, (x * NZH + z_hi) * NC + core)


def remote(src, dst, send, recv, peer):
    return pltpu.make_async_remote_copy(
        src_ref=src, dst_ref=dst, send_sem=send, recv_sem=recv, device_id=peer, device_id_type=MESH
    )


def lanes(start, size):
    return pl.ds(pl.multiple_of(start, 128), size)


def rows(start, size, unit):
    return pl.ds(pl.multiple_of(start, unit), size)


def short_mask(seg_ref):
    segment = seg_ref[...]
    square = jnp.broadcast_to(segment, (SHORT_DEV, SHORT_DEV))
    diag = lax.broadcasted_iota(jnp.int32, (SHORT_DEV, SHORT_DEV), 0) == lax.broadcasted_iota(
        jnp.int32, (SHORT_DEV, SHORT_DEV), 1
    )
    column = jnp.sum(jnp.where(diag, square.astype(F32), 0.0), axis=1, keepdims=True)
    row = jnp.concatenate([segment.astype(F32)] * 2, axis=1)
    key = lax.broadcasted_iota(jnp.int32, (SHORT_DEV, 128), 0)
    token = lax.broadcasted_iota(jnp.int32, (SHORT_DEV, 128), 1) % SHORT_DEV
    pair = jnp.where((column == row) & (key <= token), 0.0, NEG)
    return jnp.concatenate([pair] * (GROUPS // 2), axis=1)


def short_head(kh, bias, q_ref, g_ref, k_ref, v_ref, dq_ref, dk_ref, dv_ref):
    width = GROUPS * HEAD
    q = q_ref[:, lanes(kh * width, width)]
    g = g_ref[:, lanes(kh * width, width)]
    k = k_ref[:, lanes(kh * HEAD, HEAD)]
    v = v_ref[:, lanes(kh * HEAD, HEAD)]
    q = jnp.concatenate([q[:, i * HEAD : (i + 1) * HEAD] for i in range(GROUPS)], axis=0)
    g = jnp.concatenate([g[:, i * HEAD : (i + 1) * HEAD] for i in range(GROUPS)], axis=0)
    scores = dot(k, q, NT) + bias
    top = jnp.max(scores, axis=0, keepdims=True)
    raised = jnp.exp2((scores - top) * EXP_FACTOR)
    probs = raised * (1.0 / jnp.sum(raised, axis=0, keepdims=True))
    probs_low = probs.astype(BF)
    grad_probs = dot(v, g, NT)
    delta = jnp.sum(probs_low.astype(F32) * grad_probs, axis=0, keepdims=True)
    grad_scores = (probs * FACTOR * (grad_probs - delta)).astype(BF)
    dv_ref[:, lanes(kh * HEAD, HEAD)] = dot(probs_low, g).astype(BF)
    dk_ref[kh % 2, :, lanes(kh // 2 * HEAD, HEAD)] = dot(grad_scores, q).astype(BF)
    dq = dot(grad_scores, k, TN).astype(BF)
    dq_ref[:, lanes(kh * width, width)] = jnp.concatenate(
        [dq[i * SHORT_DEV : (i + 1) * SHORT_DEV] for i in range(GROUPS)], axis=1
    )


WIDE = 4 * CHUNK
STEPS = GROUPS // 4
OWN = NZH * CHUNK


def long_head(keys, hh, z_hi, q, g, kv, scores, grads, probs, low, acc_k):
    chunks = keys // CHUNK
    acc_k[0:keys, :] = jnp.zeros((keys, HEAD), F32)

    @pl.loop(0, STEPS)
    def _(p):
        col = lanes((hh * STEPS + p) * WIDE, WIDE)
        wide = lanes(p * WIDE, WIDE)
        q4, g4 = q[:, col], g[:, col]
        qs = jnp.concatenate([q4[:, i * HEAD : (i + 1) * HEAD] for i in range(4)], axis=0)
        gs = jnp.concatenate([g4[:, i * HEAD : (i + 1) * HEAD] for i in range(4)], axis=0)
        top = None
        for n in range(chunks):
            at = slice(n * CHUNK, (n + 1) * CHUNK)
            s = dot(kv[hh, at, :HEAD], qs, NT)
            if n >= chunks - 2:
                key = lax.broadcasted_iota(jnp.int32, (CHUNK, WIDE), 0) + (n - chunks + 2) * CHUNK
                token = lax.broadcasted_iota(jnp.int32, (CHUNK, WIDE), 1) % CHUNK + z_hi * CHUNK
                s = jnp.where(key <= token, s, NEG)
            scores[at, :] = s
            m = jnp.max(s, axis=0, keepdims=True)
            top = m if top is None else jnp.maximum(top, m)
        total = delta = None
        for n in range(chunks):
            at = slice(n * CHUNK, (n + 1) * CHUNK)
            e = jnp.exp2((scores[at, :] - top) * EXP_FACTOR)
            scores[at, :] = e
            dp = dot(kv[hh, at, HEAD:], gs, NT)
            grads[at, :] = dp
            part = jnp.sum(e, axis=0, keepdims=True)
            total = part if total is None else total + part
            part = jnp.sum(e * dp, axis=0, keepdims=True)
            delta = part if delta is None else delta + part
        scale = 1.0 / total
        delta = delta * scale
        for n in range(chunks):
            at = slice(n * CHUNK, (n + 1) * CHUNK)
            pr = scores[at, :] * scale
            probs[hh, at, wide] = pr.astype(BF)
            ds = (pr * ((grads[at, :] - delta) * FACTOR)).astype(BF)
            low[hh, at, wide] = ds
            acc_k[at, :] += dot(ds, qs)


def long_rest(keys, hh, g, kv, dq, probs, low, acc_v):
    width = GROUPS * HEAD
    col = lanes(hh * width, width)
    gr = g[:, col]
    gs = jnp.concatenate([gr[:, i * HEAD : (i + 1) * HEAD] for i in range(GROUPS)], axis=0)
    for n in range(keys // CHUNK):
        at = slice(n * CHUNK, (n + 1) * CHUNK)
        acc_v[at, :] = dot(probs[hh, at, :], gs)
    kt = kv[hh, 0:keys, :HEAD].T
    for p in range(STEPS):
        out = dot(kt, low[hh, 0:keys, p * WIDE : (p + 1) * WIDE]).astype(BF).T
        dq[:, lanes(hh * width + p * WIDE, WIDE)] = jnp.concatenate(
            [out[i * CHUNK : (i + 1) * CHUNK] for i in range(4)], axis=1
        )


def fold(a):
    return jnp.concatenate([a[:, :128], a[:, 128:]], axis=0)


def kernel(
    q_hbm, g_hbm, k_hbm, v_hbm, x_hbm, seg_hbm, master_hbm, first_hbm, second_hbm,
    gq, gv, master_out, first_out, second_out, weight_out,
    seg_ref, master, first, second, new_master, new_first, new_second, new_weight, kvs,
    qs, gs, ks, vs, xs, xt, sdq, sgk, sgv,
    qb, gb, kvb, dq, scores, grads, probs, low, acc_k, acc_v, dks, dvs, totk, totv,
    rxk, rxv, zsk, zrk, zsv, zrv, gkl, gvl, xg, gk, wp, wr, wsum, zf, zp, zq, nwr,
    load_sem, key_sem, own_sem, out_sem, q_send, q_recv, kv_send, kv_recv, fw_send, fw_recv, dq_send, dq_recv,
    rk_send, rk_recv, rv_send, rv_recv, zk_send, zk_recv, zv_send, zv_recv, x_send, x_recv,
    s_send, s_recv, l_send, l_recv, v_send, v_recv, w_send, w_recv, p_send, p_recv,
    nz_send, nz_recv, ny_send, ny_recv,
):
    y, z_lo, x, z_hi, core = place()
    c = lax.axis_index("ctx")
    z = z_hi * NZL + z_lo
    other = 1 - core
    sibling = device(y, z_lo, x, z_hi, other)
    partner = device(y, z_lo, x, 1 - z_hi, core)
    early, late = pl.ds(0, LONG_DEV), pl.ds(LONG_DEV, SHORT_DEV)
    my_tokens = lanes(core * TOK_DEV, TOK_DEV)

    own_rows = rows(c * LONG_DEV, LONG_DEV, 64)
    pair_rows = rows(core * LONG_DEV, LONG_DEV, 64)
    keyed = [
        pltpu.make_async_copy(
            src.at[early, pl.ds((2 * to + hh) * HEAD, HEAD)],
            kvs.at[to, hh, :, pl.ds(n * HEAD, HEAD)],
            key_sem.at[4 * to + 2 * hh + n],
        )
        for hh in range(2)
        for to in range(NC)
        for n, src in enumerate((k_hbm, v_hbm))
    ]
    loads = [
        pltpu.make_async_copy(hbm, vmem, load_sem.at[i])
        for i, (hbm, vmem) in enumerate(
            (
                (x_hbm, xs),
                (q_hbm.at[late, :], qs),
                (g_hbm.at[late, :], gs),
                (k_hbm.at[late, :], ks),
                (v_hbm.at[late, :], vs),
                (seg_hbm, seg_ref),
                (q_hbm.at[early, lanes(core * HALF_Q, HALF_Q)], qb.at[pair_rows, :]),
                (g_hbm.at[early, lanes(core * HALF_Q, HALF_Q)], gb.at[pair_rows, :]),
                (master_hbm, master),
                (first_hbm, first),
                (second_hbm, second),
            )
        )
    ]
    for copy in keyed + loads:
        copy.start()

    def x_peer(dx, sign):
        return (x + sign * dx + NX) % NX

    def z_peer(dz, sign):
        return (z + sign * dz + NZ) % NZ

    def z_device(pz):
        return device(y, pz % NZL, x, pz // NZL, core)

    group = [(dy, dc) for dy in range(NY) for dc in range(NC) if (dy, dc) != (0, 0)]

    def group_peer(i, sign):
        dy, dc = group[i]
        return (y + sign * dy + NY) % NY, (core + dc) % NC

    peers = [device(y, z_lo, x, 1 - z_hi, other)]
    peers += [z_device(z_peer(dz, 1)) for dz in (4, 3, 5, 2, 6, 1, 7)]
    peers += [device(y, z_lo, x_peer(dx, 1), z_hi, (core + dc) % NC) for dx in (2, 1, 3) for dc in (1, 0)]
    for i in range(len(group)):
        py, pc = group_peer(i, 1)
        peers.append(device(py, z_lo, x, z_hi, pc))
    barrier = pltpu.get_barrier_semaphore()
    for peer in peers:
        pl.semaphore_signal(barrier, inc=1, device_id=peer, device_id_type=MESH)

    loads[0].wait()

    @pl.loop(0, D // 1024)
    def _(i):
        for j in range(8):
            at = i * 1024 + j * 128
            xt[rows(at, 128, 128), :] = xs[:, lanes(at, 128)].T

    for copy in loads[1:6]:
        copy.wait()
    bias = short_mask(seg_ref)

    def heads(start, stop):
        @pl.loop(start, stop)
        def _(kh):
            short_head(kh, bias, qs, gs, ks, vs, sdq, sgk, sgv)

    heads(0, SHORT_FIRST)
    for copy in keyed:
        copy.wait()
    own_kv = pltpu.make_async_copy(kvs.at[core], kvb.at[:, own_rows, :], own_sem.at[4])
    own_kv.start()
    pl.semaphore_wait(barrier, len(peers))

    def kv_copy(hh, px, pz, pc, slot, sending):
        where = own_rows if sending else rows(((px * NZH + pz) * NC + pc) * LONG_DEV, LONG_DEV, 64)
        return remote(
            kvs.at[pc if sending else core, hh], kvb.at[hh, where, :], kv_send.at[hh, slot], kv_recv.at[hh, slot],
            device(y, z_lo, px, pz, pc),
        )

    def partner_copy(hh, dc, sending):
        return kv_copy(hh, x, 1 - z_hi, (core + dc) % NC, dc, sending)

    def sibling_copy(hh, sending):
        return kv_copy(hh, x, z_hi, other, 2, sending)

    def near_copy(hh, dx, dc, sending):
        return kv_copy(hh, x + dx if sending else x - dx, z_hi, (core + dc) % NC, 1 + 2 * dx + dc, sending)

    for hh in range(2):
        for dc in range(NC):
            partner_copy(hh, dc, True).start()
    for hh in range(2):
        for dx in range(1, NX):

            @pl.when(x + dx < NX)
            def _():
                for dc in range(NC):
                    near_copy(hh, dx, dc, True).start()

        sibling_copy(hh, True).start()

    swaps = [
        remote(
            src.at[early, lanes(other * HALF_Q, HALF_Q)], dst.at[pair_rows, :], q_send.at[n], q_recv.at[n], sibling
        )
        for n, (src, dst) in enumerate(((q_hbm, qb), (g_hbm, gb)))
    ]
    for copy in swaps:
        copy.start()

    def x_copy(i, sign):
        py, pc = group_peer(i, sign)
        sy, sc = (y, core) if sign > 0 else (py, pc)
        return remote(
            xt.reshape(NX * NZH, NC, NY, 96, TOK_DEV).at[:, pc, py],
            xg.at[sy, :, :, lanes(sc * TOK_DEV, TOK_DEV)],
            x_send.at[i], x_recv.at[i], device(py, z_lo, x, z_hi, pc),
        )

    for i in range(len(group)):
        x_copy(i, 1).start()
    mine = [
        pltpu.make_async_copy(
            xt.reshape(NX * NZH, NC, NY, 96, TOK_DEV).at[:, core, y], xg.at[y, :, :, my_tokens], own_sem.at[5]
        )
    ]
    mine[0].start()

    def forward(hh, dx, dc, sending):
        px = x + dx if sending else x - dx
        chip = (x if sending else px) * NZH + 1 - z_hi
        where = rows((chip * NC + (core + dc) % NC) * LONG_DEV, LONG_DEV, 64)
        return remote(
            kvb.at[hh, where, :], kvb.at[hh, where, :], fw_send.at[hh, dc, dx - 1], fw_recv.at[hh, dc, dx - 1],
            device(y, z_lo, px, z_hi, core),
        )

    for hh in range(2):
        for dc in range(NC):
            partner_copy(hh, dc, False).wait_recv()
            for dx in range(1, NX):

                @pl.when(x + dx < NX)
                def _():
                    forward(hh, dx, dc, True).start()

    heads(SHORT_FIRST, HK)

    def short_copy(i, sign):
        py, pc = group_peer(i, sign)
        sy, sc = (y, core) if sign > 0 else (py, pc)
        return remote(
            sgk, gk.at[:, sy, sc, late, :], s_send.at[i], s_recv.at[i], device(py, z_lo, x, z_hi, pc)
        )

    for i in range(len(group)):
        short_copy(i, 1).start()
    mine += [
        pltpu.make_async_copy(sgk, gk.at[:, y, core, late, :], own_sem.at[6]),
        pltpu.make_async_copy(sdq, gq.at[late, :], own_sem.at[7]),
        pltpu.make_async_copy(sgv, gv.at[late, :], own_sem.at[8]),
    ]
    for copy in mine[1:]:
        copy.start()

    for copy in loads[6:8]:
        copy.wait()
    own_kv.wait()
    for copy in swaps:
        copy.wait()

    def rk_copy(hh, dx, part, sending):
        px = x - dx if sending else x + dx
        chunk = (px if sending else x) * NZH + (1 - z_hi if part == 0 else z_hi)
        return remote(
            dks.at[hh, rows(chunk * CHUNK, CHUNK, 128), :], rxk.at[dx - 1, hh, part],
            rk_send.at[hh, part, dx - 1], rk_recv.at[hh, part, dx - 1], device(y, z_lo, px, z_hi, core),
        )

    def rv_copy(dx, sending):
        px = x - dx if sending else x + dx
        at = rows((px if sending else x) * OWN, OWN, 256)
        return remote(
            dvs.at[:, at, :], rxv.at[dx - 1], rv_send.at[dx - 1], rv_recv.at[dx - 1],
            device(y, z_lo, px, z_hi, core),
        )

    def zk_copy(hh):
        return remote(zsk.at[hh], zrk.at[hh], zk_send.at[hh], zk_recv.at[hh], partner)

    zv_copy = remote(zsv, zrv, zv_send.at[0], zv_recv.at[0], partner)
    ours = rows(z_hi * CHUNK, CHUNK, 128)
    theirs = rows((1 - z_hi) * CHUNK, CHUNK, 128)

    @pl.loop(0, 2)
    def _(hh):
        sibling_copy(hh, False).wait_recv()
        for n in range(NX):

            @pl.when(x == n)
            def _():
                keys, below = (n + 1) * OWN, n * OWN
                for dx in range(1, n + 1):
                    for dc in range(NC):
                        near_copy(hh, dx, dc, False).wait_recv()
                        forward(hh, dx, dc, False).wait_recv()
                long_head(keys, hh, z_hi, qb, gb, kvb, scores, grads, probs, low, acc_k)
                if below:
                    dks[hh, 0:below, :] = acc_k[0:below, :].astype(BF)
                totk[hh] = acc_k[below:keys, :]

        for part in range(2):
            for dx in range(1, NX):

                @pl.when(x >= dx)
                def _():
                    rk_copy(hh, dx, part, True).start()

        @pl.when(x == NX - 1)
        def _():
            zsk[hh] = totk[hh, theirs, :].astype(BF)
            zk_copy(hh).start()

    def sum_over_x(hh):
        for part in range(2):
            at = theirs if part == 0 else ours
            for dx in range(1, NX):

                @pl.when(x + dx < NX)
                def _():
                    rk_copy(hh, dx, part, False).wait_recv()
                    totk[hh, at, :] += rxk[dx - 1, hh, part].astype(F32)

            if part == 0:

                @pl.when(x < NX - 1)
                def _():
                    zsk[hh] = totk[hh, theirs, :].astype(BF)
                    zk_copy(hh).start()

    def long_copy(hh, i, sign):
        py, pc = group_peer(i, sign)
        sy, sc = (y, core) if sign > 0 else (py, pc)
        return remote(
            gkl.at[hh], gk.at[hh, sy, :, early, lanes(sc * HEAD, HEAD)], l_send.at[hh, i], l_recv.at[hh, i],
            device(py, z_lo, x, z_hi, pc),
        )

    def own_copy(hh):
        return pltpu.make_async_copy(
            gkl.at[hh], gk.at[hh, y, :, early, lanes(core * HEAD, HEAD)], own_sem.at[10 + hh]
        )

    def spread(hh):
        zk_copy(hh).wait_recv()
        both = (totk[hh, ours, :] + zrk[hh].astype(F32)).astype(BF)
        gkl[hh, 0] = both[:LONG_DEV]
        gkl[hh, 1] = both[LONG_DEV:]
        for i in range(len(group)):
            long_copy(hh, i, 1).start()
        own_copy(hh).start()

    @pl.when(x == NX - 1)
    def _():
        spread(0)

    @pl.loop(0, 2)
    def _(hh):
        for n in range(NX):

            @pl.when(x == n)
            def _():
                keys, below = (n + 1) * OWN, n * OWN
                long_rest(keys, hh, gb, kvb, dq, probs, low, acc_v)
                if below:
                    dvs[hh, 0:below, :] = acc_v[0:below, :].astype(BF)
                totv[hh] = acc_v[below:keys, :]

    for dx in range(1, NX):

        @pl.when(x >= dx)
        def _():
            rv_copy(dx, True).start()

    dq_copy = remote(
        dq.at[rows(other * LONG_DEV, LONG_DEV, 64), :], gq.at[early, lanes(core * HALF_Q, HALF_Q)],
        dq_send.at[0], dq_recv.at[0], sibling,
    )
    dq_copy.start()
    mine.append(
        pltpu.make_async_copy(dq.at[pair_rows, :], gq.at[early, lanes(core * HALF_Q, HALF_Q)], own_sem.at[9])
    )
    mine[-1].start()

    def w_copy(hh, dx, sign):
        px = x_peer(dx, sign)
        return remote(
            wp.at[hh, px], wr.at[hh, dx - 1], w_send.at[hh, dx - 1], w_recv.at[hh, dx - 1],
            device(y, z_lo, px, z_hi, core),
        )

    def product(hh, px):
        result = None
        for sy in range(NY):
            left = xg[sy, rows(NZH * px, NZH, 1)].reshape(NZH * 96, NC * TOK_DEV)
            term = dot(left, gk[hh, sy].reshape(NC * TOK_DEV, HALF_K))
            result = term if result is None else result + term
        return result.reshape(NZH, 96, HALF_K)

    def multiply(hh):
        own_copy(hh).wait()
        for i in range(len(group)):
            long_copy(hh, i, -1).wait_recv()
        for dx in (2, 1, 3):
            px = x_peer(dx, 1)
            wp[hh, px] = product(hh, px).astype(BF)
            w_copy(hh, dx, 1).start()
        wsum[hh] = product(hh, x)

    def p_copy(hh, dz, sign):
        pz = z_peer(dz, sign)
        return remote(
            zp.at[hh, pz], zq.at[hh, dz - 1], p_send.at[hh, dz - 1], p_recv.at[hh, dz - 1], z_device(pz)
        )

    def reduce_x(hh):
        for dx in (1, 3, 2):
            w_copy(hh, dx, -1).wait_recv()
            wsum[hh] += wr[hh, dx - 1].astype(F32)
        for pz in range(NZ):
            zf[hh, pz] = fold(wsum[hh, pz // NZL, (pz % NZL) * 24 : (pz % NZL + 1) * 24, :])
        zp[hh] = zf[hh].astype(BF)
        for dz in (4, 3, 5, 2, 6, 1, 7):
            p_copy(hh, dz, 1).start()

    d = lax.axis_index("dp")

    def nz_copy(hh, dz, sign):
        pz = (z_lo + sign * dz + NZL) % NZL
        slot = d if sign > 0 else y * NZL + pz
        return remote(
            nwr.at[hh, slot], nwr.at[hh, slot], nz_send.at[hh, dz - 1], nz_recv.at[hh, dz - 1],
            device(y, pz, x, z_hi, core),
        )

    def ny_copy(hh, dy, dz, sign):
        py = (y + sign * dy + NY) % NY
        slot = (y if sign > 0 else py) * NZL + (z_lo - dz + NZL) % NZL
        return remote(
            nwr.at[hh, slot], nwr.at[hh, slot], ny_send.at[hh, dy - 1, dz], ny_recv.at[hh, dy - 1, dz],
            device(py, z_lo, x, z_hi, core),
        )

    def update(hh):
        share = zf[hh, z]
        for dz in range(1, NZ):
            p_copy(hh, dz, -1).wait_recv()
            share = share + zq[hh, dz - 1].astype(F32)
        share = share * (1.0 / (TOK_DEV * NY * NZ * NX * NC))
        fresh = []
        for b in range(2):
            col = slice((2 * b + hh) * 128, (2 * b + hh + 1) * 128)
            grad = share[b * 24 : (b + 1) * 24]
            moment = BETA_ONE * first[0, :, col] + (1.0 - BETA_ONE) * grad
            square = BETA_TWO * second[0, :, col] + (1.0 - BETA_TWO) * grad * grad
            first_hat = moment / (1.0 - BETA_ONE**STEP_COUNT)
            second_hat = square / (1.0 - BETA_TWO**STEP_COUNT)
            old = master[0, :, col]
            new = old - LEARN_RATE * (first_hat / (jnp.sqrt(second_hat) + ADAM_EPS) + DECAY * old)
            new_first[0, :, col] = moment
            new_second[0, :, col] = square
            new_master[0, :, col] = new
            fresh.append(new)
        nwr[hh, d] = jnp.concatenate(fresh, axis=0).astype(BF)
        for dz in range(1, NZL):
            nz_copy(hh, dz, 1).start()
        for dy in range(1, NY):
            ny_copy(hh, dy, 0, 1).start()

    def pass_on(hh):
        for dz in (1, 3, 2):
            nz_copy(hh, dz, -1).wait_recv()
            for dy in (2, 1, 3):
                ny_copy(hh, dy, dz, 1).start()

    updated = [
        pltpu.make_async_copy(vmem, hbm, out_sem.at[i])
        for i, (vmem, hbm) in enumerate(
            ((new_master, master_out), (new_first, first_out), (new_second, second_out))
        )
    ]

    def weight_copy(hh, b):
        col = pl.ds((2 * b + hh) * 128, 128)
        return pltpu.make_async_copy(
            new_weight.at[:, :, col], weight_out.at[:, :, col], out_sem.at[3 + 2 * hh + b]
        )

    def finish(hh):
        for dy in range(1, NY):
            for dz in range(NZL):
                ny_copy(hh, dy, dz, -1).wait_recv()
        for pair in range(NY * NZL // 2):
            two = [nwr[hh, 2 * pair + i].astype(F32) for i in range(2)]
            for b in range(2):
                both = jnp.concatenate([t[b * 24 : (b + 1) * 24] for t in two], axis=0)
                new_weight[0, pair * 48 : (pair + 1) * 48, (2 * b + hh) * 128 : (2 * b + hh + 1) * 128] = both.astype(BF)
        for b in range(2):
            weight_copy(hh, b).start()

    @pl.when(x < NX - 1)
    def _():
        sum_over_x(0)
        spread(0)

    sum_over_x(1)
    mine[0].wait()
    mine[1].wait()
    for i in range(len(group)):
        x_copy(i, -1).wait_recv()
        short_copy(i, -1).wait_recv()
    multiply(0)
    spread(1)

    @pl.when(x < NX - 1)
    def _():
        for dx in range(1, NX):

            @pl.when(x + dx < NX)
            def _():
                rv_copy(dx, False).wait_recv()
                totv[...] += rxv[dx - 1].astype(F32)

    zsv[...] = totv[:, theirs, :].astype(BF)
    zv_copy.start()
    multiply(1)
    reduce_x(0)
    zv_copy.wait_recv()
    for hh in range(2):
        both = (totv[hh, ours, :] + zrv[hh].astype(F32)).astype(BF)
        gvl[0, :, hh * HEAD : (hh + 1) * HEAD] = both[:LONG_DEV]
        gvl[1, :, hh * HEAD : (hh + 1) * HEAD] = both[LONG_DEV:]
    my_keys = lanes(core * HALF_K, HALF_K)
    v_copy = remote(gvl.at[other], gv.at[early, my_keys], v_send.at[0], v_recv.at[0], sibling)
    v_copy.start()
    mine.append(pltpu.make_async_copy(gvl.at[core], gv.at[early, my_keys], own_sem.at[12]))
    mine[-1].start()
    for copy in loads[8:]:
        copy.wait()
    update(0)
    reduce_x(1)
    pass_on(0)

    for hh in range(2):
        sibling_copy(hh, True).wait_send()
        for dc in range(NC):
            partner_copy(hh, dc, True).wait_send()
    for dx in range(1, NX):

        @pl.when(x + dx < NX)
        def _():
            for hh in range(2):
                for dc in range(NC):
                    near_copy(hh, dx, dc, True).wait_send()
                    forward(hh, dx, dc, True).wait_send()

        @pl.when(x >= dx)
        def _():
            for hh in range(2):
                for part in range(2):
                    rk_copy(hh, dx, part, True).wait_send()
            rv_copy(dx, True).wait_send()

    for i in range(len(group)):
        x_copy(i, 1).wait_send()
        short_copy(i, 1).wait_send()
        for hh in range(2):
            long_copy(hh, i, 1).wait_send()
    for hh in range(2):
        zk_copy(hh).wait_send()
        for dx in range(1, NX):
            w_copy(hh, dx, 1).wait_send()
    zv_copy.wait_send()
    update(1)
    for copy in updated:
        copy.start()
    finish(0)
    pass_on(1)
    for copy in mine[2:]:
        copy.wait()
    v_copy.wait()
    dq_copy.wait()
    for hh in range(2):
        for dz in range(1, NZ):
            p_copy(hh, dz, 1).wait_send()
        for dz in range(1, NZL):
            nz_copy(hh, dz, 1).wait_send()
    for dy in range(1, NY):
        for dz in range(NZL):
            ny_copy(0, dy, dz, 1).wait_send()
    for copy in updated:
        copy.wait()
    for b in range(2):
        weight_copy(0, b).wait()
    finish(1)
    for dy in range(1, NY):
        for dz in range(NZL):
            ny_copy(1, dy, dz, 1).wait_send()
    for b in range(2):
        weight_copy(1, b).wait()


HBM = pl.BlockSpec(memory_space=pltpu.HBM)
DMA = pltpu.SemaphoreType.DMA


def array(shape, dtype=BF):
    return jax.ShapeDtypeStruct(shape, dtype)


STORE_CUTS = 4


def store_kernel(*refs):
    sources, targets, held, (sem_in, sem_out) = refs[:6], refs[6:12], refs[12:18], refs[18:]
    cut = TOK_DEV // STORE_CUTS
    parts = [(0, pl.ds(i * cut, cut)) for i in range(STORE_CUTS)] + [(i, pl.ds(0, n)) for i, n in ((1, TOK_DEV), (2, 1), (3, 1), (4, 1), (5, 1))]
    loads = [
        pltpu.make_async_copy(sources[i].at[at], held[i].at[at], sem_in.at[n]) for n, (i, at) in enumerate(parts)
    ]
    stores = [
        pltpu.make_async_copy(held[i].at[at], targets[i].at[at], sem_out.at[n]) for n, (i, at) in enumerate(parts)
    ]
    for copy in loads:
        copy.start()
    for load, store in zip(loads, stores):
        load.wait()
        store.start()
    for copy in stores:
        copy.wait()


def on_device(
    layer_inputs, queries, key_states, value_states, output_grad, short_segments, master, first_moment, second_moment
):
    keys = NX * OWN
    tile = (1, 24, KD)
    pairs = lambda *shape: [DMA(shape), DMA(shape)]
    results = [
        array((TOK_DEV, QD)),
        array((TOK_DEV, KD)),
        array(tile, F32),
        array(tile, F32),
        array(tile, F32),
        array((1, 384, KD)),
    ]
    made = pl.pallas_call(
        kernel,
        name="step",
        out_shape=results,
        in_specs=[HBM] * 9,
        out_specs=[HBM] * 6,
        scratch_shapes=[
            pltpu.VMEM((1, SHORT_DEV), jnp.int32),
            *[pltpu.VMEM(tile, F32)] * 6,
            pltpu.VMEM((1, 384, KD), BF),
            pltpu.VMEM((NC, 2, LONG_DEV, 2 * HEAD), BF),
            pltpu.VMEM((SHORT_DEV, QD), BF),
            pltpu.VMEM((SHORT_DEV, QD), BF),
            pltpu.VMEM((SHORT_DEV, KD), BF),
            pltpu.VMEM((SHORT_DEV, KD), BF),
            pltpu.VMEM((TOK_DEV, D), BF),
            pltpu.VMEM((D, TOK_DEV), BF),
            pltpu.VMEM((SHORT_DEV, QD), BF),
            pltpu.VMEM((2, SHORT_DEV, HALF_K), BF),
            pltpu.VMEM((SHORT_DEV, KD), BF),
            pltpu.VMEM((CHUNK, HALF_Q), BF),
            pltpu.VMEM((CHUNK, HALF_Q), BF),
            pltpu.VMEM((2, keys, 2 * HEAD), BF),
            pltpu.VMEM((CHUNK, HALF_Q), BF),
            pltpu.VMEM((keys, WIDE), F32),
            pltpu.VMEM((keys, WIDE), F32),
            pltpu.VMEM((2, keys, GROUPS * HEAD), BF),
            pltpu.VMEM((2, keys, GROUPS * HEAD), BF),
            pltpu.VMEM((keys, HEAD), F32),
            pltpu.VMEM((keys, HEAD), F32),
            pltpu.VMEM((2, keys, HEAD), BF),
            pltpu.VMEM((2, keys, HEAD), BF),
            pltpu.VMEM((2, OWN, HEAD), F32),
            pltpu.VMEM((2, OWN, HEAD), F32),
            pltpu.VMEM((NX - 1, 2, NZH, CHUNK, HEAD), BF),
            pltpu.VMEM((NX - 1, 2, OWN, HEAD), BF),
            pltpu.VMEM((2, CHUNK, HEAD), BF),
            pltpu.VMEM((2, CHUNK, HEAD), BF),
            pltpu.VMEM((2, CHUNK, HEAD), BF),
            pltpu.VMEM((2, CHUNK, HEAD), BF),
            pltpu.VMEM((2, NC, LONG_DEV, HEAD), BF),
            pltpu.VMEM((NC, LONG_DEV, HALF_K), BF),
            pltpu.VMEM((NY, NX * NZH, 96, NC * TOK_DEV), BF),
            pltpu.VMEM((2, NY, NC, TOK_DEV, HALF_K), BF),
            pltpu.VMEM((2, NX, NZH, 96, HALF_K), BF),
            pltpu.VMEM((2, NX - 1, NZH, 96, HALF_K), BF),
            pltpu.VMEM((2, NZH, 96, HALF_K), F32),
            pltpu.VMEM((2, NZ, 48, 128), F32),
            pltpu.VMEM((2, NZ, 48, 128), BF),
            pltpu.VMEM((2, NZ - 1, 48, 128), BF),
            pltpu.VMEM((2, NY * NZL, 48, 128), BF),
            DMA((11,)),
            DMA((8,)),
            DMA((13,)),
            DMA((7,)),
            *pairs(2),
            *pairs(2, 9),
            *pairs(2, 2, 3),
            *pairs(1),
            *pairs(2, 2, 3),
            *pairs(3),
            *pairs(2),
            *pairs(1),
            *pairs(7),
            *pairs(7),
            *pairs(2, 7),
            *pairs(1),
            *pairs(2, 3),
            *pairs(2, 7),
            *pairs(2, 3),
            *pairs(2, 3, 4),
        ],
        compiler_params=pltpu.CompilerParams(
            vmem_limit_bytes=VMEM_LIMIT, collective_id=1, has_side_effects=True
        ),
    )(
        queries, output_grad, key_states, value_states, layer_inputs, short_segments,
        master, first_moment, second_moment,
    )
    return pl.pallas_call(
        store_kernel,
        name="store",
        out_shape=results,
        in_specs=[HBM] * 6,
        out_specs=[HBM] * 6,
        scratch_shapes=[pltpu.VMEM(r.shape, r.dtype) for r in results]
        + [DMA((STORE_CUTS + 5,)), DMA((STORE_CUTS + 5,))],
        compiler_params=pltpu.CompilerParams(vmem_limit_bytes=VMEM_LIMIT),
    )(*made)


def solution(mesh):
    tokens = P(("dp", "ctx"), None)
    shard = P("ctx", "dp", None)
    return jax.shard_map(
        on_device,
        mesh=mesh,
        in_specs=(tokens,) * 6 + (shard,) * 3,
        out_specs=(tokens, tokens, shard, shard, shard, P("ctx", None, None)),
        check_vma=False,
    )
```

```python
import functools

import jax
import jax.numpy as jnp
from jax import lax
from jax.experimental import pallas as pl
from jax.experimental.pallas import tpu as pltpu
from jax.sharding import PartitionSpec as P

D = 6144
HEAD = 128
GROUPS = 12
HK = 4
SHORT_FIRST = 4
LONG_DEV = 64
SHORT_DEV = 64
TOK_DEV = 128
CHUNK = 128
KD = 512
QD = 6144
HALF_Q = 3072
HALF_K = 256
NY, NZL, NX, NZH, NC = 4, 4, 4, 2, 2
NZ = NZL * NZH

LEARN_RATE = 0.001
BETA_ONE = 0.9
BETA_TWO = 0.95
ADAM_EPS = 1e-08
DECAY = 0.1
STEP_COUNT = 10

MESH = pl.DeviceIdType.MESH
FACTOR = HEAD**-0.5
EXP_FACTOR = FACTOR * 1.4426950408889634
NEG = -1e30
BF = jnp.bfloat16
VMEM_LIMIT = 58 << 20
F32 = jnp.float32
NT = (((1,), (1,)), ((), ()))
TN = (((0,), (0,)), ((), ()))


def dot(a, b, dims=(((1,), (0,)), ((), ()))):
    return lax.dot_general(a, b, dims, preferred_element_type=F32)


def place():
    d = lax.axis_index("dp")
    c = lax.axis_index("ctx")
    return d // NZL, d % NZL, c // (NZH * NC), (c // NC) % NZH, c % NC


def device(y, z_lo, x, z_hi, core):
    return (y * NZL + z_lo, (x * NZH + z_hi) * NC + core)


def remote(src, dst, send, recv, peer):
    return pltpu.make_async_remote_copy(
        src_ref=src, dst_ref=dst, send_sem=send, recv_sem=recv, device_id=peer, device_id_type=MESH
    )


def lanes(start, size):
    return pl.ds(pl.multiple_of(start, 128), size)


def rows(start, size, unit):
    return pl.ds(pl.multiple_of(start, unit), size)


def short_mask(seg_ref):
    segment = seg_ref[...]
    square = jnp.broadcast_to(segment, (SHORT_DEV, SHORT_DEV))
    diag = lax.broadcasted_iota(jnp.int32, (SHORT_DEV, SHORT_DEV), 0) == lax.broadcasted_iota(
        jnp.int32, (SHORT_DEV, SHORT_DEV), 1
    )
    column = jnp.sum(jnp.where(diag, square.astype(F32), 0.0), axis=1, keepdims=True)
    row = jnp.concatenate([segment.astype(F32)] * 2, axis=1)
    key = lax.broadcasted_iota(jnp.int32, (SHORT_DEV, 128), 0)
    token = lax.broadcasted_iota(jnp.int32, (SHORT_DEV, 128), 1) % SHORT_DEV
    pair = jnp.where((column == row) & (key <= token), 0.0, NEG)
    return jnp.concatenate([pair] * (GROUPS // 2), axis=1)


def short_head(kh, bias, q_ref, g_ref, k_ref, v_ref, dq_ref, dk_ref, dv_ref):
    width = GROUPS * HEAD
    q = q_ref[:, lanes(kh * width, width)]
    g = g_ref[:, lanes(kh * width, width)]
    k = k_ref[:, lanes(kh * HEAD, HEAD)]
    v = v_ref[:, lanes(kh * HEAD, HEAD)]
    q = jnp.concatenate([q[:, i * HEAD : (i + 1) * HEAD] for i in range(GROUPS)], axis=0)
    g = jnp.concatenate([g[:, i * HEAD : (i + 1) * HEAD] for i in range(GROUPS)], axis=0)
    scores = dot(k, q, NT) + bias
    top = jnp.max(scores, axis=0, keepdims=True)
    raised = jnp.exp2((scores - top) * EXP_FACTOR)
    probs = raised * (1.0 / jnp.sum(raised, axis=0, keepdims=True))
    probs_low = probs.astype(BF)
    grad_probs = dot(v, g, NT)
    delta = jnp.sum(probs_low.astype(F32) * grad_probs, axis=0, keepdims=True)
    grad_scores = (probs * FACTOR * (grad_probs - delta)).astype(BF)
    dv_ref[:, lanes(kh * HEAD, HEAD)] = dot(probs_low, g).astype(BF)
    dk_ref[kh % 2, :, lanes(kh // 2 * HEAD, HEAD)] = dot(grad_scores, q).astype(BF)
    dq = dot(grad_scores, k, TN).astype(BF)
    dq_ref[:, lanes(kh * width, width)] = jnp.concatenate(
        [dq[i * SHORT_DEV : (i + 1) * SHORT_DEV] for i in range(GROUPS)], axis=1
    )


HEADS = 6
WIDE = HEADS * CHUNK
STEPS = GROUPS // HEADS
OWN = NZH * CHUNK


def long_head(keys, hh, z_hi, q, g, kv, scores, grads, probs, low, acc_k):
    chunks = keys // CHUNK
    acc_k[0:keys, :] = jnp.zeros((keys, HEAD), F32)

    @pl.loop(0, STEPS)
    def _(p):
        col = lanes((hh * STEPS + p) * WIDE, WIDE)
        wide = lanes(p * WIDE, WIDE)
        qw, gw = q[:, col], g[:, col]
        qs = jnp.concatenate([qw[:, i * HEAD : (i + 1) * HEAD] for i in range(HEADS)], axis=0)
        gs = jnp.concatenate([gw[:, i * HEAD : (i + 1) * HEAD] for i in range(HEADS)], axis=0)
        top = None
        for n in range(chunks):
            at = slice(n * CHUNK, (n + 1) * CHUNK)
            s = dot(kv[hh, at, :HEAD], qs, NT)
            if n >= chunks - 2:
                key = lax.broadcasted_iota(jnp.int32, (CHUNK, WIDE), 0) + (n - chunks + 2) * CHUNK
                token = lax.broadcasted_iota(jnp.int32, (CHUNK, WIDE), 1) % CHUNK + z_hi * CHUNK
                s = jnp.where(key <= token, s, NEG)
            scores[at, :] = s
            m = jnp.max(s, axis=0, keepdims=True)
            top = m if top is None else jnp.maximum(top, m)
        total = delta = None
        for n in range(chunks):
            at = slice(n * CHUNK, (n + 1) * CHUNK)
            e = jnp.exp2((scores[at, :] - top) * EXP_FACTOR)
            scores[at, :] = e
            dp = dot(kv[hh, at, HEAD:], gs, NT)
            grads[at, :] = dp
            part = jnp.sum(e, axis=0, keepdims=True)
            total = part if total is None else total + part
            part = jnp.sum(e * dp, axis=0, keepdims=True)
            delta = part if delta is None else delta + part
        scale = 1.0 / total
        delta = delta * scale
        for n in range(chunks):
            at = slice(n * CHUNK, (n + 1) * CHUNK)
            pr = scores[at, :] * scale
            probs[hh, at, wide] = pr.astype(BF)
            ds = (pr * ((grads[at, :] - delta) * FACTOR)).astype(BF)
            low[hh, at, wide] = ds
            acc_k[at, :] += dot(ds, qs)


def long_rest(keys, hh, g, kv, dq, probs, low, acc_v):
    width = GROUPS * HEAD
    col = lanes(hh * width, width)
    gr = g[:, col]
    gs = jnp.concatenate([gr[:, i * HEAD : (i + 1) * HEAD] for i in range(GROUPS)], axis=0)
    for n in range(keys // CHUNK):
        at = slice(n * CHUNK, (n + 1) * CHUNK)
        acc_v[at, :] = dot(probs[hh, at, :], gs)
    kt = kv[hh, 0:keys, :HEAD].T
    for p in range(STEPS):
        out = dot(kt, low[hh, 0:keys, p * WIDE : (p + 1) * WIDE]).astype(BF).T
        dq[:, lanes(hh * width + p * WIDE, WIDE)] = jnp.concatenate(
            [out[i * CHUNK : (i + 1) * CHUNK] for i in range(HEADS)], axis=1
        )


def fold(a):
    return jnp.concatenate([a[:, :128], a[:, 128:]], axis=0)


def kernel(
    q_hbm, g_hbm, k_hbm, v_hbm, x_hbm, seg_hbm, master_hbm, first_hbm, second_hbm,
    gq, gv, new_master, new_first, new_second, new_weight,
    seg_ref, master, first, second, kvs,
    qs, gs, ks, vs, xs, xt, sdq, sgk, sgv,
    qb, gb, kvb, dq, scores, grads, probs, low, acc_k, acc_v, dks, dvs, totk, totv,
    rxk, rxv, zsk, zrk, zsv, zrv, gkl, gvl, xg, gk, wp, wr, wsum, zf, zp, zq, nwr,
    load_sem, key_sem, own_sem, q_send, q_recv, kv_send, kv_recv, fw_send, fw_recv, dq_send, dq_recv,
    rk_send, rk_recv, rv_send, rv_recv, zk_send, zk_recv, zv_send, zv_recv, x_send, x_recv,
    s_send, s_recv, l_send, l_recv, v_send, v_recv, w_send, w_recv, p_send, p_recv,
    nz_send, nz_recv, ny_send, ny_recv,
):
    y, z_lo, x, z_hi, core = place()
    c = lax.axis_index("ctx")
    z = z_hi * NZL + z_lo
    other = 1 - core
    sibling = device(y, z_lo, x, z_hi, other)
    partner = device(y, z_lo, x, 1 - z_hi, core)
    early, late = pl.ds(0, LONG_DEV), pl.ds(LONG_DEV, SHORT_DEV)
    my_tokens = lanes(core * TOK_DEV, TOK_DEV)

    own_rows = rows(c * LONG_DEV, LONG_DEV, 64)
    pair_rows = rows(core * LONG_DEV, LONG_DEV, 64)
    keyed = [
        pltpu.make_async_copy(
            src.at[early, pl.ds((2 * to + hh) * HEAD, HEAD)],
            kvs.at[to, hh, :, pl.ds(n * HEAD, HEAD)],
            key_sem.at[4 * to + 2 * hh + n],
        )
        for hh in range(2)
        for to in range(NC)
        for n, src in enumerate((k_hbm, v_hbm))
    ]
    loads = [
        pltpu.make_async_copy(hbm, vmem, load_sem.at[i])
        for i, (hbm, vmem) in enumerate(
            (
                (x_hbm, xs),
                (q_hbm.at[late, :], qs),
                (g_hbm.at[late, :], gs),
                (k_hbm.at[late, :], ks),
                (v_hbm.at[late, :], vs),
                (seg_hbm, seg_ref),
                (q_hbm.at[early, lanes(core * HALF_Q, HALF_Q)], qb.at[pair_rows, :]),
                (g_hbm.at[early, lanes(core * HALF_Q, HALF_Q)], gb.at[pair_rows, :]),
                (master_hbm, master),
                (first_hbm, first),
                (second_hbm, second),
            )
        )
    ]
    for copy in keyed + loads:
        copy.start()

    def x_peer(dx, sign):
        return (x + sign * dx + NX) % NX

    def z_peer(dz, sign):
        return (z + sign * dz + NZ) % NZ

    def z_device(pz):
        return device(y, pz % NZL, x, pz // NZL, core)

    group = [(dy, dc) for dy in range(NY) for dc in range(NC) if (dy, dc) != (0, 0)]

    def group_peer(i, sign):
        dy, dc = group[i]
        return (y + sign * dy + NY) % NY, (core + dc) % NC

    peers = [device(y, z_lo, x, 1 - z_hi, other)]
    peers += [z_device(z_peer(dz, 1)) for dz in (4, 3, 5, 2, 6, 1, 7)]
    peers += [device(y, z_lo, x_peer(dx, 1), z_hi, (core + dc) % NC) for dx in (2, 1, 3) for dc in (1, 0)]
    for i in range(len(group)):
        py, pc = group_peer(i, 1)
        peers.append(device(py, z_lo, x, z_hi, pc))
    barrier = pltpu.get_barrier_semaphore()
    for peer in peers:
        pl.semaphore_signal(barrier, inc=1, device_id=peer, device_id_type=MESH)

    for copy in keyed:
        copy.wait()
    own_kv = pltpu.make_async_copy(kvs.at[core], kvb.at[:, own_rows, :], own_sem.at[4])
    own_kv.start()
    pl.semaphore_wait(barrier, len(peers))

    def kv_copy(hh, px, pz, pc, slot, sending):
        where = own_rows if sending else rows(((px * NZH + pz) * NC + pc) * LONG_DEV, LONG_DEV, 64)
        return remote(
            kvs.at[pc if sending else core, hh], kvb.at[hh, where, :], kv_send.at[hh, slot], kv_recv.at[hh, slot],
            device(y, z_lo, px, pz, pc),
        )

    def partner_copy(hh, dc, sending):
        return kv_copy(hh, x, 1 - z_hi, (core + dc) % NC, dc, sending)

    def sibling_copy(hh, sending):
        return kv_copy(hh, x, z_hi, other, 2, sending)

    def near_copy(hh, dx, dc, sending):
        return kv_copy(hh, x + dx if sending else x - dx, z_hi, (core + dc) % NC, 1 + 2 * dx + dc, sending)

    for hh in range(2):
        for dc in range(NC):
            partner_copy(hh, dc, True).start()
    for hh in range(2):
        for dx in range(1, NX):

            @pl.when(x + dx < NX)
            def _():
                for dc in range(NC):
                    near_copy(hh, dx, dc, True).start()

        sibling_copy(hh, True).start()

    swaps = [
        remote(
            src.at[early, lanes(other * HALF_Q, HALF_Q)], dst.at[pair_rows, :], q_send.at[n], q_recv.at[n], sibling
        )
        for n, (src, dst) in enumerate(((q_hbm, qb), (g_hbm, gb)))
    ]
    for copy in swaps:
        copy.start()

    loads[0].wait()

    @pl.loop(0, D // 1024)
    def _(i):
        for j in range(8):
            at = i * 1024 + j * 128
            xt[rows(at, 128, 128), :] = xs[:, lanes(at, 128)].T

    def x_copy(i, sign):
        py, pc = group_peer(i, sign)
        sy, sc = (y, core) if sign > 0 else (py, pc)
        return remote(
            xt.reshape(NX * NZH, NC, NY, 96, TOK_DEV).at[:, pc, py],
            xg.at[sy, :, :, lanes(sc * TOK_DEV, TOK_DEV)],
            x_send.at[i], x_recv.at[i], device(py, z_lo, x, z_hi, pc),
        )

    for i in range(len(group)):
        x_copy(i, 1).start()
    mine = [
        pltpu.make_async_copy(
            xt.reshape(NX * NZH, NC, NY, 96, TOK_DEV).at[:, core, y], xg.at[y, :, :, my_tokens], own_sem.at[5]
        )
    ]
    mine[0].start()

    for copy in loads[1:6]:
        copy.wait()
    bias = short_mask(seg_ref)

    def heads(start, stop):
        @pl.loop(start, stop)
        def _(kh):
            short_head(kh, bias, qs, gs, ks, vs, sdq, sgk, sgv)

    heads(0, SHORT_FIRST)

    def forward(hh, dx, dc, sending):
        px = x + dx if sending else x - dx
        chip = (x if sending else px) * NZH + 1 - z_hi
        where = rows((chip * NC + (core + dc) % NC) * LONG_DEV, LONG_DEV, 64)
        return remote(
            kvb.at[hh, where, :], kvb.at[hh, where, :], fw_send.at[hh, dc, dx - 1], fw_recv.at[hh, dc, dx - 1],
            device(y, z_lo, px, z_hi, core),
        )

    for hh in range(2):
        for dc in range(NC):
            partner_copy(hh, dc, False).wait_recv()
            for dx in range(1, NX):

                @pl.when(x + dx < NX)
                def _():
                    forward(hh, dx, dc, True).start()

    heads(SHORT_FIRST, HK)

    def short_copy(i, sign):
        py, pc = group_peer(i, sign)
        sy, sc = (y, core) if sign > 0 else (py, pc)
        return remote(
            sgk, gk.at[:, sy, sc, late, :], s_send.at[i], s_recv.at[i], device(py, z_lo, x, z_hi, pc)
        )

    for i in range(len(group)):
        short_copy(i, 1).start()
    mine += [
        pltpu.make_async_copy(sgk, gk.at[:, y, core, late, :], own_sem.at[6]),
        pltpu.make_async_copy(sdq, gq.at[late, :], own_sem.at[7]),
        pltpu.make_async_copy(sgv, gv.at[late, :], own_sem.at[8]),
    ]
    for copy in mine[1:]:
        copy.start()

    for copy in loads[6:8]:
        copy.wait()
    own_kv.wait()
    for copy in swaps:
        copy.wait()

    def rk_copy(hh, dx, part, sending):
        px = x - dx if sending else x + dx
        chunk = (px if sending else x) * NZH + (1 - z_hi if part == 0 else z_hi)
        return remote(
            dks.at[hh, rows(chunk * CHUNK, CHUNK, 128), :], rxk.at[dx - 1, hh, part],
            rk_send.at[hh, part, dx - 1], rk_recv.at[hh, part, dx - 1], device(y, z_lo, px, z_hi, core),
        )

    def rv_copy(dx, sending):
        px = x - dx if sending else x + dx
        at = rows((px if sending else x) * OWN, OWN, 256)
        return remote(
            dvs.at[:, at, :], rxv.at[dx - 1], rv_send.at[dx - 1], rv_recv.at[dx - 1],
            device(y, z_lo, px, z_hi, core),
        )

    def zk_copy(hh):
        return remote(zsk.at[hh], zrk.at[hh], zk_send.at[hh], zk_recv.at[hh], partner)

    zv_copy = remote(zsv, zrv, zv_send.at[0], zv_recv.at[0], partner)
    ours = rows(z_hi * CHUNK, CHUNK, 128)
    theirs = rows((1 - z_hi) * CHUNK, CHUNK, 128)

    @pl.loop(0, 2)
    def _(hh):
        sibling_copy(hh, False).wait_recv()
        for n in range(NX):

            @pl.when(x == n)
            def _():
                keys, below = (n + 1) * OWN, n * OWN
                for dx in range(1, n + 1):
                    for dc in range(NC):
                        near_copy(hh, dx, dc, False).wait_recv()
                        forward(hh, dx, dc, False).wait_recv()
                long_head(keys, hh, z_hi, qb, gb, kvb, scores, grads, probs, low, acc_k)
                if below:
                    dks[hh, 0:below, :] = acc_k[0:below, :].astype(BF)
                totk[hh] = acc_k[below:keys, :]

        for part in range(2):
            for dx in range(1, NX):

                @pl.when(x >= dx)
                def _():
                    rk_copy(hh, dx, part, True).start()

        @pl.when(x == NX - 1)
        def _():
            zsk[hh] = totk[hh, theirs, :].astype(BF)
            zk_copy(hh).start()

    def sum_over_x(hh):
        for part in range(2):
            at = theirs if part == 0 else ours
            for dx in range(1, NX):

                @pl.when(x + dx < NX)
                def _():
                    rk_copy(hh, dx, part, False).wait_recv()
                    totk[hh, at, :] += rxk[dx - 1, hh, part].astype(F32)

            if part == 0:

                @pl.when(x < NX - 1)
                def _():
                    zsk[hh] = totk[hh, theirs, :].astype(BF)
                    zk_copy(hh).start()

    def long_copy(hh, i, sign):
        py, pc = group_peer(i, sign)
        sy, sc = (y, core) if sign > 0 else (py, pc)
        return remote(
            gkl.at[hh], gk.at[hh, sy, :, early, lanes(sc * HEAD, HEAD)], l_send.at[hh, i], l_recv.at[hh, i],
            device(py, z_lo, x, z_hi, pc),
        )

    def own_copy(hh):
        return pltpu.make_async_copy(
            gkl.at[hh], gk.at[hh, y, :, early, lanes(core * HEAD, HEAD)], own_sem.at[10 + hh]
        )

    def spread(hh):
        zk_copy(hh).wait_recv()
        both = (totk[hh, ours, :] + zrk[hh].astype(F32)).astype(BF)
        gkl[hh, 0] = both[:LONG_DEV]
        gkl[hh, 1] = both[LONG_DEV:]
        for i in range(len(group)):
            long_copy(hh, i, 1).start()
        own_copy(hh).start()

    @pl.when(x == NX - 1)
    def _():
        spread(0)

    @pl.loop(0, 2)
    def _(hh):
        for n in range(NX):

            @pl.when(x == n)
            def _():
                keys, below = (n + 1) * OWN, n * OWN
                long_rest(keys, hh, gb, kvb, dq, probs, low, acc_v)
                if below:
                    dvs[hh, 0:below, :] = acc_v[0:below, :].astype(BF)
                totv[hh] = acc_v[below:keys, :]

    for dx in range(1, NX):

        @pl.when(x >= dx)
        def _():
            rv_copy(dx, True).start()

    dq_copy = remote(
        dq.at[rows(other * LONG_DEV, LONG_DEV, 64), :], gq.at[early, lanes(core * HALF_Q, HALF_Q)],
        dq_send.at[0], dq_recv.at[0], sibling,
    )
    dq_copy.start()
    mine.append(
        pltpu.make_async_copy(dq.at[pair_rows, :], gq.at[early, lanes(core * HALF_Q, HALF_Q)], own_sem.at[9])
    )
    mine[-1].start()

    def w_copy(hh, dx, sign):
        px = x_peer(dx, sign)
        return remote(
            wp.at[hh, px], wr.at[hh, dx - 1], w_send.at[hh, dx - 1], w_recv.at[hh, dx - 1],
            device(y, z_lo, px, z_hi, core),
        )

    def product(hh, px):
        result = None
        for sy in range(NY):
            left = xg[sy, rows(NZH * px, NZH, 1)].reshape(NZH * 96, NC * TOK_DEV)
            term = dot(left, gk[hh, sy].reshape(NC * TOK_DEV, HALF_K))
            result = term if result is None else result + term
        return result.reshape(NZH, 96, HALF_K)

    def multiply(hh):
        own_copy(hh).wait()
        for i in range(len(group)):
            long_copy(hh, i, -1).wait_recv()
        for dx in (2, 1, 3):
            px = x_peer(dx, 1)
            wp[hh, px] = product(hh, px).astype(BF)
            w_copy(hh, dx, 1).start()
        wsum[hh] = product(hh, x)

    def p_copy(hh, dz, sign):
        pz = z_peer(dz, sign)
        return remote(
            zp.at[hh, pz], zq.at[hh, dz - 1], p_send.at[hh, dz - 1], p_recv.at[hh, dz - 1], z_device(pz)
        )

    def reduce_x(hh):
        for dx in (1, 3, 2):
            w_copy(hh, dx, -1).wait_recv()
            wsum[hh] += wr[hh, dx - 1].astype(F32)
        for pz in range(NZ):
            zf[hh, pz] = fold(wsum[hh, pz // NZL, (pz % NZL) * 24 : (pz % NZL + 1) * 24, :])
        zp[hh] = zf[hh].astype(BF)
        for dz in (4, 3, 5, 2, 6, 1, 7):
            p_copy(hh, dz, 1).start()

    d = lax.axis_index("dp")

    def nz_copy(hh, dz, sign):
        pz = (z_lo + sign * dz + NZL) % NZL
        slot = d if sign > 0 else y * NZL + pz
        return remote(
            nwr.at[hh, slot], nwr.at[hh, slot], nz_send.at[hh, dz - 1], nz_recv.at[hh, dz - 1],
            device(y, pz, x, z_hi, core),
        )

    def ny_copy(hh, dy, dz, sign):
        py = (y + sign * dy + NY) % NY
        slot = (y if sign > 0 else py) * NZL + (z_lo - dz + NZL) % NZL
        return remote(
            nwr.at[hh, slot], nwr.at[hh, slot], ny_send.at[hh, dy - 1, dz], ny_recv.at[hh, dy - 1, dz],
            device(py, z_lo, x, z_hi, core),
        )

    def update(hh):
        share = zf[hh, z]
        for dz in range(1, NZ):
            p_copy(hh, dz, -1).wait_recv()
            share = share + zq[hh, dz - 1].astype(F32)
        share = share * (1.0 / (TOK_DEV * NY * NZ * NX * NC))
        fresh = []
        for b in range(2):
            col = slice((2 * b + hh) * 128, (2 * b + hh + 1) * 128)
            grad = share[b * 24 : (b + 1) * 24]
            moment = BETA_ONE * first[0, :, col] + (1.0 - BETA_ONE) * grad
            square = BETA_TWO * second[0, :, col] + (1.0 - BETA_TWO) * grad * grad
            first_hat = moment / (1.0 - BETA_ONE**STEP_COUNT)
            second_hat = square / (1.0 - BETA_TWO**STEP_COUNT)
            old = master[0, :, col]
            new = old - LEARN_RATE * (first_hat / (jnp.sqrt(second_hat) + ADAM_EPS) + DECAY * old)
            new_first[0, :, col] = moment
            new_second[0, :, col] = square
            new_master[0, :, col] = new
            fresh.append(new)
        nwr[hh, d] = jnp.concatenate(fresh, axis=0).astype(BF)
        for dz in range(1, NZL):
            nz_copy(hh, dz, 1).start()
        for dy in range(1, NY):
            ny_copy(hh, dy, 0, 1).start()

    def pass_on(hh):
        for dz in (1, 3, 2):
            nz_copy(hh, dz, -1).wait_recv()
            for dy in (2, 1, 3):
                ny_copy(hh, dy, dz, 1).start()

    def finish(hh):
        for dy in range(1, NY):
            for dz in range(NZL):
                ny_copy(hh, dy, dz, -1).wait_recv()
        for pair in range(NY * NZL // 2):
            two = [nwr[hh, 2 * pair + i].astype(F32) for i in range(2)]
            for b in range(2):
                both = jnp.concatenate([t[b * 24 : (b + 1) * 24] for t in two], axis=0)
                new_weight[0, pair * 48 : (pair + 1) * 48, (2 * b + hh) * 128 : (2 * b + hh + 1) * 128] = both.astype(BF)

    @pl.when(x < NX - 1)
    def _():
        sum_over_x(0)
        spread(0)

    sum_over_x(1)
    mine[0].wait()
    mine[1].wait()
    for i in range(len(group)):
        x_copy(i, -1).wait_recv()
        short_copy(i, -1).wait_recv()
    multiply(0)
    spread(1)

    @pl.when(x < NX - 1)
    def _():
        for dx in range(1, NX):

            @pl.when(x + dx < NX)
            def _():
                rv_copy(dx, False).wait_recv()
                totv[...] += rxv[dx - 1].astype(F32)

    zsv[...] = totv[:, theirs, :].astype(BF)
    zv_copy.start()
    multiply(1)
    reduce_x(0)
    zv_copy.wait_recv()
    for hh in range(2):
        both = (totv[hh, ours, :] + zrv[hh].astype(F32)).astype(BF)
        gvl[0, :, hh * HEAD : (hh + 1) * HEAD] = both[:LONG_DEV]
        gvl[1, :, hh * HEAD : (hh + 1) * HEAD] = both[LONG_DEV:]
    my_keys = lanes(core * HALF_K, HALF_K)
    v_copy = remote(gvl.at[other], gv.at[early, my_keys], v_send.at[0], v_recv.at[0], sibling)
    v_copy.start()
    mine.append(pltpu.make_async_copy(gvl.at[core], gv.at[early, my_keys], own_sem.at[12]))
    mine[-1].start()
    for copy in loads[8:]:
        copy.wait()
    update(0)
    reduce_x(1)
    pass_on(0)

    for hh in range(2):
        sibling_copy(hh, True).wait_send()
        for dc in range(NC):
            partner_copy(hh, dc, True).wait_send()
    for dx in range(1, NX):

        @pl.when(x + dx < NX)
        def _():
            for hh in range(2):
                for dc in range(NC):
                    near_copy(hh, dx, dc, True).wait_send()
                    forward(hh, dx, dc, True).wait_send()

        @pl.when(x >= dx)
        def _():
            for hh in range(2):
                for part in range(2):
                    rk_copy(hh, dx, part, True).wait_send()
            rv_copy(dx, True).wait_send()

    for i in range(len(group)):
        x_copy(i, 1).wait_send()
        short_copy(i, 1).wait_send()
        for hh in range(2):
            long_copy(hh, i, 1).wait_send()
    for hh in range(2):
        zk_copy(hh).wait_send()
        for dx in range(1, NX):
            w_copy(hh, dx, 1).wait_send()
    zv_copy.wait_send()
    update(1)
    finish(0)
    pass_on(1)
    for copy in mine[2:]:
        copy.wait()
    v_copy.wait()
    dq_copy.wait()
    for hh in range(2):
        for dz in range(1, NZ):
            p_copy(hh, dz, 1).wait_send()
        for dz in range(1, NZL):
            nz_copy(hh, dz, 1).wait_send()
    for dy in range(1, NY):
        for dz in range(NZL):
            ny_copy(0, dy, dz, 1).wait_send()
    finish(1)
    for dy in range(1, NY):
        for dz in range(NZL):
            ny_copy(1, dy, dz, 1).wait_send()


HBM = pl.BlockSpec(memory_space=pltpu.HBM)
VMEM = pl.BlockSpec(memory_space=pltpu.VMEM)
DMA = pltpu.SemaphoreType.DMA


def array(shape, dtype=BF):
    return jax.ShapeDtypeStruct(shape, dtype)


def store_kernel(*refs):
    copies = [pltpu.make_async_copy(refs[i], refs[6 + i], refs[12].at[i]) for i in range(6)]
    for copy in copies:
        copy.start()
    for copy in copies:
        copy.wait()


def on_device(
    layer_inputs, queries, key_states, value_states, output_grad, short_segments, master, first_moment, second_moment
):
    keys = NX * OWN
    tile = (1, 24, KD)
    pairs = lambda *shape: [DMA(shape), DMA(shape)]
    results = [
        array((TOK_DEV, QD)),
        array((TOK_DEV, KD)),
        array(tile, F32),
        array(tile, F32),
        array(tile, F32),
        array((1, 384, KD)),
    ]
    made = pl.pallas_call(
        kernel,
        name="step",
        out_shape=[pltpu.VMEM(r.shape, r.dtype) for r in results],
        in_specs=[HBM] * 9,
        out_specs=[VMEM] * 6,
        scratch_shapes=[
            pltpu.VMEM((1, SHORT_DEV), jnp.int32),
            *[pltpu.VMEM(tile, F32)] * 3,
            pltpu.VMEM((NC, 2, LONG_DEV, 2 * HEAD), BF),
            pltpu.VMEM((SHORT_DEV, QD), BF),
            pltpu.VMEM((SHORT_DEV, QD), BF),
            pltpu.VMEM((SHORT_DEV, KD), BF),
            pltpu.VMEM((SHORT_DEV, KD), BF),
            pltpu.VMEM((TOK_DEV, D), BF),
            pltpu.VMEM((D, TOK_DEV), BF),
            pltpu.VMEM((SHORT_DEV, QD), BF),
            pltpu.VMEM((2, SHORT_DEV, HALF_K), BF),
            pltpu.VMEM((SHORT_DEV, KD), BF),
            pltpu.VMEM((CHUNK, HALF_Q), BF),
            pltpu.VMEM((CHUNK, HALF_Q), BF),
            pltpu.VMEM((2, keys, 2 * HEAD), BF),
            pltpu.VMEM((CHUNK, HALF_Q), BF),
            pltpu.VMEM((keys, WIDE), F32),
            pltpu.VMEM((keys, WIDE), F32),
            pltpu.VMEM((2, keys, GROUPS * HEAD), BF),
            pltpu.VMEM((2, keys, GROUPS * HEAD), BF),
            pltpu.VMEM((keys, HEAD), F32),
            pltpu.VMEM((keys, HEAD), F32),
            pltpu.VMEM((2, keys, HEAD), BF),
            pltpu.VMEM((2, keys, HEAD), BF),
            pltpu.VMEM((2, OWN, HEAD), F32),
            pltpu.VMEM((2, OWN, HEAD), F32),
            pltpu.VMEM((NX - 1, 2, NZH, CHUNK, HEAD), BF),
            pltpu.VMEM((NX - 1, 2, OWN, HEAD), BF),
            pltpu.VMEM((2, CHUNK, HEAD), BF),
            pltpu.VMEM((2, CHUNK, HEAD), BF),
            pltpu.VMEM((2, CHUNK, HEAD), BF),
            pltpu.VMEM((2, CHUNK, HEAD), BF),
            pltpu.VMEM((2, NC, LONG_DEV, HEAD), BF),
            pltpu.VMEM((NC, LONG_DEV, HALF_K), BF),
            pltpu.VMEM((NY, NX * NZH, 96, NC * TOK_DEV), BF),
            pltpu.VMEM((2, NY, NC, TOK_DEV, HALF_K), BF),
            pltpu.VMEM((2, NX, NZH, 96, HALF_K), BF),
            pltpu.VMEM((2, NX - 1, NZH, 96, HALF_K), BF),
            pltpu.VMEM((2, NZH, 96, HALF_K), F32),
            pltpu.VMEM((2, NZ, 48, 128), F32),
            pltpu.VMEM((2, NZ, 48, 128), BF),
            pltpu.VMEM((2, NZ - 1, 48, 128), BF),
            pltpu.VMEM((2, NY * NZL, 48, 128), BF),
            DMA((11,)),
            DMA((8,)),
            DMA((13,)),
            *pairs(2),
            *pairs(2, 9),
            *pairs(2, 2, 3),
            *pairs(1),
            *pairs(2, 2, 3),
            *pairs(3),
            *pairs(2),
            *pairs(1),
            *pairs(7),
            *pairs(7),
            *pairs(2, 7),
            *pairs(1),
            *pairs(2, 3),
            *pairs(2, 7),
            *pairs(2, 3),
            *pairs(2, 3, 4),
        ],
        compiler_params=pltpu.CompilerParams(
            vmem_limit_bytes=VMEM_LIMIT, collective_id=1, has_side_effects=True
        ),
    )(
        queries, output_grad, key_states, value_states, layer_inputs, short_segments,
        master, first_moment, second_moment,
    )
    return pl.pallas_call(
        store_kernel,
        name="store",
        out_shape=results,
        in_specs=[VMEM] * 6,
        out_specs=[HBM] * 6,
        scratch_shapes=[DMA((6,))],
        compiler_params=pltpu.CompilerParams(vmem_limit_bytes=8 << 20),
    )(*made)


def solution(mesh):
    tokens = P(("dp", "ctx"), None)
    shard = P("ctx", "dp", None)
    return jax.shard_map(
        on_device,
        mesh=mesh,
        in_specs=(tokens,) * 6 + (shard,) * 3,
        out_specs=(tokens, tokens, shard, shard, shard, P("ctx", None, None)),
        check_vma=False,
    )
```

```python
import functools

import jax
import jax.numpy as jnp
from jax import lax
from jax.experimental import pallas as pl
from jax.experimental.pallas import tpu as pltpu
from jax.sharding import PartitionSpec as P

D = 6144
HEAD = 128
GROUPS = 12
HK = 4
SHORT_FIRST = 4
LONG_DEV = 64
SHORT_DEV = 64
TOK_DEV = 128
CHUNK = 128
KD = 512
QD = 6144
HALF_Q = 3072
HALF_K = 256
NY, NZL, NX, NZH, NC = 4, 4, 4, 2, 2
NZ = NZL * NZH

LEARN_RATE = 0.001
BETA_ONE = 0.9
BETA_TWO = 0.95
ADAM_EPS = 1e-08
DECAY = 0.1
STEP_COUNT = 10

MESH = pl.DeviceIdType.MESH
FACTOR = HEAD**-0.5
EXP_FACTOR = FACTOR * 1.4426950408889634
NEG = -1e30
BF = jnp.bfloat16
VMEM_LIMIT = 58 << 20
F32 = jnp.float32
NT = (((1,), (1,)), ((), ()))
TN = (((0,), (0,)), ((), ()))


def dot(a, b, dims=(((1,), (0,)), ((), ()))):
    return lax.dot_general(a, b, dims, preferred_element_type=F32)


def place():
    d = lax.axis_index("dp")
    c = lax.axis_index("ctx")
    return d // NZL, d % NZL, c // (NZH * NC), (c // NC) % NZH, c % NC


def device(y, z_lo, x, z_hi, core):
    return (y * NZL + z_lo, (x * NZH + z_hi) * NC + core)


def remote(src, dst, send, recv, peer):
    return pltpu.make_async_remote_copy(
        src_ref=src, dst_ref=dst, send_sem=send, recv_sem=recv, device_id=peer, device_id_type=MESH
    )


def lanes(start, size):
    return pl.ds(pl.multiple_of(start, 128), size)


def rows(start, size, unit):
    return pl.ds(pl.multiple_of(start, unit), size)


def short_mask(seg_ref):
    segment = seg_ref[...]
    square = jnp.broadcast_to(segment, (SHORT_DEV, SHORT_DEV))
    diag = lax.broadcasted_iota(jnp.int32, (SHORT_DEV, SHORT_DEV), 0) == lax.broadcasted_iota(
        jnp.int32, (SHORT_DEV, SHORT_DEV), 1
    )
    column = jnp.sum(jnp.where(diag, square.astype(F32), 0.0), axis=1, keepdims=True)
    row = jnp.concatenate([segment.astype(F32)] * 2, axis=1)
    key = lax.broadcasted_iota(jnp.int32, (SHORT_DEV, 128), 0)
    token = lax.broadcasted_iota(jnp.int32, (SHORT_DEV, 128), 1) % SHORT_DEV
    pair = jnp.where((column == row) & (key <= token), 0.0, NEG)
    return jnp.concatenate([pair] * (GROUPS // 2), axis=1)


def short_head(kh, bias, q_ref, g_ref, k_ref, v_ref, dq_ref, dk_ref, dv_ref):
    width = GROUPS * HEAD
    q = q_ref[:, lanes(kh * width, width)]
    g = g_ref[:, lanes(kh * width, width)]
    k = k_ref[:, lanes(kh * HEAD, HEAD)]
    v = v_ref[:, lanes(kh * HEAD, HEAD)]
    q = jnp.concatenate([q[:, i * HEAD : (i + 1) * HEAD] for i in range(GROUPS)], axis=0)
    g = jnp.concatenate([g[:, i * HEAD : (i + 1) * HEAD] for i in range(GROUPS)], axis=0)
    scores = dot(k, q, NT) + bias
    top = jnp.max(scores, axis=0, keepdims=True)
    raised = jnp.exp2((scores - top) * EXP_FACTOR)
    probs = raised * (1.0 / jnp.sum(raised, axis=0, keepdims=True))
    probs_low = probs.astype(BF)
    grad_probs = dot(v, g, NT)
    delta = jnp.sum(probs_low.astype(F32) * grad_probs, axis=0, keepdims=True)
    grad_scores = (probs * FACTOR * (grad_probs - delta)).astype(BF)
    dv_ref[:, lanes(kh * HEAD, HEAD)] = dot(probs_low, g).astype(BF)
    dk_ref[kh % 2, :, lanes(kh // 2 * HEAD, HEAD)] = dot(grad_scores, q).astype(BF)
    dq = dot(grad_scores, k, TN).astype(BF)
    dq_ref[:, lanes(kh * width, width)] = jnp.concatenate(
        [dq[i * SHORT_DEV : (i + 1) * SHORT_DEV] for i in range(GROUPS)], axis=1
    )


HEADS = 6
WIDE = HEADS * CHUNK
STEPS = GROUPS // HEADS
OWN = NZH * CHUNK


def long_head(keys, hh, z_hi, q, g, kv, scores, grads, probs, low, acc_k):
    chunks = keys // CHUNK
    acc_k[0:keys, :] = jnp.zeros((keys, HEAD), F32)

    @pl.loop(0, STEPS)
    def _(p):
        col = lanes((hh * STEPS + p) * WIDE, WIDE)
        wide = lanes(p * WIDE, WIDE)
        qw, gw = q[:, col], g[:, col]
        qs = jnp.concatenate([qw[:, i * HEAD : (i + 1) * HEAD] for i in range(HEADS)], axis=0)
        gs = jnp.concatenate([gw[:, i * HEAD : (i + 1) * HEAD] for i in range(HEADS)], axis=0)
        top = None
        for n in range(chunks):
            at = slice(n * CHUNK, (n + 1) * CHUNK)
            s = dot(kv[hh, at, :HEAD], qs, NT)
            if n >= chunks - 2:
                key = lax.broadcasted_iota(jnp.int32, (CHUNK, WIDE), 0) + (n - chunks + 2) * CHUNK
                token = lax.broadcasted_iota(jnp.int32, (CHUNK, WIDE), 1) % CHUNK + z_hi * CHUNK
                s = jnp.where(key <= token, s, NEG)
            scores[at, :] = s
            m = jnp.max(s, axis=0, keepdims=True)
            top = m if top is None else jnp.maximum(top, m)
        total = delta = None
        for n in range(chunks):
            at = slice(n * CHUNK, (n + 1) * CHUNK)
            e = jnp.exp2((scores[at, :] - top) * EXP_FACTOR)
            scores[at, :] = e
            dp = dot(kv[hh, at, HEAD:], gs, NT)
            grads[at, :] = dp
            part = jnp.sum(e, axis=0, keepdims=True)
            total = part if total is None else total + part
            part = jnp.sum(e * dp, axis=0, keepdims=True)
            delta = part if delta is None else delta + part
        scale = 1.0 / total
        delta = delta * scale
        for n in range(chunks):
            at = slice(n * CHUNK, (n + 1) * CHUNK)
            pr = scores[at, :] * scale
            probs[hh, at, wide] = pr.astype(BF)
            ds = (pr * ((grads[at, :] - delta) * FACTOR)).astype(BF)
            low[hh, at, wide] = ds
            acc_k[at, :] += dot(ds, qs)


def long_rest(keys, hh, g, kv, dq, probs, low, acc_v):
    width = GROUPS * HEAD
    col = lanes(hh * width, width)
    gr = g[:, col]
    gs = jnp.concatenate([gr[:, i * HEAD : (i + 1) * HEAD] for i in range(GROUPS)], axis=0)
    for n in range(keys // CHUNK):
        at = slice(n * CHUNK, (n + 1) * CHUNK)
        acc_v[at, :] = dot(probs[hh, at, :], gs)
    kt = kv[hh, 0:keys, :HEAD].T
    for p in range(STEPS):
        out = dot(kt, low[hh, 0:keys, p * WIDE : (p + 1) * WIDE]).astype(BF).T
        dq[:, lanes(hh * width + p * WIDE, WIDE)] = jnp.concatenate(
            [out[i * CHUNK : (i + 1) * CHUNK] for i in range(HEADS)], axis=1
        )


def fold(a):
    return jnp.concatenate([a[:, :128], a[:, 128:]], axis=0)


def kernel(
    q_hbm, g_hbm, k_hbm, v_hbm, x_hbm, seg_hbm, master_hbm, first_hbm, second_hbm,
    gq, gv, new_master, new_first, new_second, new_weight,
    seg_ref, master, first, second, kvs,
    qs, gs, ks, vs, xs, xt, sdq, sgk, sgv,
    qb, gb, kvb, dq, scores, grads, probs, low, acc_k, acc_v, dks, dvs, totk, totv,
    rxk, rxv, zsk, zrk, zsv, zrv, gkl, gvl, xg, gk, wp, wr, wsum, zf, zp, zq, nwr,
    load_sem, key_sem, own_sem, q_send, q_recv, kv_send, kv_recv, fw_send, fw_recv, dq_send, dq_recv,
    rk_send, rk_recv, rv_send, rv_recv, zk_send, zk_recv, zv_send, zv_recv, x_send, x_recv,
    s_send, s_recv, l_send, l_recv, v_send, v_recv, w_send, w_recv, p_send, p_recv,
    nz_send, nz_recv, ny_send, ny_recv,
):
    y, z_lo, x, z_hi, core = place()
    c = lax.axis_index("ctx")
    z = z_hi * NZL + z_lo
    other = 1 - core
    sibling = device(y, z_lo, x, z_hi, other)
    partner = device(y, z_lo, x, 1 - z_hi, core)
    early, late = pl.ds(0, LONG_DEV), pl.ds(LONG_DEV, SHORT_DEV)
    my_tokens = lanes(core * TOK_DEV, TOK_DEV)

    own_rows = rows(c * LONG_DEV, LONG_DEV, 64)
    pair_rows = rows(core * LONG_DEV, LONG_DEV, 64)
    keyed = [
        pltpu.make_async_copy(
            src.at[early, pl.ds((2 * to + hh) * HEAD, HEAD)],
            kvs.at[to, hh, :, pl.ds(n * HEAD, HEAD)],
            key_sem.at[4 * to + 2 * hh + n],
        )
        for hh in range(2)
        for to in range(NC)
        for n, src in enumerate((k_hbm, v_hbm))
    ]
    loads = [
        pltpu.make_async_copy(hbm, vmem, load_sem.at[i])
        for i, (hbm, vmem) in enumerate(
            (
                (x_hbm, xs),
                (q_hbm.at[late, :], qs),
                (g_hbm.at[late, :], gs),
                (k_hbm.at[late, :], ks),
                (v_hbm.at[late, :], vs),
                (seg_hbm, seg_ref),
                (q_hbm.at[early, lanes(core * HALF_Q, HALF_Q)], qb.at[pair_rows, :]),
                (g_hbm.at[early, lanes(core * HALF_Q, HALF_Q)], gb.at[pair_rows, :]),
                (master_hbm, master),
                (first_hbm, first),
                (second_hbm, second),
            )
        )
    ]
    for copy in keyed + loads:
        copy.start()

    def x_peer(dx, sign):
        return (x + sign * dx + NX) % NX

    def z_peer(dz, sign):
        return (z + sign * dz + NZ) % NZ

    def z_device(pz):
        return device(y, pz % NZL, x, pz // NZL, core)

    group = [(dy, dc) for dy in range(NY) for dc in range(NC) if (dy, dc) != (0, 0)]

    def group_peer(i, sign):
        dy, dc = group[i]
        return (y + sign * dy + NY) % NY, (core + dc) % NC

    peers = [device(y, z_lo, x, 1 - z_hi, other)]
    peers += [z_device(z_peer(dz, 1)) for dz in (4, 3, 5, 2, 6, 1, 7)]
    peers += [device(y, z_lo, x_peer(dx, 1), z_hi, (core + dc) % NC) for dx in (2, 1, 3) for dc in (1, 0)]
    for i in range(len(group)):
        py, pc = group_peer(i, 1)
        peers.append(device(py, z_lo, x, z_hi, pc))
    barrier = pltpu.get_barrier_semaphore()
    for peer in peers:
        pl.semaphore_signal(barrier, inc=1, device_id=peer, device_id_type=MESH)

    for copy in keyed:
        copy.wait()
    own_kv = pltpu.make_async_copy(kvs.at[core], kvb.at[:, own_rows, :], own_sem.at[4])
    own_kv.start()
    pl.semaphore_wait(barrier, len(peers))

    def kv_copy(hh, px, pz, pc, slot, sending):
        where = own_rows if sending else rows(((px * NZH + pz) * NC + pc) * LONG_DEV, LONG_DEV, 64)
        return remote(
            kvs.at[pc if sending else core, hh], kvb.at[hh, where, :], kv_send.at[hh, slot], kv_recv.at[hh, slot],
            device(y, z_lo, px, pz, pc),
        )

    def partner_copy(hh, dc, sending):
        return kv_copy(hh, x, 1 - z_hi, (core + dc) % NC, dc, sending)

    def sibling_copy(hh, sending):
        return kv_copy(hh, x, z_hi, other, 2, sending)

    def near_copy(hh, dx, dc, sending):
        return kv_copy(hh, x + dx if sending else x - dx, z_hi, (core + dc) % NC, 1 + 2 * dx + dc, sending)

    for hh in range(2):
        for dc in range(NC):
            partner_copy(hh, dc, True).start()
    for hh in range(2):
        for dx in range(1, NX):

            @pl.when(x + dx < NX)
            def _():
                for dc in range(NC):
                    near_copy(hh, dx, dc, True).start()

        sibling_copy(hh, True).start()

    swaps = [
        remote(
            src.at[early, lanes(other * HALF_Q, HALF_Q)], dst.at[pair_rows, :], q_send.at[n], q_recv.at[n], sibling
        )
        for n, (src, dst) in enumerate(((q_hbm, qb), (g_hbm, gb)))
    ]
    for copy in swaps:
        copy.start()

    loads[0].wait()

    @pl.loop(0, D // 1024)
    def _(i):
        for j in range(8):
            at = i * 1024 + j * 128
            xt[rows(at, 128, 128), :] = xs[:, lanes(at, 128)].T

    def x_copy(i, sign):
        py, pc = group_peer(i, sign)
        sy, sc = (y, core) if sign > 0 else (py, pc)
        return remote(
            xt.reshape(NX * NZH, NC, NY, 96, TOK_DEV).at[:, pc, py],
            xg.at[sy, :, :, lanes(sc * TOK_DEV, TOK_DEV)],
            x_send.at[i], x_recv.at[i], device(py, z_lo, x, z_hi, pc),
        )

    for i in range(len(group)):
        x_copy(i, 1).start()
    mine = [
        pltpu.make_async_copy(
            xt.reshape(NX * NZH, NC, NY, 96, TOK_DEV).at[:, core, y], xg.at[y, :, :, my_tokens], own_sem.at[5]
        )
    ]
    mine[0].start()

    for copy in loads[1:6]:
        copy.wait()
    bias = short_mask(seg_ref)

    def heads(start, stop):
        @pl.loop(start, stop)
        def _(kh):
            short_head(kh, bias, qs, gs, ks, vs, sdq, sgk, sgv)

    heads(0, SHORT_FIRST)

    def forward(hh, dx, dc, sending):
        px = x + dx if sending else x - dx
        chip = (x if sending else px) * NZH + 1 - z_hi
        where = rows((chip * NC + (core + dc) % NC) * LONG_DEV, LONG_DEV, 64)
        return remote(
            kvb.at[hh, where, :], kvb.at[hh, where, :], fw_send.at[hh, dc, dx - 1], fw_recv.at[hh, dc, dx - 1],
            device(y, z_lo, px, z_hi, core),
        )

    for hh in range(2):
        for dc in range(NC):
            partner_copy(hh, dc, False).wait_recv()
            for dx in range(1, NX):

                @pl.when(x + dx < NX)
                def _():
                    forward(hh, dx, dc, True).start()

    heads(SHORT_FIRST, HK)

    def short_copy(i, sign):
        py, pc = group_peer(i, sign)
        sy, sc = (y, core) if sign > 0 else (py, pc)
        return remote(
            sgk, gk.at[:, sy, sc, late, :], s_send.at[i], s_recv.at[i], device(py, z_lo, x, z_hi, pc)
        )

    for i in range(len(group)):
        short_copy(i, 1).start()
    mine += [
        pltpu.make_async_copy(sgk, gk.at[:, y, core, late, :], own_sem.at[6]),
        pltpu.make_async_copy(sdq, gq.at[late, :], own_sem.at[7]),
        pltpu.make_async_copy(sgv, gv.at[late, :], own_sem.at[8]),
    ]
    for copy in mine[1:]:
        copy.start()

    for copy in loads[6:8]:
        copy.wait()
    own_kv.wait()
    for copy in swaps:
        copy.wait()

    def rk_copy(hh, dx, part, sending):
        px = x - dx if sending else x + dx
        chunk = (px if sending else x) * NZH + (1 - z_hi if part == 0 else z_hi)
        return remote(
            dks.at[hh, rows(chunk * CHUNK, CHUNK, 128), :], rxk.at[dx - 1, hh, part],
            rk_send.at[hh, part, dx - 1], rk_recv.at[hh, part, dx - 1], device(y, z_lo, px, z_hi, core),
        )

    def rv_copy(dx, sending):
        px = x - dx if sending else x + dx
        at = rows((px if sending else x) * OWN, OWN, 256)
        return remote(
            dvs.at[:, at, :], rxv.at[dx - 1], rv_send.at[dx - 1], rv_recv.at[dx - 1],
            device(y, z_lo, px, z_hi, core),
        )

    def zk_copy(hh):
        return remote(zsk.at[hh], zrk.at[hh], zk_send.at[hh], zk_recv.at[hh], partner)

    zv_copy = remote(zsv, zrv, zv_send.at[0], zv_recv.at[0], partner)
    ours = rows(z_hi * CHUNK, CHUNK, 128)
    theirs = rows((1 - z_hi) * CHUNK, CHUNK, 128)

    @pl.loop(0, 2)
    def _(hh):
        sibling_copy(hh, False).wait_recv()
        for n in range(NX):

            @pl.when(x == n)
            def _():
                keys, below = (n + 1) * OWN, n * OWN
                for dx in range(1, n + 1):
                    for dc in range(NC):
                        near_copy(hh, dx, dc, False).wait_recv()
                        forward(hh, dx, dc, False).wait_recv()
                long_head(keys, hh, z_hi, qb, gb, kvb, scores, grads, probs, low, acc_k)
                if below:
                    dks[hh, 0:below, :] = acc_k[0:below, :].astype(BF)
                totk[hh] = acc_k[below:keys, :]

        for part in range(2):
            for dx in range(1, NX):

                @pl.when(x >= dx)
                def _():
                    rk_copy(hh, dx, part, True).start()

        @pl.when(x == NX - 1)
        def _():
            zsk[hh] = totk[hh, theirs, :].astype(BF)
            zk_copy(hh).start()

    def sum_over_x(hh):
        for part in range(2):
            at = theirs if part == 0 else ours
            for dx in range(1, NX):

                @pl.when(x + dx < NX)
                def _():
                    rk_copy(hh, dx, part, False).wait_recv()
                    totk[hh, at, :] += rxk[dx - 1, hh, part].astype(F32)

            if part == 0:

                @pl.when(x < NX - 1)
                def _():
                    zsk[hh] = totk[hh, theirs, :].astype(BF)
                    zk_copy(hh).start()

    def long_copy(hh, i, sign):
        py, pc = group_peer(i, sign)
        sy, sc = (y, core) if sign > 0 else (py, pc)
        return remote(
            gkl.at[hh], gk.at[hh, sy, :, early, lanes(sc * HEAD, HEAD)], l_send.at[hh, i], l_recv.at[hh, i],
            device(py, z_lo, x, z_hi, pc),
        )

    def own_copy(hh):
        return pltpu.make_async_copy(
            gkl.at[hh], gk.at[hh, y, :, early, lanes(core * HEAD, HEAD)], own_sem.at[10 + hh]
        )

    def spread(hh):
        zk_copy(hh).wait_recv()
        both = (totk[hh, ours, :] + zrk[hh].astype(F32)).astype(BF)
        gkl[hh, 0] = both[:LONG_DEV]
        gkl[hh, 1] = both[LONG_DEV:]
        for i in range(len(group)):
            long_copy(hh, i, 1).start()
        own_copy(hh).start()

    @pl.when(x == NX - 1)
    def _():
        spread(0)

    @pl.loop(0, 2)
    def _(hh):
        for n in range(NX):

            @pl.when(x == n)
            def _():
                keys, below = (n + 1) * OWN, n * OWN
                long_rest(keys, hh, gb, kvb, dq, probs, low, acc_v)
                if below:
                    dvs[hh, 0:below, :] = acc_v[0:below, :].astype(BF)
                totv[hh] = acc_v[below:keys, :]

    for dx in range(1, NX):

        @pl.when(x >= dx)
        def _():
            rv_copy(dx, True).start()

    dq_copy = remote(
        dq.at[rows(other * LONG_DEV, LONG_DEV, 64), :], gq.at[early, lanes(core * HALF_Q, HALF_Q)],
        dq_send.at[0], dq_recv.at[0], sibling,
    )
    dq_copy.start()
    mine.append(
        pltpu.make_async_copy(dq.at[pair_rows, :], gq.at[early, lanes(core * HALF_Q, HALF_Q)], own_sem.at[9])
    )
    mine[-1].start()

    def w_copy(hh, dx, sign):
        px = x_peer(dx, sign)
        return remote(
            wp.at[hh, px], wr.at[hh, dx - 1], w_send.at[hh, dx - 1], w_recv.at[hh, dx - 1],
            device(y, z_lo, px, z_hi, core),
        )

    def product(hh, px):
        result = None
        for sy in range(NY):
            left = xg[sy, rows(NZH * px, NZH, 1)].reshape(NZH * 96, NC * TOK_DEV)
            term = dot(left, gk[hh, sy].reshape(NC * TOK_DEV, HALF_K))
            result = term if result is None else result + term
        return result.reshape(NZH, 96, HALF_K)

    def multiply(hh):
        own_copy(hh).wait()
        for i in range(len(group)):
            long_copy(hh, i, -1).wait_recv()
        for dx in (2, 1, 3):
            px = x_peer(dx, 1)
            wp[hh, px] = product(hh, px).astype(BF)
            w_copy(hh, dx, 1).start()
        wsum[hh] = product(hh, x)

    def p_copy(hh, dz, sign):
        pz = z_peer(dz, sign)
        return remote(
            zp.at[hh, pz], zq.at[hh, dz - 1], p_send.at[hh, dz - 1], p_recv.at[hh, dz - 1], z_device(pz)
        )

    def reduce_x(hh):
        for dx in (1, 3, 2):
            w_copy(hh, dx, -1).wait_recv()
            wsum[hh] += wr[hh, dx - 1].astype(F32)
        for pz in range(NZ):
            zf[hh, pz] = fold(wsum[hh, pz // NZL, (pz % NZL) * 24 : (pz % NZL + 1) * 24, :])
        zp[hh] = zf[hh].astype(BF)
        for dz in (4, 3, 5, 2, 6, 1, 7):
            p_copy(hh, dz, 1).start()

    d = lax.axis_index("dp")

    def nz_copy(hh, dz, sign):
        pz = (z_lo + sign * dz + NZL) % NZL
        slot = d if sign > 0 else y * NZL + pz
        return remote(
            nwr.at[hh, slot], nwr.at[hh, slot], nz_send.at[hh, dz - 1], nz_recv.at[hh, dz - 1],
            device(y, pz, x, z_hi, core),
        )

    def ny_copy(hh, dy, sign):
        py = (y + sign * dy + NY) % NY
        slots = rows((y if sign > 0 else py) * NZL, NZL, 1)
        return remote(
            nwr.at[hh, slots], nwr.at[hh, slots], ny_send.at[hh, dy - 1], ny_recv.at[hh, dy - 1],
            device(py, z_lo, x, z_hi, core),
        )

    def update(hh):
        share = zf[hh, z]
        for dz in range(1, NZ):
            p_copy(hh, dz, -1).wait_recv()
            share = share + zq[hh, dz - 1].astype(F32)
        share = share * (1.0 / (TOK_DEV * NY * NZ * NX * NC))
        fresh = []
        for b in range(2):
            col = slice((2 * b + hh) * 128, (2 * b + hh + 1) * 128)
            grad = share[b * 24 : (b + 1) * 24]
            moment = BETA_ONE * first[0, :, col] + (1.0 - BETA_ONE) * grad
            square = BETA_TWO * second[0, :, col] + (1.0 - BETA_TWO) * grad * grad
            first_hat = moment / (1.0 - BETA_ONE**STEP_COUNT)
            second_hat = square / (1.0 - BETA_TWO**STEP_COUNT)
            old = master[0, :, col]
            new = old - LEARN_RATE * (first_hat / (jnp.sqrt(second_hat) + ADAM_EPS) + DECAY * old)
            new_first[0, :, col] = moment
            new_second[0, :, col] = square
            new_master[0, :, col] = new
            fresh.append(new)
        nwr[hh, d] = jnp.concatenate(fresh, axis=0).astype(BF)
        for dz in range(1, NZL):
            nz_copy(hh, dz, 1).start()

    def pass_on(hh):
        for dz in (1, 3, 2):
            nz_copy(hh, dz, -1).wait_recv()
        for dy in (2, 1, 3):
            ny_copy(hh, dy, 1).start()

    def finish(hh):
        for dy in range(1, NY):
            ny_copy(hh, dy, -1).wait_recv()
        for pair in range(NY * NZL // 2):
            two = [nwr[hh, 2 * pair + i].astype(F32) for i in range(2)]
            for b in range(2):
                both = jnp.concatenate([t[b * 24 : (b + 1) * 24] for t in two], axis=0)
                new_weight[0, pair * 48 : (pair + 1) * 48, (2 * b + hh) * 128 : (2 * b + hh + 1) * 128] = both.astype(BF)

    for hh in range(2):
        sibling_copy(hh, True).wait_send()
        for dc in range(NC):
            partner_copy(hh, dc, True).wait_send()
    for dx in range(1, NX):

        @pl.when(x + dx < NX)
        def _():
            for hh in range(2):
                for dc in range(NC):
                    near_copy(hh, dx, dc, True).wait_send()
                    forward(hh, dx, dc, True).wait_send()

    @pl.when(x < NX - 1)
    def _():
        sum_over_x(0)
        spread(0)

    sum_over_x(1)
    spread(1)
    mine[0].wait()
    mine[1].wait()
    for i in range(len(group)):
        x_copy(i, -1).wait_recv()
        short_copy(i, -1).wait_recv()
    multiply(0)

    @pl.when(x < NX - 1)
    def _():
        for dx in range(1, NX):

            @pl.when(x + dx < NX)
            def _():
                rv_copy(dx, False).wait_recv()
                totv[...] += rxv[dx - 1].astype(F32)

    zsv[...] = totv[:, theirs, :].astype(BF)
    zv_copy.start()
    multiply(1)
    reduce_x(0)
    for copy in loads[8:]:
        copy.wait()
    reduce_x(1)
    update(0)
    zv_copy.wait_recv()
    for hh in range(2):
        both = (totv[hh, ours, :] + zrv[hh].astype(F32)).astype(BF)
        gvl[0, :, hh * HEAD : (hh + 1) * HEAD] = both[:LONG_DEV]
        gvl[1, :, hh * HEAD : (hh + 1) * HEAD] = both[LONG_DEV:]
    my_keys = lanes(core * HALF_K, HALF_K)
    v_copy = remote(gvl.at[other], gv.at[early, my_keys], v_send.at[0], v_recv.at[0], sibling)
    v_copy.start()
    mine.append(pltpu.make_async_copy(gvl.at[core], gv.at[early, my_keys], own_sem.at[12]))
    mine[-1].start()

    for dx in range(1, NX):

        @pl.when(x >= dx)
        def _():
            for hh in range(2):
                for part in range(2):
                    rk_copy(hh, dx, part, True).wait_send()
            rv_copy(dx, True).wait_send()

    for i in range(len(group)):
        x_copy(i, 1).wait_send()
        short_copy(i, 1).wait_send()
        for hh in range(2):
            long_copy(hh, i, 1).wait_send()
    for hh in range(2):
        zk_copy(hh).wait_send()
        for dx in range(1, NX):
            w_copy(hh, dx, 1).wait_send()
    zv_copy.wait_send()
    pass_on(0)
    update(1)
    finish(0)
    pass_on(1)
    for copy in mine[2:]:
        copy.wait()
    v_copy.wait()
    dq_copy.wait()
    for hh in range(2):
        for dz in range(1, NZ):
            p_copy(hh, dz, 1).wait_send()
        for dz in range(1, NZL):
            nz_copy(hh, dz, 1).wait_send()
    for dy in range(1, NY):
        ny_copy(0, dy, 1).wait_send()
    finish(1)
    for dy in range(1, NY):
        ny_copy(1, dy, 1).wait_send()


HBM = pl.BlockSpec(memory_space=pltpu.HBM)
VMEM = pl.BlockSpec(memory_space=pltpu.VMEM)
DMA = pltpu.SemaphoreType.DMA


def array(shape, dtype=BF):
    return jax.ShapeDtypeStruct(shape, dtype)


def store_kernel(*refs):
    copies = [pltpu.make_async_copy(refs[i], refs[6 + i], refs[12].at[i]) for i in range(6)]
    for copy in copies:
        copy.start()
    for copy in copies:
        copy.wait()


def on_device(
    layer_inputs, queries, key_states, value_states, output_grad, short_segments, master, first_moment, second_moment
):
    keys = NX * OWN
    tile = (1, 24, KD)
    pairs = lambda *shape: [DMA(shape), DMA(shape)]
    results = [
        array((TOK_DEV, QD)),
        array((TOK_DEV, KD)),
        array(tile, F32),
        array(tile, F32),
        array(tile, F32),
        array((1, 384, KD)),
    ]
    made = pl.pallas_call(
        kernel,
        name="step",
        out_shape=[pltpu.VMEM(r.shape, r.dtype) for r in results],
        in_specs=[HBM] * 9,
        out_specs=[VMEM] * 6,
        scratch_shapes=[
            pltpu.VMEM((1, SHORT_DEV), jnp.int32),
            *[pltpu.VMEM(tile, F32)] * 3,
            pltpu.VMEM((NC, 2, LONG_DEV, 2 * HEAD), BF),
            pltpu.VMEM((SHORT_DEV, QD), BF),
            pltpu.VMEM((SHORT_DEV, QD), BF),
            pltpu.VMEM((SHORT_DEV, KD), BF),
            pltpu.VMEM((SHORT_DEV, KD), BF),
            pltpu.VMEM((TOK_DEV, D), BF),
            pltpu.VMEM((D, TOK_DEV), BF),
            pltpu.VMEM((SHORT_DEV, QD), BF),
            pltpu.VMEM((2, SHORT_DEV, HALF_K), BF),
            pltpu.VMEM((SHORT_DEV, KD), BF),
            pltpu.VMEM((CHUNK, HALF_Q), BF),
            pltpu.VMEM((CHUNK, HALF_Q), BF),
            pltpu.VMEM((2, keys, 2 * HEAD), BF),
            pltpu.VMEM((CHUNK, HALF_Q), BF),
            pltpu.VMEM((keys, WIDE), F32),
            pltpu.VMEM((keys, WIDE), F32),
            pltpu.VMEM((2, keys, GROUPS * HEAD), BF),
            pltpu.VMEM((2, keys, GROUPS * HEAD), BF),
            pltpu.VMEM((keys, HEAD), F32),
            pltpu.VMEM((keys, HEAD), F32),
            pltpu.VMEM((2, keys, HEAD), BF),
            pltpu.VMEM((2, keys, HEAD), BF),
            pltpu.VMEM((2, OWN, HEAD), F32),
            pltpu.VMEM((2, OWN, HEAD), F32),
            pltpu.VMEM((NX - 1, 2, NZH, CHUNK, HEAD), BF),
            pltpu.VMEM((NX - 1, 2, OWN, HEAD), BF),
            pltpu.VMEM((2, CHUNK, HEAD), BF),
            pltpu.VMEM((2, CHUNK, HEAD), BF),
            pltpu.VMEM((2, CHUNK, HEAD), BF),
            pltpu.VMEM((2, CHUNK, HEAD), BF),
            pltpu.VMEM((2, NC, LONG_DEV, HEAD), BF),
            pltpu.VMEM((NC, LONG_DEV, HALF_K), BF),
            pltpu.VMEM((NY, NX * NZH, 96, NC * TOK_DEV), BF),
            pltpu.VMEM((2, NY, NC, TOK_DEV, HALF_K), BF),
            pltpu.VMEM((2, NX, NZH, 96, HALF_K), BF),
            pltpu.VMEM((2, NX - 1, NZH, 96, HALF_K), BF),
            pltpu.VMEM((2, NZH, 96, HALF_K), F32),
            pltpu.VMEM((2, NZ, 48, 128), F32),
            pltpu.VMEM((2, NZ, 48, 128), BF),
            pltpu.VMEM((2, NZ - 1, 48, 128), BF),
            pltpu.VMEM((2, NY * NZL, 48, 128), BF),
            DMA((11,)),
            DMA((8,)),
            DMA((13,)),
            *pairs(2),
            *pairs(2, 9),
            *pairs(2, 2, 3),
            *pairs(1),
            *pairs(2, 2, 3),
            *pairs(3),
            *pairs(2),
            *pairs(1),
            *pairs(7),
            *pairs(7),
            *pairs(2, 7),
            *pairs(1),
            *pairs(2, 3),
            *pairs(2, 7),
            *pairs(2, 3),
            *pairs(2, 3),
        ],
        compiler_params=pltpu.CompilerParams(
            vmem_limit_bytes=VMEM_LIMIT, collective_id=1, has_side_effects=True
        ),
    )(
        queries, output_grad, key_states, value_states, layer_inputs, short_segments,
        master, first_moment, second_moment,
    )
    return pl.pallas_call(
        store_kernel,
        name="store",
        out_shape=results,
        in_specs=[VMEM] * 6,
        out_specs=[HBM] * 6,
        scratch_shapes=[DMA((6,))],
        compiler_params=pltpu.CompilerParams(vmem_limit_bytes=8 << 20),
    )(*made)


def solution(mesh):
    tokens = P(("dp", "ctx"), None)
    shard = P("ctx", "dp", None)
    return jax.shard_map(
        on_device,
        mesh=mesh,
        in_specs=(tokens,) * 6 + (shard,) * 3,
        out_specs=(tokens, tokens, shard, shard, shard, P("ctx", None, None)),
        check_vma=False,
    )
```

```python
import functools

import jax
import jax.numpy as jnp
from jax import lax
from jax.experimental import pallas as pl
from jax.experimental.pallas import tpu as pltpu
from jax.sharding import PartitionSpec as P

D = 6144
HEAD = 128
GROUPS = 12
HK = 4
SHORT_FIRST = 4
LONG_DEV = 64
SHORT_DEV = 64
TOK_DEV = 128
CHUNK = 128
KD = 512
QD = 6144
HALF_Q = 3072
HALF_K = 256
NY, NZL, NX, NZH, NC = 4, 4, 4, 2, 2
NZ = NZL * NZH

LEARN_RATE = 0.001
BETA_ONE = 0.9
BETA_TWO = 0.95
ADAM_EPS = 1e-08
DECAY = 0.1
STEP_COUNT = 10

MESH = pl.DeviceIdType.MESH
FACTOR = HEAD**-0.5
EXP_FACTOR = FACTOR * 1.4426950408889634
NEG = -1e30
BF = jnp.bfloat16
VMEM_LIMIT = 58 << 20
F32 = jnp.float32
NT = (((1,), (1,)), ((), ()))
TN = (((0,), (0,)), ((), ()))


def dot(a, b, dims=(((1,), (0,)), ((), ()))):
    return lax.dot_general(a, b, dims, preferred_element_type=F32)


def place():
    d = lax.axis_index("dp")
    c = lax.axis_index("ctx")
    return d // NZL, d % NZL, c // (NZH * NC), (c // NC) % NZH, c % NC


def device(y, z_lo, x, z_hi, core):
    return (y * NZL + z_lo, (x * NZH + z_hi) * NC + core)


def remote(src, dst, send, recv, peer):
    return pltpu.make_async_remote_copy(
        src_ref=src, dst_ref=dst, send_sem=send, recv_sem=recv, device_id=peer, device_id_type=MESH
    )


def lanes(start, size):
    return pl.ds(pl.multiple_of(start, 128), size)


def rows(start, size, unit):
    return pl.ds(pl.multiple_of(start, unit), size)


def short_mask(seg_ref):
    segment = seg_ref[...]
    square = jnp.broadcast_to(segment, (SHORT_DEV, SHORT_DEV))
    diag = lax.broadcasted_iota(jnp.int32, (SHORT_DEV, SHORT_DEV), 0) == lax.broadcasted_iota(
        jnp.int32, (SHORT_DEV, SHORT_DEV), 1
    )
    column = jnp.sum(jnp.where(diag, square.astype(F32), 0.0), axis=1, keepdims=True)
    row = jnp.concatenate([segment.astype(F32)] * 2, axis=1)
    key = lax.broadcasted_iota(jnp.int32, (SHORT_DEV, 128), 0)
    token = lax.broadcasted_iota(jnp.int32, (SHORT_DEV, 128), 1) % SHORT_DEV
    pair = jnp.where((column == row) & (key <= token), 0.0, NEG)
    return jnp.concatenate([pair] * (GROUPS // 2), axis=1)


def short_head(kh, bias, q_ref, g_ref, k_ref, v_ref, dq_ref, dk_ref, dv_ref):
    width = GROUPS * HEAD
    q = q_ref[:, lanes(kh * width, width)]
    g = g_ref[:, lanes(kh * width, width)]
    k = k_ref[:, lanes(kh * HEAD, HEAD)]
    v = v_ref[:, lanes(kh * HEAD, HEAD)]
    q = jnp.concatenate([q[:, i * HEAD : (i + 1) * HEAD] for i in range(GROUPS)], axis=0)
    g = jnp.concatenate([g[:, i * HEAD : (i + 1) * HEAD] for i in range(GROUPS)], axis=0)
    scores = dot(k, q, NT) + bias
    top = jnp.max(scores, axis=0, keepdims=True)
    raised = jnp.exp2((scores - top) * EXP_FACTOR)
    probs = raised * (1.0 / jnp.sum(raised, axis=0, keepdims=True))
    probs_low = probs.astype(BF)
    grad_probs = dot(v, g, NT)
    delta = jnp.sum(probs_low.astype(F32) * grad_probs, axis=0, keepdims=True)
    grad_scores = (probs * FACTOR * (grad_probs - delta)).astype(BF)
    dv_ref[:, lanes(kh * HEAD, HEAD)] = dot(probs_low, g).astype(BF)
    dk_ref[kh % 2, :, lanes(kh // 2 * HEAD, HEAD)] = dot(grad_scores, q).astype(BF)
    dq = dot(grad_scores, k, TN).astype(BF)
    dq_ref[:, lanes(kh * width, width)] = jnp.concatenate(
        [dq[i * SHORT_DEV : (i + 1) * SHORT_DEV] for i in range(GROUPS)], axis=1
    )


HEADS = 6
WIDE = HEADS * CHUNK
STEPS = GROUPS // HEADS
OWN = NZH * CHUNK


def long_head(keys, hh, z_hi, q, g, kv, scores, grads, probs, low, acc_k):
    chunks = keys // CHUNK
    acc_k[0:keys, :] = jnp.zeros((keys, HEAD), F32)

    @pl.loop(0, STEPS)
    def _(p):
        col = lanes((hh * STEPS + p) * WIDE, WIDE)
        wide = lanes(p * WIDE, WIDE)
        qw, gw = q[:, col], g[:, col]
        qs = jnp.concatenate([qw[:, i * HEAD : (i + 1) * HEAD] for i in range(HEADS)], axis=0)
        gs = jnp.concatenate([gw[:, i * HEAD : (i + 1) * HEAD] for i in range(HEADS)], axis=0)
        top = None
        for n in range(chunks):
            at = slice(n * CHUNK, (n + 1) * CHUNK)
            s = dot(kv[hh, at, :HEAD], qs, NT)
            if n >= chunks - 2:
                key = lax.broadcasted_iota(jnp.int32, (CHUNK, WIDE), 0) + (n - chunks + 2) * CHUNK
                token = lax.broadcasted_iota(jnp.int32, (CHUNK, WIDE), 1) % CHUNK + z_hi * CHUNK
                s = jnp.where(key <= token, s, NEG)
            scores[at, :] = s
            m = jnp.max(s, axis=0, keepdims=True)
            top = m if top is None else jnp.maximum(top, m)
        total = delta = None
        for n in range(chunks):
            at = slice(n * CHUNK, (n + 1) * CHUNK)
            e = jnp.exp2((scores[at, :] - top) * EXP_FACTOR)
            scores[at, :] = e
            dp = dot(kv[hh, at, HEAD:], gs, NT)
            grads[at, :] = dp
            part = jnp.sum(e, axis=0, keepdims=True)
            total = part if total is None else total + part
            part = jnp.sum(e * dp, axis=0, keepdims=True)
            delta = part if delta is None else delta + part
        scale = 1.0 / total
        delta = delta * scale
        for n in range(chunks):
            at = slice(n * CHUNK, (n + 1) * CHUNK)
            pr = scores[at, :] * scale
            probs[hh, at, wide] = pr.astype(BF)
            ds = (pr * ((grads[at, :] - delta) * FACTOR)).astype(BF)
            low[hh, at, wide] = ds
            acc_k[at, :] += dot(ds, qs)


def long_rest(keys, hh, g, kv, dq, probs, low, acc_v):
    width = GROUPS * HEAD
    col = lanes(hh * width, width)
    gr = g[:, col]
    gs = jnp.concatenate([gr[:, i * HEAD : (i + 1) * HEAD] for i in range(GROUPS)], axis=0)
    for n in range(keys // CHUNK):
        at = slice(n * CHUNK, (n + 1) * CHUNK)
        acc_v[at, :] = dot(probs[hh, at, :], gs)
    kt = kv[hh, 0:keys, :HEAD].T
    for p in range(STEPS):
        out = dot(kt, low[hh, 0:keys, p * WIDE : (p + 1) * WIDE]).astype(BF).T
        dq[:, lanes(hh * width + p * WIDE, WIDE)] = jnp.concatenate(
            [out[i * CHUNK : (i + 1) * CHUNK] for i in range(HEADS)], axis=1
        )


def fold(a):
    return jnp.concatenate([a[:, :128], a[:, 128:]], axis=0)


def kernel(
    q_hbm, g_hbm, k_hbm, v_hbm, x_hbm, seg_hbm, master_hbm, first_hbm, second_hbm,
    gq, gv, new_master, new_first, new_second, new_weight,
    seg_ref, master, first, second, kvs,
    qs, gs, ks, vs, xs, xt, sdq, sgk, sgv,
    qb, gb, kvb, dq, scores, grads, probs, low, acc_k, acc_v, dks, dvs, totk, totv,
    rxk, rxv, zsk, zrk, zsv, zrv, gkl, gvl, xg, gk, wp, wr, wsum, zf, zp, zq, nwr,
    load_sem, key_sem, own_sem, q_send, q_recv, kv_send, kv_recv, fw_send, fw_recv, dq_send, dq_recv,
    rk_send, rk_recv, rv_send, rv_recv, zk_send, zk_recv, zv_send, zv_recv, x_send, x_recv,
    s_send, s_recv, l_send, l_recv, v_send, v_recv, w_send, w_recv, p_send, p_recv,
    nz_send, nz_recv, ny_send, ny_recv,
):
    y, z_lo, x, z_hi, core = place()
    c = lax.axis_index("ctx")
    z = z_hi * NZL + z_lo
    other = 1 - core
    sibling = device(y, z_lo, x, z_hi, other)
    partner = device(y, z_lo, x, 1 - z_hi, core)
    early, late = pl.ds(0, LONG_DEV), pl.ds(LONG_DEV, SHORT_DEV)
    my_tokens = lanes(core * TOK_DEV, TOK_DEV)

    own_rows = rows(c * LONG_DEV, LONG_DEV, 64)
    pair_rows = rows(core * LONG_DEV, LONG_DEV, 64)
    keyed = [
        pltpu.make_async_copy(
            src.at[early, pl.ds((2 * to + hh) * HEAD, HEAD)],
            kvs.at[to, hh, :, pl.ds(n * HEAD, HEAD)],
            key_sem.at[4 * to + 2 * hh + n],
        )
        for hh in range(2)
        for to in range(NC)
        for n, src in enumerate((k_hbm, v_hbm))
    ]
    loads = [
        pltpu.make_async_copy(hbm, vmem, load_sem.at[i])
        for i, (hbm, vmem) in enumerate(
            (
                (x_hbm, xs),
                (q_hbm.at[late, :], qs),
                (g_hbm.at[late, :], gs),
                (k_hbm.at[late, :], ks),
                (v_hbm.at[late, :], vs),
                (seg_hbm, seg_ref),
                (q_hbm.at[early, lanes(core * HALF_Q, HALF_Q)], qb.at[pair_rows, :]),
                (g_hbm.at[early, lanes(core * HALF_Q, HALF_Q)], gb.at[pair_rows, :]),
                (master_hbm, master),
                (first_hbm, first),
                (second_hbm, second),
            )
        )
    ]
    for copy in keyed + loads:
        copy.start()

    def x_peer(dx, sign):
        return (x + sign * dx + NX) % NX

    def z_peer(dz, sign):
        return (z + sign * dz + NZ) % NZ

    def z_device(pz):
        return device(y, pz % NZL, x, pz // NZL, core)

    group = [(dy, dc) for dy in range(NY) for dc in range(NC) if (dy, dc) != (0, 0)]

    def group_peer(i, sign):
        dy, dc = group[i]
        return (y + sign * dy + NY) % NY, (core + dc) % NC

    peers = [device(y, z_lo, x, 1 - z_hi, other)]
    peers += [z_device(z_peer(dz, 1)) for dz in (4, 3, 5, 2, 6, 1, 7)]
    peers += [device(y, z_lo, x_peer(dx, 1), z_hi, (core + dc) % NC) for dx in (2, 1, 3) for dc in (1, 0)]
    for i in range(len(group)):
        py, pc = group_peer(i, 1)
        peers.append(device(py, z_lo, x, z_hi, pc))
    barrier = pltpu.get_barrier_semaphore()
    for peer in peers:
        pl.semaphore_signal(barrier, inc=1, device_id=peer, device_id_type=MESH)

    for copy in keyed:
        copy.wait()
    own_kv = pltpu.make_async_copy(kvs.at[core], kvb.at[:, own_rows, :], own_sem.at[4])
    own_kv.start()
    pl.semaphore_wait(barrier, len(peers))

    def kv_copy(hh, px, pz, pc, slot, sending):
        where = own_rows if sending else rows(((px * NZH + pz) * NC + pc) * LONG_DEV, LONG_DEV, 64)
        return remote(
            kvs.at[pc if sending else core, hh], kvb.at[hh, where, :], kv_send.at[hh, slot], kv_recv.at[hh, slot],
            device(y, z_lo, px, pz, pc),
        )

    def partner_copy(hh, dc, sending):
        return kv_copy(hh, x, 1 - z_hi, (core + dc) % NC, dc, sending)

    def sibling_copy(hh, sending):
        return kv_copy(hh, x, z_hi, other, 2, sending)

    def near_copy(hh, dx, dc, sending):
        return kv_copy(hh, x + dx if sending else x - dx, z_hi, (core + dc) % NC, 1 + 2 * dx + dc, sending)

    for hh in range(2):
        for dc in range(NC):
            partner_copy(hh, dc, True).start()
    for hh in range(2):
        for dx in range(1, NX):

            @pl.when(x + dx < NX)
            def _():
                for dc in range(NC):
                    near_copy(hh, dx, dc, True).start()

        sibling_copy(hh, True).start()

    swaps = [
        remote(
            src.at[early, lanes(other * HALF_Q, HALF_Q)], dst.at[pair_rows, :], q_send.at[n], q_recv.at[n], sibling
        )
        for n, (src, dst) in enumerate(((q_hbm, qb), (g_hbm, gb)))
    ]
    for copy in swaps:
        copy.start()

    loads[0].wait()

    @pl.loop(0, D // 1024)
    def _(i):
        for j in range(8):
            at = i * 1024 + j * 128
            xt[rows(at, 128, 128), :] = xs[:, lanes(at, 128)].T

    def x_copy(i, sign):
        py, pc = group_peer(i, sign)
        sy, sc = (y, core) if sign > 0 else (py, pc)
        return remote(
            xt.reshape(NX * NZH, NC, NY, 96, TOK_DEV).at[:, pc, py],
            xg.at[sy, :, :, lanes(sc * TOK_DEV, TOK_DEV)],
            x_send.at[i], x_recv.at[i], device(py, z_lo, x, z_hi, pc),
        )

    for i in range(len(group)):
        x_copy(i, 1).start()
    mine = [
        pltpu.make_async_copy(
            xt.reshape(NX * NZH, NC, NY, 96, TOK_DEV).at[:, core, y], xg.at[y, :, :, my_tokens], own_sem.at[5]
        )
    ]
    mine[0].start()

    for copy in loads[1:6]:
        copy.wait()
    bias = short_mask(seg_ref)

    def heads(start, stop):
        @pl.loop(start, stop)
        def _(kh):
            short_head(kh, bias, qs, gs, ks, vs, sdq, sgk, sgv)

    heads(0, SHORT_FIRST)

    def forward(hh, dx, dc, sending):
        px = x + dx if sending else x - dx
        chip = (x if sending else px) * NZH + 1 - z_hi
        where = rows((chip * NC + (core + dc) % NC) * LONG_DEV, LONG_DEV, 64)
        return remote(
            kvb.at[hh, where, :], kvb.at[hh, where, :], fw_send.at[hh, dc, dx - 1], fw_recv.at[hh, dc, dx - 1],
            device(y, z_lo, px, z_hi, core),
        )

    for hh in range(2):
        for dc in range(NC):
            partner_copy(hh, dc, False).wait_recv()
            for dx in range(1, NX):

                @pl.when(x + dx < NX)
                def _():
                    forward(hh, dx, dc, True).start()

    heads(SHORT_FIRST, HK)

    def short_copy(i, sign):
        py, pc = group_peer(i, sign)
        sy, sc = (y, core) if sign > 0 else (py, pc)
        return remote(
            sgk, gk.at[:, sy, sc, late, :], s_send.at[i], s_recv.at[i], device(py, z_lo, x, z_hi, pc)
        )

    for i in range(len(group)):
        short_copy(i, 1).start()
    mine += [
        pltpu.make_async_copy(sgk, gk.at[:, y, core, late, :], own_sem.at[6]),
        pltpu.make_async_copy(sdq, gq.at[late, :], own_sem.at[7]),
        pltpu.make_async_copy(sgv, gv.at[late, :], own_sem.at[8]),
    ]
    for copy in mine[1:]:
        copy.start()

    for copy in loads[6:8]:
        copy.wait()
    own_kv.wait()
    for copy in swaps:
        copy.wait()

    def rk_copy(hh, dx, part, sending):
        px = x - dx if sending else x + dx
        chunk = (px if sending else x) * NZH + (1 - z_hi if part == 0 else z_hi)
        return remote(
            dks.at[hh, rows(chunk * CHUNK, CHUNK, 128), :], rxk.at[dx - 1, hh, part],
            rk_send.at[hh, part, dx - 1], rk_recv.at[hh, part, dx - 1], device(y, z_lo, px, z_hi, core),
        )

    def rv_copy(dx, sending):
        px = x - dx if sending else x + dx
        at = rows((px if sending else x) * OWN, OWN, 256)
        return remote(
            dvs.at[:, at, :], rxv.at[dx - 1], rv_send.at[dx - 1], rv_recv.at[dx - 1],
            device(y, z_lo, px, z_hi, core),
        )

    def zk_copy(hh):
        return remote(zsk.at[hh], zrk.at[hh], zk_send.at[hh], zk_recv.at[hh], partner)

    zv_copy = remote(zsv, zrv, zv_send.at[0], zv_recv.at[0], partner)
    ours = rows(z_hi * CHUNK, CHUNK, 128)
    theirs = rows((1 - z_hi) * CHUNK, CHUNK, 128)

    @pl.loop(0, 2)
    def _(hh):
        sibling_copy(hh, False).wait_recv()
        for n in range(NX):

            @pl.when(x == n)
            def _():
                keys, below = (n + 1) * OWN, n * OWN
                for dx in range(1, n + 1):
                    for dc in range(NC):
                        near_copy(hh, dx, dc, False).wait_recv()
                        forward(hh, dx, dc, False).wait_recv()
                long_head(keys, hh, z_hi, qb, gb, kvb, scores, grads, probs, low, acc_k)
                if below:
                    dks[hh, 0:below, :] = acc_k[0:below, :].astype(BF)
                totk[hh] = acc_k[below:keys, :]

        for part in range(2):
            for dx in range(1, NX):

                @pl.when(x >= dx)
                def _():
                    rk_copy(hh, dx, part, True).start()

        @pl.when(x == NX - 1)
        def _():
            zsk[hh] = totk[hh, theirs, :].astype(BF)
            zk_copy(hh).start()

    def sum_over_x(hh):
        for part in range(2):
            at = theirs if part == 0 else ours
            for dx in range(1, NX):

                @pl.when(x + dx < NX)
                def _():
                    rk_copy(hh, dx, part, False).wait_recv()
                    totk[hh, at, :] += rxk[dx - 1, hh, part].astype(F32)

            if part == 0:

                @pl.when(x < NX - 1)
                def _():
                    zsk[hh] = totk[hh, theirs, :].astype(BF)
                    zk_copy(hh).start()

    def long_copy(hh, i, sign):
        py, pc = group_peer(i, sign)
        sy, sc = (y, core) if sign > 0 else (py, pc)
        return remote(
            gkl.at[hh], gk.at[hh, sy, :, early, lanes(sc * HEAD, HEAD)], l_send.at[hh, i], l_recv.at[hh, i],
            device(py, z_lo, x, z_hi, pc),
        )

    def own_copy(hh):
        return pltpu.make_async_copy(
            gkl.at[hh], gk.at[hh, y, :, early, lanes(core * HEAD, HEAD)], own_sem.at[10 + hh]
        )

    def spread(hh):
        zk_copy(hh).wait_recv()
        both = (totk[hh, ours, :] + zrk[hh].astype(F32)).astype(BF)
        gkl[hh, 0] = both[:LONG_DEV]
        gkl[hh, 1] = both[LONG_DEV:]
        for i in range(len(group)):
            long_copy(hh, i, 1).start()
        own_copy(hh).start()

    @pl.when(x == NX - 1)
    def _():
        spread(0)

    @pl.loop(0, 2)
    def _(hh):
        for n in range(NX):

            @pl.when(x == n)
            def _():
                keys, below = (n + 1) * OWN, n * OWN
                long_rest(keys, hh, gb, kvb, dq, probs, low, acc_v)
                if below:
                    dvs[hh, 0:below, :] = acc_v[0:below, :].astype(BF)
                totv[hh] = acc_v[below:keys, :]

    for dx in range(1, NX):

        @pl.when(x >= dx)
        def _():
            rv_copy(dx, True).start()

    dq_copy = remote(
        dq.at[rows(other * LONG_DEV, LONG_DEV, 64), :], gq.at[early, lanes(core * HALF_Q, HALF_Q)],
        dq_send.at[0], dq_recv.at[0], sibling,
    )
    dq_copy.start()
    mine.append(
        pltpu.make_async_copy(dq.at[pair_rows, :], gq.at[early, lanes(core * HALF_Q, HALF_Q)], own_sem.at[9])
    )
    mine[-1].start()

    def w_copy(hh, dx, sign):
        px = x_peer(dx, sign)
        return remote(
            wp.at[hh, px], wr.at[hh, dx - 1], w_send.at[hh, dx - 1], w_recv.at[hh, dx - 1],
            device(y, z_lo, px, z_hi, core),
        )

    def product(hh, px):
        result = None
        for sy in range(NY):
            left = xg[sy, rows(NZH * px, NZH, 1)].reshape(NZH * 96, NC * TOK_DEV)
            term = dot(left, gk[hh, sy].reshape(NC * TOK_DEV, HALF_K))
            result = term if result is None else result + term
        return result.reshape(NZH, 96, HALF_K)

    def multiply(hh):
        own_copy(hh).wait()
        for i in range(len(group)):
            long_copy(hh, i, -1).wait_recv()
        for dx in (2, 1, 3):
            px = x_peer(dx, 1)
            wp[hh, px] = product(hh, px).astype(BF)
            w_copy(hh, dx, 1).start()
        wsum[hh] = product(hh, x)

    def p_copy(hh, dz, sign):
        pz = z_peer(dz, sign)
        return remote(
            zp.at[hh, pz], zq.at[hh, dz - 1], p_send.at[hh, dz - 1], p_recv.at[hh, dz - 1], z_device(pz)
        )

    def reduce_x(hh):
        for dx in (1, 3, 2):
            w_copy(hh, dx, -1).wait_recv()
            wsum[hh] += wr[hh, dx - 1].astype(F32)
        for pz in range(NZ):
            zf[hh, pz] = fold(wsum[hh, pz // NZL, (pz % NZL) * 24 : (pz % NZL + 1) * 24, :])
        zp[hh] = zf[hh].astype(BF)
        for dz in (4, 3, 5, 2, 6, 1, 7):
            p_copy(hh, dz, 1).start()

    d = lax.axis_index("dp")

    def nz_copy(hh, dz, sign):
        pz = (z_lo + sign * dz + NZL) % NZL
        slot = d if sign > 0 else y * NZL + pz
        return remote(
            nwr.at[hh, slot], nwr.at[hh, slot], nz_send.at[hh, dz - 1], nz_recv.at[hh, dz - 1],
            device(y, pz, x, z_hi, core),
        )

    def ny_copy(hh, dy, sign):
        py = (y + sign * dy + NY) % NY
        slots = rows((y if sign > 0 else py) * NZL, NZL, 1)
        return remote(
            nwr.at[hh, slots], nwr.at[hh, slots], ny_send.at[hh, dy - 1], ny_recv.at[hh, dy - 1],
            device(py, z_lo, x, z_hi, core),
        )

    def update(hh):
        share = zf[hh, z]
        for dz in range(1, NZ):
            p_copy(hh, dz, -1).wait_recv()
            share = share + zq[hh, dz - 1].astype(F32)
        share = share * (1.0 / (TOK_DEV * NY * NZ * NX * NC))
        fresh = []
        for b in range(2):
            col = slice((2 * b + hh) * 128, (2 * b + hh + 1) * 128)
            grad = share[b * 24 : (b + 1) * 24]
            moment = BETA_ONE * first[0, :, col] + (1.0 - BETA_ONE) * grad
            square = BETA_TWO * second[0, :, col] + (1.0 - BETA_TWO) * grad * grad
            first_hat = moment / (1.0 - BETA_ONE**STEP_COUNT)
            second_hat = square / (1.0 - BETA_TWO**STEP_COUNT)
            old = master[0, :, col]
            new = old - LEARN_RATE * (first_hat / (jnp.sqrt(second_hat) + ADAM_EPS) + DECAY * old)
            new_first[0, :, col] = moment
            new_second[0, :, col] = square
            new_master[0, :, col] = new
            fresh.append(new)
        nwr[hh, d] = jnp.concatenate(fresh, axis=0).astype(BF)
        for dz in (3, 1, 2):
            nz_copy(hh, dz, 1).start()

    def pass_on(hh):
        for dz in (1, 3, 2):
            nz_copy(hh, dz, -1).wait_recv()
        for dy in (2, 1, 3):
            ny_copy(hh, dy, 1).start()

    def finish(hh):
        for dy in range(1, NY):
            ny_copy(hh, dy, -1).wait_recv()
        for pair in range(NY * NZL // 2):
            two = [nwr[hh, 2 * pair + i].astype(F32) for i in range(2)]
            for b in range(2):
                both = jnp.concatenate([t[b * 24 : (b + 1) * 24] for t in two], axis=0)
                new_weight[0, pair * 48 : (pair + 1) * 48, (2 * b + hh) * 128 : (2 * b + hh + 1) * 128] = both.astype(BF)

    for hh in range(2):
        sibling_copy(hh, True).wait_send()
        for dc in range(NC):
            partner_copy(hh, dc, True).wait_send()
    for dx in range(1, NX):

        @pl.when(x + dx < NX)
        def _():
            for hh in range(2):
                for dc in range(NC):
                    near_copy(hh, dx, dc, True).wait_send()
                    forward(hh, dx, dc, True).wait_send()

    @pl.when(x < NX - 1)
    def _():
        sum_over_x(0)
        spread(0)

    sum_over_x(1)
    spread(1)
    mine[0].wait()
    mine[1].wait()
    for i in range(len(group)):
        x_copy(i, -1).wait_recv()
        short_copy(i, -1).wait_recv()
    multiply(0)

    @pl.when(x < NX - 1)
    def _():
        for dx in range(1, NX):

            @pl.when(x + dx < NX)
            def _():
                rv_copy(dx, False).wait_recv()
                totv[...] += rxv[dx - 1].astype(F32)

    zsv[...] = totv[:, theirs, :].astype(BF)
    zv_copy.start()
    multiply(1)
    reduce_x(0)
    for copy in loads[8:]:
        copy.wait()
    reduce_x(1)
    update(0)
    zv_copy.wait_recv()
    for hh in range(2):
        both = (totv[hh, ours, :] + zrv[hh].astype(F32)).astype(BF)
        gvl[0, :, hh * HEAD : (hh + 1) * HEAD] = both[:LONG_DEV]
        gvl[1, :, hh * HEAD : (hh + 1) * HEAD] = both[LONG_DEV:]
    my_keys = lanes(core * HALF_K, HALF_K)
    v_copy = remote(gvl.at[other], gv.at[early, my_keys], v_send.at[0], v_recv.at[0], sibling)
    v_copy.start()
    mine.append(pltpu.make_async_copy(gvl.at[core], gv.at[early, my_keys], own_sem.at[12]))
    mine[-1].start()

    for dx in range(1, NX):

        @pl.when(x >= dx)
        def _():
            for hh in range(2):
                for part in range(2):
                    rk_copy(hh, dx, part, True).wait_send()
            rv_copy(dx, True).wait_send()

    for i in range(len(group)):
        x_copy(i, 1).wait_send()
        short_copy(i, 1).wait_send()
        for hh in range(2):
            long_copy(hh, i, 1).wait_send()
    for hh in range(2):
        zk_copy(hh).wait_send()
        for dx in range(1, NX):
            w_copy(hh, dx, 1).wait_send()
    zv_copy.wait_send()
    pass_on(0)
    update(1)
    finish(0)
    pass_on(1)
    for copy in mine[2:]:
        copy.wait()
    v_copy.wait()
    dq_copy.wait()
    for hh in range(2):
        for dz in range(1, NZ):
            p_copy(hh, dz, 1).wait_send()
        for dz in range(1, NZL):
            nz_copy(hh, dz, 1).wait_send()
    for dy in range(1, NY):
        ny_copy(0, dy, 1).wait_send()
    finish(1)
    for dy in range(1, NY):
        ny_copy(1, dy, 1).wait_send()


HBM = pl.BlockSpec(memory_space=pltpu.HBM)
VMEM = pl.BlockSpec(memory_space=pltpu.VMEM)
DMA = pltpu.SemaphoreType.DMA


def array(shape, dtype=BF):
    return jax.ShapeDtypeStruct(shape, dtype)


def store_kernel(*refs):
    copies = [pltpu.make_async_copy(refs[i], refs[6 + i], refs[12].at[i]) for i in range(6)]
    for copy in copies:
        copy.start()
    for copy in copies:
        copy.wait()


def on_device(
    layer_inputs, queries, key_states, value_states, output_grad, short_segments, master, first_moment, second_moment
):
    keys = NX * OWN
    tile = (1, 24, KD)
    pairs = lambda *shape: [DMA(shape), DMA(shape)]
    results = [
        array((TOK_DEV, QD)),
        array((TOK_DEV, KD)),
        array(tile, F32),
        array(tile, F32),
        array(tile, F32),
        array((1, 384, KD)),
    ]
    made = pl.pallas_call(
        kernel,
        name="step",
        out_shape=[pltpu.VMEM(r.shape, r.dtype) for r in results],
        in_specs=[HBM] * 9,
        out_specs=[VMEM] * 6,
        scratch_shapes=[
            pltpu.VMEM((1, SHORT_DEV), jnp.int32),
            *[pltpu.VMEM(tile, F32)] * 3,
            pltpu.VMEM((NC, 2, LONG_DEV, 2 * HEAD), BF),
            pltpu.VMEM((SHORT_DEV, QD), BF),
            pltpu.VMEM((SHORT_DEV, QD), BF),
            pltpu.VMEM((SHORT_DEV, KD), BF),
            pltpu.VMEM((SHORT_DEV, KD), BF),
            pltpu.VMEM((TOK_DEV, D), BF),
            pltpu.VMEM((D, TOK_DEV), BF),
            pltpu.VMEM((SHORT_DEV, QD), BF),
            pltpu.VMEM((2, SHORT_DEV, HALF_K), BF),
            pltpu.VMEM((SHORT_DEV, KD), BF),
            pltpu.VMEM((CHUNK, HALF_Q), BF),
            pltpu.VMEM((CHUNK, HALF_Q), BF),
            pltpu.VMEM((2, keys, 2 * HEAD), BF),
            pltpu.VMEM((CHUNK, HALF_Q), BF),
            pltpu.VMEM((keys, WIDE), F32),
            pltpu.VMEM((keys, WIDE), F32),
            pltpu.VMEM((2, keys, GROUPS * HEAD), BF),
            pltpu.VMEM((2, keys, GROUPS * HEAD), BF),
            pltpu.VMEM((keys, HEAD), F32),
            pltpu.VMEM((keys, HEAD), F32),
            pltpu.VMEM((2, keys, HEAD), BF),
            pltpu.VMEM((2, keys, HEAD), BF),
            pltpu.VMEM((2, OWN, HEAD), F32),
            pltpu.VMEM((2, OWN, HEAD), F32),
            pltpu.VMEM((NX - 1, 2, NZH, CHUNK, HEAD), BF),
            pltpu.VMEM((NX - 1, 2, OWN, HEAD), BF),
            pltpu.VMEM((2, CHUNK, HEAD), BF),
            pltpu.VMEM((2, CHUNK, HEAD), BF),
            pltpu.VMEM((2, CHUNK, HEAD), BF),
            pltpu.VMEM((2, CHUNK, HEAD), BF),
            pltpu.VMEM((2, NC, LONG_DEV, HEAD), BF),
            pltpu.VMEM((NC, LONG_DEV, HALF_K), BF),
            pltpu.VMEM((NY, NX * NZH, 96, NC * TOK_DEV), BF),
            pltpu.VMEM((2, NY, NC, TOK_DEV, HALF_K), BF),
            pltpu.VMEM((2, NX, NZH, 96, HALF_K), BF),
            pltpu.VMEM((2, NX - 1, NZH, 96, HALF_K), BF),
            pltpu.VMEM((2, NZH, 96, HALF_K), F32),
            pltpu.VMEM((2, NZ, 48, 128), F32),
            pltpu.VMEM((2, NZ, 48, 128), BF),
            pltpu.VMEM((2, NZ - 1, 48, 128), BF),
            pltpu.VMEM((2, NY * NZL, 48, 128), BF),
            DMA((11,)),
            DMA((8,)),
            DMA((13,)),
            *pairs(2),
            *pairs(2, 9),
            *pairs(2, 2, 3),
            *pairs(1),
            *pairs(2, 2, 3),
            *pairs(3),
            *pairs(2),
            *pairs(1),
            *pairs(7),
            *pairs(7),
            *pairs(2, 7),
            *pairs(1),
            *pairs(2, 3),
            *pairs(2, 7),
            *pairs(2, 3),
            *pairs(2, 3),
        ],
        compiler_params=pltpu.CompilerParams(
            vmem_limit_bytes=VMEM_LIMIT, collective_id=1, has_side_effects=True
        ),
    )(
        queries, output_grad, key_states, value_states, layer_inputs, short_segments,
        master, first_moment, second_moment,
    )
    return pl.pallas_call(
        store_kernel,
        name="store",
        out_shape=results,
        in_specs=[VMEM] * 6,
        out_specs=[HBM] * 6,
        scratch_shapes=[DMA((6,))],
        compiler_params=pltpu.CompilerParams(vmem_limit_bytes=8 << 20),
    )(*made)


def solution(mesh):
    tokens = P(("dp", "ctx"), None)
    shard = P("ctx", "dp", None)
    return jax.shard_map(
        on_device,
        mesh=mesh,
        in_specs=(tokens,) * 6 + (shard,) * 3,
        out_specs=(tokens, tokens, shard, shard, shard, P("ctx", None, None)),
        check_vma=False,
    )
```
